32 devices in a mesh: dp: 4 (over x, core), row: 2 (over y), col: 4 (over z).
Axes of the slice: x: 2, y: 2, z: 4, core: 2. Of those that a mesh axis runs over, the one named last changes fastest.
Arguments:
- inputs: bfloat16 [768, 4096], P('dp', 'row'), may hold values from -6 to 6
- weight: bfloat16 [4096, 14336], P('row', 'col'), may hold values from -0.09375 to 0.09375
- cotangent: bfloat16 [768, 14336], P(('dp', 'row'), 'col'), may hold values from -6 to 6
- anchor: bfloat16 [4096, 14336], P(('row', 'dp'), 'col'), may hold values from -0.09375 to 0.09375
- first_moment: float32 [4096, 14336], P(('row', 'dp'), 'col'), may hold values from -0.15625 to 0.15625
- second_moment: float32 [4096, 14336], P(('row', 'dp'), 'col'), may hold values from 1e-06 to 0.0001
Outputs:
- outputs: bfloat16 [768, 14336], P(('dp', 'row'), 'col')
- input_grad: bfloat16 [768, 4096], P(('dp', 'col'), 'row')
- new_weight: bfloat16 [4096, 14336], P(('row', 'dp'), 'col')
- new_first: float32 [4096, 14336], P(('row', 'dp'), 'col')
- new_second: float32 [4096, 14336], P(('row', 'dp'), 'col')
The draws below stay inside these ranges and needn't reach their ends.
All inputs are finite; a program needn't handle non-finite values.
Results may differ from the reference program's by a relative error of at most 0.013.
Values may be sent and summed in bfloat16 or wider, within the bound.
No kernel may reach another device: no remote copies, remote signals or barrier semaphores. Data moves between devices by JAX's collectives and lax.ppermute only.
A program may use at most 128 MiB of HBM per device.

```python
import math
import jax
import jax.numpy as jnp
from jax import lax

D = 4096
F = 14336
TOK_DEV = 192
TOKENS = 768
DR = 2048
FC = 3584
N_DP = 4
N_ROW = 2
N_COL = 4


def steps_of(key, dims, shards, smallest, top_value):
    def one(dim, shards_of):
        steps = jax.random.uniform(jax.random.fold_in(jax.random.fold_in(key, 6), dim), (shards_of,), jnp.float32, smallest / len(shards), top_value / len(shards))
        return jnp.repeat(jnp.exp(steps), dims[dim] // shards_of).reshape((-1,) + (1,) * (len(dims) - dim - 1))

    gain = one(*shards[0])
    for cut in shards[1:]:
        gain = gain * one(*cut)
    return gain


def noise(key, extent, scale, limit, shards=(), kind=jnp.bfloat16):
    drawn = scale * jax.random.normal(key, extent, jnp.float32)
    if shards:
        drawn = drawn * steps_of(key, extent, shards, -0.22, 0.18)
    return jnp.clip(drawn, -limit, limit).astype(kind)


def setup_inputs(seed: int = 0) -> dict:
    seeds = jax.random.split(jax.random.key(seed), 7)
    inputs = noise(seeds[0], (TOKENS, D), 1.0, 6.0, ((0, 4), (1, 2)))
    weight = noise(seeds[1], (D, F), D ** -0.5, 0.09375, ((0, 2), (1, 4)))
    cotangent = noise(seeds[2], (TOKENS, F), 1.0, 6.0, ((0, 8), (1, 4)))
    anchor = noise(seeds[3], (D, F), D ** -0.5, 0.09375, ((0, 8), (1, 4)))
    first_moment = noise(seeds[4], (D, F), 0.01, 0.15625, ((0, 8), (1, 4)), jnp.float32)
    second_moment = jnp.clip(jnp.exp(math.log(0.0001) - 4.6051702 * jax.random.uniform(seeds[5], (D, F), jnp.float32) ** steps_of(seeds[5], (D, F), ((0, 8), (1, 4)), -0.2, 0.2)), 9.999999974752427e-07, 0.0001)
    return dict(inputs=inputs, weight=weight, cotangent=cotangent, anchor=anchor, first_moment=first_moment, second_moment=second_moment)


beta_one = 0.9
beta_two = 0.999
learn_rate = 0.002
anchor_pull = 0.5
epsilon = 1e-08
step_count = 100.0

def rounded(value):
    narrow = lax.optimization_barrier(value.astype(jnp.bfloat16))
    return narrow.astype(jnp.float32)

def reference(inputs, weight, cotangent, anchor, first_moment, second_moment):
    total = jnp.zeros((TOKENS, F), jnp.float32)
    for block in range(N_ROW):
        part = jnp.dot(inputs[:, block * DR:(block + 1) * DR], weight[block * DR:(block + 1) * DR, :], preferred_element_type=jnp.float32)
        total = total + rounded(part)
    outputs = total.astype(jnp.bfloat16)
    grad_total = jnp.zeros((TOKENS, D), jnp.float32)
    for block in range(N_COL):
        gpart = lax.dot_general(cotangent[:, block * FC:(block + 1) * FC], weight[:, block * FC:(block + 1) * FC], (((1,), (1,)), ((), ())), preferred_element_type=jnp.float32)
        grad_total = grad_total + rounded(gpart)
    input_grad = grad_total.astype(jnp.bfloat16)
    summed = jnp.zeros((D, F), jnp.float32)
    for block in range(N_DP):
        piece = lax.dot_general(inputs[block * TOK_DEV:(block + 1) * TOK_DEV, :], cotangent[block * TOK_DEV:(block + 1) * TOK_DEV, :], (((0,), (0,)), ((), ())), preferred_element_type=jnp.float32)
        summed = summed + rounded(piece)
    current = weight.astype(jnp.float32)
    grad = summed / TOKENS + anchor_pull * (current - anchor.astype(jnp.float32))
    new_first = beta_one * first_moment + (1.0 - beta_one) * grad
    new_second = beta_two * second_moment + (1.0 - beta_two) * grad * grad
    mhat = new_first / (1.0 - beta_one ** step_count)
    vhat = new_second / (1.0 - beta_two ** step_count)
    new_weight = (current - learn_rate * mhat / (jnp.sqrt(vhat) + epsilon)).astype(jnp.bfloat16)
    return (outputs, input_grad, new_weight, new_first, new_second)
```

```python
import jax
import jax.numpy as jnp
from jax import lax
from jax.sharding import PartitionSpec as P

beta_one = 0.9
beta_two = 0.999
learn_rate = 0.002
anchor_pull = 0.5
epsilon = 1e-08
step_count = 100.0


def per_device(inputs, weight, cotangent, anchor, first_moment, second_moment):
    n_dp, n_row, n_col = (lax.axis_size(a) for a in ("dp", "row", "col"))
    dp, row, col = (lax.axis_index(a) for a in ("dp", "row", "col"))
    cores = 2 if n_dp % 2 == 0 else 1
    chips = n_dp // cores
    tokens = inputs.shape[0]
    own_tokens = cotangent.shape[0]
    slice_rows = weight.shape[0] // n_dp

    def along(axis, n, shift):
        return lambda a: lax.ppermute(a, axis, [(i, (i + shift) % n) for i in range(n)])

    def chip_shift(shift):
        return lambda a: lax.ppermute(
            a, "dp", [(i, (i + shift * cores) % n_dp) for i in range(n_dp)]
        )

    def swap_cores(a):
        return lax.ppermute(a, "dp", [(i, i ^ 1) for i in range(n_dp)])

    def in_row_order(pieces):
        whole = jnp.zeros((n_row * own_tokens, cotangent.shape[1]), cotangent.dtype)
        for shift, piece in enumerate(pieces):
            start = lax.rem(row - shift + n_row, n_row) * own_tokens
            whole = lax.dynamic_update_slice_in_dim(whole, piece, start, 0)
        return whole

    by_row = [cotangent] + [along("row", n_row, s)(cotangent) for s in range(1, n_row)]
    mine = {(0, s): p for s, p in enumerate(by_row)}
    for c in range(1, chips):
        for s, p in enumerate(by_row):
            mine[c, s] = chip_shift(c)(p)

    def columns_for(peer):
        return lax.dynamic_slice_in_dim(inputs, peer * slice_rows, slice_rows, 1)

    held = {0: columns_for(dp)}
    for s in range(1, n_dp):
        held[s] = along("dp", n_dp, s)(columns_for(lax.rem(dp + s, n_dp)))

    part = jnp.dot(inputs, weight, preferred_element_type=jnp.float32)
    outputs = lax.dynamic_slice_in_dim(part, row * own_tokens, own_tokens, 0)
    for s in range(1, n_row):
        start = lax.rem(row + s, n_row) * own_tokens
        sent = lax.dynamic_slice_in_dim(part.astype(jnp.bfloat16), start, own_tokens, 0)
        outputs = outputs + along("row", n_row, s)(sent).astype(jnp.float32)
    outputs = outputs.astype(jnp.bfloat16)

    gathered = in_row_order(by_row)
    gpart = lax.dot_general(
        gathered, weight, (((1,), (1,)), ((), ())), preferred_element_type=jnp.float32
    )
    share = tokens // n_col
    input_grad = lax.dynamic_slice_in_dim(gpart, col * share, share, 0)
    for s in range(1, n_col):
        start = lax.rem(col + s, n_col) * share
        sent = lax.dynamic_slice_in_dim(gpart.astype(jnp.bfloat16), start, share, 0)
        input_grad = input_grad + along("col", n_col, s)(sent).astype(jnp.float32)
    input_grad = input_grad.astype(jnp.bfloat16)

    lefts, rights = [], []
    for c in range(chips):
        for other in range(cores):
            pieces = [mine[c, s] for s in range(n_row)]
            if other:
                pieces = [swap_cores(p) for p in pieces]
            rights.append(gathered if (c, other) == (0, 0) else in_row_order(pieces))
            came = lax.rem((dp ^ 1 if other else dp) - c * cores + n_dp, n_dp)
            shift = lax.rem(dp - came + n_dp, n_dp)
            lefts.append(lax.dynamic_index_in_dim(jnp.stack([held[k] for k in range(n_dp)]), shift, 0, keepdims=False))
    summed = lax.dot_general(
        jnp.concatenate(lefts, 0),
        jnp.concatenate(rights, 0),
        (((0,), (0,)), ((), ())),
        preferred_element_type=jnp.float32,
    )

    tokens_all = tokens * n_dp
    current = lax.dynamic_slice_in_dim(weight, dp * slice_rows, slice_rows, 0).astype(jnp.float32)
    grad = summed / tokens_all + anchor_pull * (current - anchor.astype(jnp.float32))
    new_first = beta_one * first_moment + (1.0 - beta_one) * grad
    new_second = beta_two * second_moment + (1.0 - beta_two) * grad * grad
    mhat = new_first / (1.0 - beta_one**step_count)
    vhat = new_second / (1.0 - beta_two**step_count)
    new_weight = (current - learn_rate * mhat / (jnp.sqrt(vhat) + epsilon)).astype(jnp.bfloat16)
    return (outputs, input_grad, new_weight, new_first, new_second)


def solution(mesh):
    in_specs = (
        P("dp", "row"),
        P("row", "col"),
        P(("dp", "row"), "col"),
        P(("row", "dp"), "col"),
        P(("row", "dp"), "col"),
        P(("row", "dp"), "col"),
    )
    out_specs = (
        P(("dp", "row"), "col"),
        P(("dp", "col"), "row"),
        P(("row", "dp"), "col"),
        P(("row", "dp"), "col"),
        P(("row", "dp"), "col"),
    )
    return jax.shard_map(
        per_device, mesh=mesh, in_specs=in_specs, out_specs=out_specs, check_vma=False
    )
```

```python
import functools
import math

import jax
import jax.numpy as jnp
from jax import lax
from jax.experimental import pallas as pl
from jax.experimental.pallas import tpu as pltpu
from jax.sharding import PartitionSpec as P

beta_one = 0.9
beta_two = 0.999
learn_rate = 0.002
anchor_pull = 0.5
epsilon = 1e-08
step_count = 100.0

BF16, F32 = jnp.bfloat16, jnp.float32
MIB = 1 << 20


def block_of(size, most):
    return max(b for b in range(128, most + 1, 128) if size % b == 0)


def struct(shape, dtype):
    return jax.ShapeDtypeStruct(shape, dtype)


def run(kernel, name, grid, in_specs, out_specs, out_shape, scratch, limit, args):
    return pl.pallas_call(
        kernel,
        name=name,
        grid_spec=pltpu.PrefetchScalarGridSpec(
            num_scalar_prefetch=1,
            grid=grid,
            in_specs=in_specs,
            out_specs=out_specs,
            scratch_shapes=scratch,
        ),
        out_shape=out_shape,
        compiler_params=pltpu.CompilerParams(vmem_limit_bytes=limit * MIB),
        cost_estimate=pl.CostEstimate(flops=1, bytes_accessed=1, transcendentals=0),
    )(*args)


def fixed(shape):
    return pl.BlockSpec(shape, lambda j, place: (0,) * len(shape))


def columns(rows, width):
    return pl.BlockSpec((rows, width), lambda j, place: (0, j))


def forward_kernel(n_dp, n_row, own, slice_rows, place, x_ref, w_ref, *rest):
    parts, sent, xs = rest[:n_row], rest[n_row : n_row + n_dp - 1], rest[-1]
    dp, row = place[0], place[1]

    @pl.when(pl.program_id(0) == 0)
    def _():
        for s in range(n_row):
            start = pl.multiple_of(lax.rem(row + s, n_row) * own, own)
            xs[s * own : (s + 1) * own, :] = x_ref[pl.ds(start, own), :]
        for s in range(1, n_dp):
            start = pl.multiple_of(lax.rem(dp + s, n_dp) * slice_rows, slice_rows)
            sent[s - 1][...] = x_ref[:, pl.ds(start, slice_rows)]

    acc = jnp.dot(xs[...], w_ref[...], preferred_element_type=F32)
    for s in range(n_row):
        parts[s][...] = acc[s * own : (s + 1) * own].astype(parts[s].dtype)


def forward_call(place, inputs, weight, own, n_dp, n_row, slice_rows):
    tokens, depth = inputs.shape
    width = weight.shape[1]
    block = block_of(width, 512)
    return run(
        functools.partial(forward_kernel, n_dp, n_row, own, slice_rows),
        "forward",
        (width // block,),
        [fixed((tokens, depth)), columns(depth, block)],
        [columns(own, block)] * n_row + [fixed((tokens, slice_rows))] * (n_dp - 1),
        [struct((own, width), F32)]
        + [struct((own, width), BF16)] * (n_row - 1)
        + [struct((tokens, slice_rows), BF16)] * (n_dp - 1),
        [pltpu.VMEM((tokens, depth), BF16)],
        24,
        (place, inputs, weight),
    )


def input_grad_kernel(n_row, n_col, own, share, place, *rest):
    pieces, w_ref = rest[:n_row], rest[n_row]
    parts, (cs, acc) = rest[n_row + 1 : n_row + 1 + n_col], rest[-2:]
    row, col = place[1], place[2]

    @pl.when(pl.program_id(0) == 0)
    def _():
        for s in range(n_row):
            start = pl.multiple_of(lax.rem(row - s + n_row, n_row) * own, own)
            cs[pl.ds(start, own), :] = pieces[s][...]

    acc[...] = lax.dot_general(
        cs[...], w_ref[...], (((1,), (1,)), ((), ())), preferred_element_type=F32
    )
    for s in range(n_col):
        start = pl.multiple_of(lax.rem(col + s, n_col) * share, share)
        parts[s][...] = acc[pl.ds(start, share), :].astype(parts[s].dtype)


def input_grad_call(place, by_row, weight, share, n_row, n_col):
    own, width = by_row[0].shape
    depth = weight.shape[0]
    block = block_of(depth, 256)
    return run(
        functools.partial(input_grad_kernel, n_row, n_col, own, share),
        "input_grad",
        (depth // block,),
        [fixed((own, width))] * n_row + [pl.BlockSpec((block, width), lambda j, place: (j, 0))],
        [columns(share, block)] * n_col,
        [struct((share, depth), F32)] + [struct((share, depth), BF16)] * (n_col - 1),
        [pltpu.VMEM((n_row * own, width), BF16), pltpu.VMEM((n_row * own, block), F32)],
        24,
        (place, *by_row, weight),
    )


def transpose_kernel(n_dp, tokens, place, *rest):
    pieces, out, xs = rest[:n_dp], rest[n_dp], rest[n_dp + 1]
    for s in range(n_dp):
        start = pl.multiple_of(lax.rem(place[0] - s + n_dp, n_dp) * tokens, tokens)
        xs[pl.ds(start, tokens), :] = pieces[s][...]
    out[...] = xs[...].T


def transpose_call(place, inputs, pieces, slice_rows):
    tokens, n_dp = inputs.shape[0], len(pieces) + 1
    return run(
        functools.partial(transpose_kernel, n_dp, tokens),
        "features",
        (1,),
        [pl.BlockSpec((tokens, slice_rows), lambda j, place: (0, place[0]))]
        + [fixed((tokens, slice_rows))] * (n_dp - 1),
        fixed((slice_rows, n_dp * tokens)),
        struct((slice_rows, n_dp * tokens), BF16),
        [pltpu.VMEM((n_dp * tokens, slice_rows), BF16)],
        16,
        (place, inputs, *pieces),
    )


def updated(grad_sum, tokens_all, current, anchor, first, second):
    grad = grad_sum * (1.0 / tokens_all) + anchor_pull * (current - anchor)
    first = beta_one * first + (1.0 - beta_one) * grad
    second = beta_two * second + (1.0 - beta_two) * grad * grad
    scale = learn_rate / (1.0 - beta_one**step_count)
    spread = jnp.sqrt(second * (1.0 / (1.0 - beta_two**step_count))) + epsilon
    return current - scale * first / spread, first, second


def update_kernel(origins, tokens_all, chunk, place, x_ref, *rest):
    n = len(origins)
    pieces = rest[:n]
    w_ref, a_ref, m_ref, v_ref, new_w, new_m, new_v, cs, acc = rest[n:]
    own = pieces[0].shape[0]
    for piece, origin in zip(pieces, origins):
        cs[pl.ds(pl.multiple_of(origin(place[0], place[1]) * own, own), own), :] = piece[...]
    acc[...] = jnp.dot(x_ref[...], cs[...], preferred_element_type=F32)

    @pl.loop(0, acc.shape[0] // chunk)
    def _(i):
        at = pl.ds(pl.multiple_of(i * chunk, chunk), chunk)
        weight, first, second = updated(
            acc[at, :],
            tokens_all,
            w_ref[at, :].astype(F32),
            a_ref[at, :].astype(F32),
            m_ref[at, :],
            v_ref[at, :],
        )
        new_w[at, :] = weight.astype(BF16)
        new_m[at, :] = first
        new_v[at, :] = second


def update_call(place, features, pieces, origins, weight, anchor, first, second):
    rows, width = first.shape
    tokens_all = features.shape[1]
    block = block_of(width, 512)
    own = pieces[0].shape[0]
    tile = columns(rows, block)
    return run(
        functools.partial(update_kernel, origins, tokens_all, math.gcd(rows, 16)),
        "update",
        (width // block,),
        [fixed((rows, tokens_all))]
        + [columns(own, block)] * len(pieces)
        + [pl.BlockSpec((rows, block), lambda j, place: (place[0], j)), tile, tile, tile],
        [tile] * 3,
        [struct((rows, width), BF16), struct((rows, width), F32), struct((rows, width), F32)],
        [pltpu.VMEM((tokens_all, block), BF16), pltpu.VMEM((rows, block), F32)],
        32,
        (place, features, *pieces, weight, anchor, first, second),
    )


def per_device(inputs, weight, cotangent, anchor, first_moment, second_moment):
    n_dp, n_row, n_col = (lax.axis_size(a) for a in ("dp", "row", "col"))
    dp, row, col = (lax.axis_index(a) for a in ("dp", "row", "col"))
    place = jnp.stack([dp, row, col]).astype(jnp.int32)
    cores = 2 if n_dp % 2 == 0 else 1
    chips = n_dp // cores
    tokens = inputs.shape[0]
    own = cotangent.shape[0]
    share = tokens // n_col
    slice_rows = weight.shape[0] // n_dp
    tiled = own % 16 == 0 and share % 16 == 0 and slice_rows % 128 == 0

    def along(axis, n, shift):
        return lambda a: lax.ppermute(a, axis, [(i, (i + shift) % n) for i in range(n)])

    def chip_shift(shift):
        return along("dp", n_dp, shift * cores)

    def swap_cores(a):
        return lax.ppermute(a, "dp", [(i, i ^ 1) for i in range(n_dp)])

    def in_order(pieces, places, rows):
        whole = jnp.zeros((len(pieces) * rows, pieces[0].shape[1]), pieces[0].dtype)
        for piece, at in zip(pieces, places):
            whole = lax.dynamic_update_slice_in_dim(whole, piece, at * rows, 0)
        return whole

    by_row = [cotangent] + [along("row", n_row, s)(cotangent) for s in range(1, n_row)]
    pieces, origins = [], []
    for c in range(chips):
        for s in range(n_row):
            piece = chip_shift(c)(by_row[s]) if c else by_row[s]

            def origin(dp, row, c=c, s=s, flip=0):
                core = lax.rem(dp, cores)
                from_core = 1 - core if flip else core
                from_dp = lax.rem(dp - core - c * cores + n_dp, n_dp) + from_core
                return from_dp * n_row + lax.rem(row - s + n_row, n_row)

            pieces.append(piece)
            origins.append(origin)
            if cores == 2:
                pieces.append(swap_cores(piece))
                origins.append(functools.partial(origin, flip=1))

    if tiled:
        made = forward_call(place, inputs, weight, own, n_dp, n_row, slice_rows)
        parts, to_send = made[:n_row], made[n_row:]
    else:
        part = jnp.dot(inputs, weight, preferred_element_type=F32)
        parts = [
            lax.dynamic_slice_in_dim(part, lax.rem(row + s, n_row) * own, own, 0).astype(
                BF16 if s else F32
            )
            for s in range(n_row)
        ]
        to_send = [
            lax.dynamic_slice_in_dim(
                inputs, lax.rem(dp + s, n_dp) * slice_rows, slice_rows, 1
            )
            for s in range(1, n_dp)
        ]
    held = [along("dp", n_dp, s)(to_send[s - 1]) for s in range(1, n_dp)]
    outputs = parts[0]
    for s in range(1, n_row):
        outputs = outputs + along("row", n_row, s)(parts[s]).astype(F32)
    outputs = outputs.astype(BF16)

    if tiled:
        gparts = input_grad_call(place, by_row, weight, share, n_row, n_col)
    else:
        gathered = in_order(by_row, [lax.rem(row - s + n_row, n_row) for s in range(n_row)], own)
        gpart = lax.dot_general(
            gathered, weight, (((1,), (1,)), ((), ())), preferred_element_type=F32
        )
        gparts = [
            lax.dynamic_slice_in_dim(gpart, lax.rem(col + s, n_col) * share, share, 0).astype(
                BF16 if s else F32
            )
            for s in range(n_col)
        ]
    input_grad = gparts[0]
    for s in range(1, n_col):
        input_grad = input_grad + along("col", n_col, s)(gparts[s]).astype(F32)
    input_grad = input_grad.astype(BF16)

    if tiled:
        features = transpose_call(place, inputs, held, slice_rows)
        new_weight, new_first, new_second = update_call(
            place, features, pieces, origins, weight, anchor, first_moment, second_moment
        )
    else:
        mine = lax.dynamic_slice_in_dim(inputs, dp * slice_rows, slice_rows, 1)
        features = in_order(
            [mine] + held, [lax.rem(dp - s + n_dp, n_dp) for s in range(n_dp)], tokens
        )
        gathered = in_order(pieces, [origin(dp, row) for origin in origins], own)
        summed = lax.dot_general(
            features, gathered, (((0,), (0,)), ((), ())), preferred_element_type=F32
        )
        current = lax.dynamic_slice_in_dim(weight, dp * slice_rows, slice_rows, 0).astype(F32)
        new_weight, new_first, new_second = updated(
            summed,
            tokens * n_dp,
            current,
            anchor.astype(F32),
            first_moment,
            second_moment,
        )
        new_weight = new_weight.astype(BF16)
    return (outputs, input_grad, new_weight, new_first, new_second)


def solution(mesh):
    in_specs = (
        P("dp", "row"),
        P("row", "col"),
        P(("dp", "row"), "col"),
        P(("row", "dp"), "col"),
        P(("row", "dp"), "col"),
        P(("row", "dp"), "col"),
    )
    out_specs = (
        P(("dp", "row"), "col"),
        P(("dp", "col"), "row"),
        P(("row", "dp"), "col"),
        P(("row", "dp"), "col"),
        P(("row", "dp"), "col"),
    )
    return jax.shard_map(
        per_device, mesh=mesh, in_specs=in_specs, out_specs=out_specs, check_vma=False
    )
```

```python
import functools
import math

import jax
import jax.numpy as jnp
from jax import lax
from jax.experimental import pallas as pl
from jax.experimental.pallas import tpu as pltpu
from jax.sharding import PartitionSpec as P

beta_one = 0.9
beta_two = 0.999
learn_rate = 0.002
anchor_pull = 0.5
epsilon = 1e-08
step_count = 100.0

BF16, F32 = jnp.bfloat16, jnp.float32
MIB = 1 << 20


def block_of(size, most):
    return max(b for b in range(128, most + 1, 128) if size % b == 0)


def struct(shape, dtype):
    return jax.ShapeDtypeStruct(shape, dtype)


def run(kernel, name, grid, in_specs, out_specs, out_shape, scratch, limit, args, bytes_moved=1):
    return pl.pallas_call(
        kernel,
        name=name,
        grid_spec=pltpu.PrefetchScalarGridSpec(
            num_scalar_prefetch=1,
            grid=grid,
            in_specs=in_specs,
            out_specs=out_specs,
            scratch_shapes=scratch,
        ),
        out_shape=out_shape,
        compiler_params=pltpu.CompilerParams(vmem_limit_bytes=limit * MIB),
        cost_estimate=pl.CostEstimate(
            flops=1, bytes_accessed=bytes_moved, transcendentals=0
        ),
    )(*args)


def fixed(shape):
    return pl.BlockSpec(shape, lambda j, place: (0,) * len(shape))


def columns(rows, width):
    return pl.BlockSpec((rows, width), lambda j, place: (0, j))


def forward_kernel(n_row, own, slice_rows, targets, place, x_ref, w_ref, *rest):
    parts, sent, xs = rest[:n_row], rest[n_row:-1], rest[-1]
    dp, row = place[0], place[1]
    tokens = x_ref.shape[0]

    @pl.when(pl.program_id(0) == 0)
    def _():
        for s in range(n_row):
            start = pl.multiple_of(lax.rem(row + s, n_row) * own, own)
            xs[s * own : (s + 1) * own, :] = x_ref[pl.ds(start, own), :]
        for out, owners in zip(sent, targets):
            for k, owner in enumerate(owners):
                start = pl.multiple_of(owner(dp) * slice_rows, slice_rows)
                out[k * tokens : (k + 1) * tokens, :] = x_ref[:, pl.ds(start, slice_rows)]

    acc = jnp.dot(xs[...], w_ref[...], preferred_element_type=F32)
    for s in range(n_row):
        parts[s][...] = acc[s * own : (s + 1) * own].astype(parts[s].dtype)


def forward_call(place, inputs, weight, own, n_row, slice_rows, targets):
    tokens, depth = inputs.shape
    width = weight.shape[1]
    block = block_of(width, 512)
    sent = [(len(owners) * tokens, slice_rows) for owners in targets]
    return run(
        functools.partial(forward_kernel, n_row, own, slice_rows, targets),
        "forward",
        (width // block,),
        [fixed((tokens, depth)), columns(depth, block)],
        [columns(own, block)] * n_row + [fixed(shape) for shape in sent],
        [struct((own, width), F32)]
        + [struct((own, width), BF16)] * (n_row - 1)
        + [struct(shape, BF16) for shape in sent],
        [pltpu.VMEM((tokens, depth), BF16)],
        52,
        (place, inputs, weight),
    )


def input_grad_kernel(n_row, n_col, own, share, place, *rest):
    pieces, w_ref = rest[:n_row], rest[n_row]
    parts, (cs, acc) = rest[n_row + 1 : n_row + 1 + n_col], rest[-2:]
    row, col = place[1], place[2]

    @pl.when(pl.program_id(0) == 0)
    def _():
        for s in range(n_row):
            start = pl.multiple_of(lax.rem(row - s + n_row, n_row) * own, own)
            cs[pl.ds(start, own), :] = pieces[s][...]

    acc[...] = lax.dot_general(
        cs[...], w_ref[...], (((1,), (1,)), ((), ())), preferred_element_type=F32
    )
    for s in range(n_col):
        start = pl.multiple_of(lax.rem(col + s, n_col) * share, share)
        parts[s][...] = acc[pl.ds(start, share), :].astype(parts[s].dtype)


def input_grad_call(place, by_row, weight, share, n_row, n_col):
    own, width = by_row[0].shape
    depth = weight.shape[0]
    block = block_of(depth, 256)
    return run(
        functools.partial(input_grad_kernel, n_row, n_col, own, share),
        "input_grad",
        (depth // block,),
        [fixed((own, width))] * n_row + [pl.BlockSpec((block, width), lambda j, place: (j, 0))],
        [columns(share, block)] * n_col,
        [struct((share, depth), F32)] + [struct((share, depth), BF16)] * (n_col - 1),
        [pltpu.VMEM((n_row * own, width), BF16), pltpu.VMEM((n_row * own, block), F32)],
        52,
        (place, *by_row, weight),
    )


def features_kernel(sources, tokens, place, *rest):
    n = len(sources)
    pieces, out, xs = rest[:n], rest[n], rest[n + 1]
    for piece, (origin, skip) in zip(pieces, sources):
        start = pl.multiple_of(origin(place[0]) * tokens, tokens)
        xs[pl.ds(start, tokens), :] = piece[skip : skip + tokens, :]
    out[...] = xs[...].T


def features_call(place, inputs, held, sources, slice_rows):
    tokens, n_dp = inputs.shape[0], len(sources)
    return run(
        functools.partial(features_kernel, sources, tokens),
        "features",
        (1,),
        [pl.BlockSpec((tokens, slice_rows), lambda j, place: (0, place[0]))]
        + [fixed(piece.shape) for piece in held],
        fixed((slice_rows, n_dp * tokens)),
        struct((slice_rows, n_dp * tokens), BF16),
        [pltpu.VMEM((n_dp * tokens, slice_rows), BF16)],
        16,
        (place, inputs, *held),
    )


def updated(grad_sum, tokens_all, current, anchor, first, second):
    grad = grad_sum * (1.0 / tokens_all) + anchor_pull * (current - anchor)
    first = beta_one * first + (1.0 - beta_one) * grad
    second = beta_two * second + (1.0 - beta_two) * grad * grad
    scale = learn_rate / (1.0 - beta_one**step_count)
    spread = jnp.sqrt(second * (1.0 / (1.0 - beta_two**step_count))) + epsilon
    return current - scale * first / spread, first, second


def update_kernel(origins, tokens_all, chunk, place, x_ref, *rest):
    n = len(origins)
    pieces = rest[:n]
    w_ref, a_ref, m_ref, v_ref, new_w, new_m, new_v, cs, acc = rest[n:]
    own = pieces[0].shape[0]
    for piece, origin in zip(pieces, origins):
        cs[pl.ds(pl.multiple_of(origin(place[0], place[1]) * own, own), own), :] = piece[...]
    acc[...] = jnp.dot(x_ref[...], cs[...], preferred_element_type=F32)

    @pl.loop(0, acc.shape[0] // chunk, unroll=4)
    def _(i):
        at = pl.ds(pl.multiple_of(i * chunk, chunk), chunk)
        weight, first, second = updated(
            acc[at, :],
            tokens_all,
            w_ref[at, :].astype(F32),
            a_ref[at, :].astype(F32),
            m_ref[at, :],
            v_ref[at, :],
        )
        new_w[at, :] = weight.astype(BF16)
        new_m[at, :] = first
        new_v[at, :] = second


def update_call(place, features, pieces, origins, weight, anchor, first, second):
    rows, width = first.shape
    tokens_all = features.shape[1]
    block = block_of(width, 512)
    own = pieces[0].shape[0]
    tile = columns(rows, block)
    return run(
        functools.partial(update_kernel, origins, tokens_all, math.gcd(rows, 32)),
        "update",
        (width // block,),
        [fixed((rows, tokens_all))]
        + [columns(own, block)] * len(pieces)
        + [pl.BlockSpec((rows, block), lambda j, place: (place[0], j)), tile, tile, tile],
        [tile] * 3,
        [struct((rows, width), BF16), struct((rows, width), F32), struct((rows, width), F32)],
        [pltpu.VMEM((tokens_all, block), BF16), pltpu.VMEM((rows, block), F32)],
        40,
        (place, features, *pieces, weight, anchor, first, second),
    )


def after(value, *others):
    return lax.optimization_barrier((value, *others))[0]


def per_device(inputs, weight, cotangent, anchor, first_moment, second_moment):
    n_dp, n_row, n_col = (lax.axis_size(a) for a in ("dp", "row", "col"))
    dp, row, col = (lax.axis_index(a) for a in ("dp", "row", "col"))
    place = jnp.stack([dp, row, col]).astype(jnp.int32)
    cores = 2 if n_dp % 2 == 0 else 1
    chips = n_dp // cores
    tokens = inputs.shape[0]
    own = cotangent.shape[0]
    share = tokens // n_col
    slice_rows = weight.shape[0] // n_dp
    tiled = own % 16 == 0 and share % 16 == 0 and slice_rows % 128 == 0

    def along(axis, n, shift):
        return lambda a: lax.ppermute(a, axis, [(i, (i + shift) % n) for i in range(n)])

    def chip_shift(shift):
        return along("dp", n_dp, shift * cores)

    def swap_cores(a):
        return lax.ppermute(a, "dp", [(i, i ^ 1) for i in range(n_dp)])

    def in_order(pieces, places, rows):
        whole = jnp.zeros((len(pieces) * rows, pieces[0].shape[1]), pieces[0].dtype)
        for piece, at in zip(pieces, places):
            whole = lax.dynamic_update_slice_in_dim(whole, piece, at * rows, 0)
        return whole

    def dp_of(dp, c, flip):
        core = lax.rem(dp, cores)
        return lax.rem(dp - core - c * cores + n_dp, n_dp) + (1 - core if flip else core)

    by_row = [cotangent] + [along("row", n_row, s)(cotangent) for s in range(1, n_row)]
    by_chip = {(c, 0): chip_shift(c)(cotangent) for c in range(1, chips)}
    swapped = {(0, 0): swap_cores(cotangent)} if cores == 2 else {}

    flips = range(cores)
    targets = [[functools.partial(dp_of, c=0, flip=1)]] if cores == 2 else []
    targets += [[functools.partial(dp_of, c=chips - c, flip=f) for f in flips] for c in range(1, chips)]
    if tiled:
        made = forward_call(place, inputs, weight, own, n_row, slice_rows, targets)
        parts, to_send = made[:n_row], made[n_row:]
    else:
        part = jnp.dot(inputs, weight, preferred_element_type=F32)
        parts = [
            lax.dynamic_slice_in_dim(part, lax.rem(row + s, n_row) * own, own, 0).astype(
                BF16 if s else F32
            )
            for s in range(n_row)
        ]
        to_send = [
            jnp.concatenate(
                [
                    lax.dynamic_slice_in_dim(inputs, owner(dp) * slice_rows, slice_rows, 1)
                    for owner in owners
                ],
                0,
            )
            for owners in targets
        ]
    to_send = list(to_send)
    sums = [
        along("row", n_row, s)(after(parts[s], *swapped.values())) for s in range(1, n_row)
    ]
    near = [swap_cores(to_send.pop(0))] if cores == 2 else []
    first = [by_chip[c, 0] for c in range(1, chips)]
    far = [chip_shift(c)(after(to_send[c - 1], *first)) for c in range(1, chips)]
    for s in range(1, n_row):
        by_row[s] = after(by_row[s], parts[0], *near, *first, *swapped.values())
        if cores == 2:
            swapped[0, s] = swap_cores(by_row[s])
    if cores == 2:
        for c in range(1, chips):
            swapped[c, 0] = swap_cores(by_chip[c, 0])

    if tiled:
        gparts = input_grad_call(place, by_row, weight, share, n_row, n_col)
    else:
        gathered = in_order(by_row, [lax.rem(row - s + n_row, n_row) for s in range(n_row)], own)
        gpart = lax.dot_general(
            gathered, weight, (((1,), (1,)), ((), ())), preferred_element_type=F32
        )
        gparts = [
            lax.dynamic_slice_in_dim(gpart, lax.rem(col + s, n_col) * share, share, 0).astype(
                BF16 if s else F32
            )
            for s in range(n_col)
        ]
    held, sources = [], [(functools.partial(dp_of, c=0, flip=0), 0)]
    if cores == 2:
        held.append(swap_cores(after(near, gparts[0])))
        sources.append((functools.partial(dp_of, c=0, flip=1), 0))
    for c in range(1, chips):
        for f in flips:
            piece = far[c - 1]
            held.append(swap_cores(after(piece, gparts[0])) if f else piece)
            sources.append((functools.partial(dp_of, c=c, flip=f), f * tokens))
    pieces, origins = [], []
    for (c, s), piece in by_chip.items():

        def origin(dp, row, c=c, s=s, flip=0):
            return dp_of(dp, c, flip) * n_row + lax.rem(row - s + n_row, n_row)

        pieces.append(piece)
        origins.append(origin)
        if cores == 2:
            pieces.append(swap_cores(after(piece, gparts[0])))
            origins.append(functools.partial(origin, flip=1))

    early = [swapped[k] for k in swapped]
    for s in range(1, n_row):
        relayed = after(by_row[s], gparts[0])
        for c in range(1, chips):
            by_chip[c, s] = chip_shift(c)(relayed)
    shares = [None] * n_col
    for s in sorted(range(1, n_col), key=lambda s: (abs(2 * s - n_col), s)):
        shares[s] = along("col", n_col, s)(after(gparts[s], *early))
    outputs = parts[0]
    for part in sums:
        outputs = outputs + part.astype(F32)
    outputs = outputs.astype(BF16)

    held, sources = list(near), [(functools.partial(dp_of, c=0, flip=0), 0)]
    if cores == 2:
        sources.append((functools.partial(dp_of, c=0, flip=1), 0))
    for c in range(1, chips):
        for f in flips:
            piece = far[c - 1]
            held.append(swap_cores(after(piece, *shares[1:])) if f else piece)
            sources.append((functools.partial(dp_of, c=c, flip=f), f * tokens))
    pieces, origins = [], []
    for c in range(chips):
        for s in range(n_row):

            def origin(dp, row, c=c, s=s, flip=0):
                return dp_of(dp, c, flip) * n_row + lax.rem(row - s + n_row, n_row)

            piece = by_chip[c, s] if c else by_row[s]
            pieces.append(piece)
            origins.append(origin)
            if cores == 2:
                other = swapped[c, s] if (c, s) in swapped else swap_cores(after(piece, *shares[1:]))
                pieces.append(other)
                origins.append(functools.partial(origin, flip=1))

    if tiled:
        features = features_call(place, inputs, held, sources, slice_rows)
        new_weight, new_first, new_second = update_call(
            place, features, pieces, origins, weight, anchor, first_moment, second_moment
        )
    else:
        mine = lax.dynamic_slice_in_dim(inputs, dp * slice_rows, slice_rows, 1)
        features = in_order(
            [mine] + [h[skip : skip + tokens] for h, (_, skip) in zip(held, sources[1:])],
            [origin(dp) for origin, _ in sources],
            tokens,
        )
        gathered = in_order(pieces, [origin(dp, row) for origin in origins], own)
        summed = lax.dot_general(
            features, gathered, (((0,), (0,)), ((), ())), preferred_element_type=F32
        )
        current = lax.dynamic_slice_in_dim(weight, dp * slice_rows, slice_rows, 0).astype(F32)
        new_weight, new_first, new_second = updated(
            summed,
            tokens * n_dp,
            current,
            anchor.astype(F32),
            first_moment,
            second_moment,
        )
        new_weight = new_weight.astype(BF16)
    input_grad = after(gparts[0], new_first)
    for s in range(1, n_col):
        input_grad = input_grad + shares[s].astype(F32)
    input_grad = input_grad.astype(BF16)
    return (outputs, input_grad, new_weight, new_first, new_second)


def solution(mesh):
    in_specs = (
        P("dp", "row"),
        P("row", "col"),
        P(("dp", "row"), "col"),
        P(("row", "dp"), "col"),
        P(("row", "dp"), "col"),
        P(("row", "dp"), "col"),
    )
    out_specs = (
        P(("dp", "row"), "col"),
        P(("dp", "col"), "row"),
        P(("row", "dp"), "col"),
        P(("row", "dp"), "col"),
        P(("row", "dp"), "col"),
    )
    return jax.shard_map(
        per_device, mesh=mesh, in_specs=in_specs, out_specs=out_specs, check_vma=False
    )
```

```python
import functools
import math

import jax
import jax.numpy as jnp
from jax import lax
from jax.experimental import pallas as pl
from jax.experimental.pallas import tpu as pltpu
from jax.sharding import PartitionSpec as P

beta_one = 0.9
beta_two = 0.999
learn_rate = 0.002
anchor_pull = 0.5
epsilon = 1e-08
step_count = 100.0

BF16, F32 = jnp.bfloat16, jnp.float32
MIB = 1 << 20


def block_of(size, most):
    return max(b for b in range(128, most + 1, 128) if size % b == 0)


def struct(shape, dtype):
    return jax.ShapeDtypeStruct(shape, dtype)


def run(kernel, name, grid, in_specs, out_specs, out_shape, scratch, limit, args, bytes_moved=1):
    return pl.pallas_call(
        kernel,
        name=name,
        grid_spec=pltpu.PrefetchScalarGridSpec(
            num_scalar_prefetch=1,
            grid=grid,
            in_specs=in_specs,
            out_specs=out_specs,
            scratch_shapes=scratch,
        ),
        out_shape=out_shape,
        compiler_params=pltpu.CompilerParams(vmem_limit_bytes=limit * MIB),
        cost_estimate=pl.CostEstimate(
            flops=1, bytes_accessed=bytes_moved, transcendentals=0
        ),
    )(*args)


def fixed(shape):
    return pl.BlockSpec(shape, lambda j, place: (0,) * len(shape))


def columns(rows, width):
    return pl.BlockSpec((rows, width), lambda j, place: (0, j))


def forward_kernel(n_row, own, slice_rows, targets, cuts, place, x_ref, *rest):
    w_refs, rest = rest[:cuts], rest[cuts:]
    parts, sent, xs = rest[:n_row], rest[n_row:-1], rest[-1]
    dp, row = place[0], place[1]
    tokens = x_ref.shape[0]

    @pl.when(pl.program_id(0) == 0)
    def _():
        for s in range(n_row):
            start = pl.multiple_of(lax.rem(row + s, n_row) * own, own)
            xs[s * own : (s + 1) * own, :] = x_ref[pl.ds(start, own), :]
        for out, owners in zip(sent, targets):
            for k, owner in enumerate(owners):
                start = pl.multiple_of(owner(dp) * slice_rows, slice_rows)
                out[k * tokens : (k + 1) * tokens, :] = x_ref[:, pl.ds(start, slice_rows)]

    acc, at = None, 0
    for w_ref in w_refs:
        deep = w_ref.shape[0]
        part = jnp.dot(xs[:, at : at + deep], w_ref[...], preferred_element_type=F32)
        acc, at = part if acc is None else acc + part, at + deep
    for s in range(n_row):
        parts[s][...] = acc[s * own : (s + 1) * own].astype(parts[s].dtype)


def forward_call(place, inputs, weight, own, n_row, slice_rows, targets):
    tokens, depth = inputs.shape
    width = weight.shape[1]
    block = block_of(width, 512)
    cuts = 4 if depth % 1024 == 0 else 1
    sent = [(len(owners) * tokens, slice_rows) for owners in targets]
    return run(
        functools.partial(forward_kernel, n_row, own, slice_rows, targets, cuts),
        "forward",
        (width // block,),
        [fixed((tokens, depth))]
        + [
            pl.BlockSpec(
                (depth // cuts, block), lambda j, place, k=k: (k, j)
            )
            for k in range(cuts)
        ],
        [columns(own, block)] * n_row + [fixed(shape) for shape in sent],
        [struct((own, width), F32)]
        + [struct((own, width), BF16)] * (n_row - 1)
        + [struct(shape, BF16) for shape in sent],
        [pltpu.VMEM((tokens, depth), BF16)],
        52,
        (place, inputs, *[weight] * cuts),
    )


def input_grad_kernel(n_row, own, cuts, place, *rest):
    pieces, w_refs = rest[:n_row], rest[n_row : n_row + cuts]
    out, cs = rest[n_row + cuts :]
    row = place[1]

    @pl.when(pl.program_id(0) == 0)
    def _():
        for s in range(n_row):
            start = pl.multiple_of(lax.rem(row - s + n_row, n_row) * own, own)
            cs[pl.ds(start, own), :] = pieces[s][...]

    acc, at = None, 0
    for w_ref in w_refs:
        deep = w_ref.shape[1]
        part = lax.dot_general(
            cs[:, at : at + deep],
            w_ref[...],
            (((1,), (1,)), ((), ())),
            preferred_element_type=F32,
        )
        acc, at = part if acc is None else acc + part, at + deep
    out[...] = acc.astype(BF16)


def input_grad_call(place, by_row, weight, n_row):
    own, width = by_row[0].shape
    depth = weight.shape[0]
    block = block_of(depth, 256)
    cuts = 2 if width % 512 == 0 else 1
    return run(
        functools.partial(input_grad_kernel, n_row, own, cuts),
        "input_grad",
        (depth // block,),
        [fixed((own, width))] * n_row
        + [
            pl.BlockSpec(
                (block, width // cuts), lambda j, place, k=k: (j, k)
            )
            for k in range(cuts)
        ],
        columns(n_row * own, block),
        struct((n_row * own, depth), BF16),
        [pltpu.VMEM((n_row * own, width), BF16)],
        52,
        (place, *by_row, *[weight] * cuts),
    )


def features_kernel(sources, tokens, place, *rest):
    n = len(sources)
    pieces, out, xs = rest[:n], rest[n], rest[n + 1]
    for piece, (origin, skip) in zip(pieces, sources):
        start = pl.multiple_of(origin(place[0]) * tokens, tokens)
        xs[pl.ds(start, tokens), :] = piece[skip : skip + tokens, :]
    out[...] = xs[...].T


def features_call(place, inputs, held, sources, slice_rows):
    tokens, n_dp = inputs.shape[0], len(sources)
    return run(
        functools.partial(features_kernel, sources, tokens),
        "features",
        (1,),
        [pl.BlockSpec((tokens, slice_rows), lambda j, place: (0, place[0]))]
        + [fixed(piece.shape) for piece in held],
        fixed((slice_rows, n_dp * tokens)),
        struct((slice_rows, n_dp * tokens), BF16),
        [pltpu.VMEM((n_dp * tokens, slice_rows), BF16)],
        16,
        (place, inputs, *held),
    )


def inverse(value):
    guess = pl.reciprocal(value, approx=True)
    return guess * (2.0 - value * guess)


def updated(grad_sum, tokens_all, current, anchor, first, second, invert):
    grad = grad_sum * (1.0 / tokens_all) + anchor_pull * (current - anchor)
    first = beta_one * first + (1.0 - beta_one) * grad
    second = beta_two * second + (1.0 - beta_two) * grad * grad
    root = math.sqrt(1.0 / (1.0 - beta_two**step_count))
    scale = learn_rate / (1.0 - beta_one**step_count) / root
    spread = second * lax.rsqrt(second) + epsilon / root
    return current - (scale * first) * invert(spread), first, second


def update_kernel(origins, tokens_all, chunk, place, x_ref, *rest):
    n = len(origins)
    pieces = rest[:n]
    w_ref, a_ref, m_ref, v_ref, new_w, new_m, new_v, cs, acc = rest[n:]
    own = pieces[0].shape[0]
    for piece, origin in zip(pieces, origins):
        cs[pl.ds(pl.multiple_of(origin(place[0], place[1]) * own, own), own), :] = piece[...]
    acc[...] = jnp.dot(x_ref[...], cs[...], preferred_element_type=F32)

    @pl.loop(0, acc.shape[0] // chunk, unroll=4)
    def _(i):
        at = pl.ds(pl.multiple_of(i * chunk, chunk), chunk)
        weight, first, second = updated(
            acc[at, :],
            tokens_all,
            w_ref[at, :].astype(F32),
            a_ref[at, :].astype(F32),
            m_ref[at, :],
            v_ref[at, :],
            inverse,
        )
        new_w[at, :] = weight.astype(BF16)
        new_m[at, :] = first
        new_v[at, :] = second


def update_call(place, features, pieces, origins, weight, anchor, first, second):
    rows, width = first.shape
    tokens_all = features.shape[1]
    block = block_of(width, 512)
    own = pieces[0].shape[0]
    tile = columns(rows, block)
    return run(
        functools.partial(update_kernel, origins, tokens_all, math.gcd(rows, 32)),
        "update",
        (width // block,),
        [fixed((rows, tokens_all))]
        + [columns(own, block)] * len(pieces)
        + [pl.BlockSpec((rows, block), lambda j, place: (place[0], j)), tile, tile, tile],
        [tile] * 3,
        [struct((rows, width), BF16), struct((rows, width), F32), struct((rows, width), F32)],
        [pltpu.VMEM((tokens_all, block), BF16), pltpu.VMEM((rows, block), F32)],
        40,
        (place, features, *pieces, weight, anchor, first, second),
    )


def after(value, *others):
    return lax.optimization_barrier((value, *others))[0]


def per_device(inputs, weight, cotangent, anchor, first_moment, second_moment):
    n_dp, n_row, n_col = (lax.axis_size(a) for a in ("dp", "row", "col"))
    dp, row, col = (lax.axis_index(a) for a in ("dp", "row", "col"))
    place = jnp.stack([dp, row, col]).astype(jnp.int32)
    cores = 2 if n_dp % 2 == 0 else 1
    chips = n_dp // cores
    tokens = inputs.shape[0]
    own = cotangent.shape[0]
    share = tokens // n_col
    slice_rows = weight.shape[0] // n_dp
    tiled = own % 16 == 0 and share % 16 == 0 and slice_rows % 128 == 0

    def along(axis, n, shift):
        return lambda a: lax.ppermute(a, axis, [(i, (i + shift) % n) for i in range(n)])

    def chip_shift(shift):
        return along("dp", n_dp, shift * cores)

    def swap_cores(a):
        return lax.ppermute(a, "dp", [(i, i ^ 1) for i in range(n_dp)])

    def in_order(pieces, places, rows):
        whole = jnp.zeros((len(pieces) * rows, pieces[0].shape[1]), pieces[0].dtype)
        for piece, at in zip(pieces, places):
            whole = lax.dynamic_update_slice_in_dim(whole, piece, at * rows, 0)
        return whole

    def dp_of(dp, c, flip):
        core = lax.rem(dp, cores)
        return lax.rem(dp - core - c * cores + n_dp, n_dp) + (1 - core if flip else core)

    by_row = [cotangent] + [along("row", n_row, s)(cotangent) for s in range(1, n_row)]
    by_chip = {(c, 0): chip_shift(c)(cotangent) for c in range(1, chips)}
    swapped = {(0, 0): swap_cores(cotangent)} if cores == 2 else {}

    flips = range(cores)
    targets = [[functools.partial(dp_of, c=0, flip=1)]] if cores == 2 else []
    targets += [[functools.partial(dp_of, c=chips - c, flip=f) for f in flips] for c in range(1, chips)]
    if tiled:
        made = forward_call(place, inputs, weight, own, n_row, slice_rows, targets)
        parts, to_send = made[:n_row], made[n_row:]
    else:
        part = jnp.dot(inputs, weight, preferred_element_type=F32)
        parts = [
            lax.dynamic_slice_in_dim(part, lax.rem(row + s, n_row) * own, own, 0).astype(
                BF16 if s else F32
            )
            for s in range(n_row)
        ]
        to_send = [
            jnp.concatenate(
                [
                    lax.dynamic_slice_in_dim(inputs, owner(dp) * slice_rows, slice_rows, 1)
                    for owner in owners
                ],
                0,
            )
            for owners in targets
        ]
    to_send = list(to_send)
    sums = [
        along("row", n_row, s)(after(parts[s], *swapped.values())) for s in range(1, n_row)
    ]
    near = [swap_cores(to_send.pop(0))] if cores == 2 else []
    first = [by_chip[c, 0] for c in range(1, chips)]
    far = [chip_shift(c)(after(to_send[c - 1], *first)) for c in range(1, chips)]
    for s in range(1, n_row):
        by_row[s] = after(by_row[s], parts[0], *near, *first, *swapped.values())
        if cores == 2:
            swapped[0, s] = swap_cores(by_row[s])
    if cores == 2:
        for c in range(1, chips):
            swapped[c, 0] = swap_cores(by_chip[c, 0])

    if tiled:
        gpart = input_grad_call(place, by_row, weight, n_row)
    else:
        gathered = in_order(by_row, [lax.rem(row - s + n_row, n_row) for s in range(n_row)], own)
        gpart = lax.dot_general(
            gathered, weight, (((1,), (1,)), ((), ())), preferred_element_type=F32
        ).astype(BF16)
    gparts = lax.all_to_all(gpart, "col", 0, 0, tiled=True)
    for s in range(1, n_row):
        for c in range(1, chips):
            by_chip[c, s] = chip_shift(c)(by_row[s])
    outputs = parts[0]
    for part in sums:
        outputs = outputs + part.astype(F32)
    outputs = outputs.astype(BF16)

    held, sources = list(near), [(functools.partial(dp_of, c=0, flip=0), 0)]
    if cores == 2:
        sources.append((functools.partial(dp_of, c=0, flip=1), 0))
    for c in range(1, chips):
        for f in flips:
            piece = far[c - 1]
            held.append(swap_cores(piece) if f else piece)
            sources.append((functools.partial(dp_of, c=c, flip=f), f * tokens))
    pieces, origins = [], []
    for c in range(chips):
        for s in range(n_row):

            def origin(dp, row, c=c, s=s, flip=0):
                return dp_of(dp, c, flip) * n_row + lax.rem(row - s + n_row, n_row)

            piece = by_chip[c, s] if c else by_row[s]
            pieces.append(piece)
            origins.append(origin)
            if cores == 2:
                other = swapped[c, s] if (c, s) in swapped else swap_cores(piece)
                pieces.append(other)
                origins.append(functools.partial(origin, flip=1))

    if tiled:
        features = features_call(place, inputs, held, sources, slice_rows)
        new_weight, new_first, new_second = update_call(
            place, features, pieces, origins, weight, anchor, first_moment, second_moment
        )
    else:
        mine = lax.dynamic_slice_in_dim(inputs, dp * slice_rows, slice_rows, 1)
        features = in_order(
            [mine] + [h[skip : skip + tokens] for h, (_, skip) in zip(held, sources[1:])],
            [origin(dp) for origin, _ in sources],
            tokens,
        )
        gathered = in_order(pieces, [origin(dp, row) for origin in origins], own)
        summed = lax.dot_general(
            features, gathered, (((0,), (0,)), ((), ())), preferred_element_type=F32
        )
        current = lax.dynamic_slice_in_dim(weight, dp * slice_rows, slice_rows, 0).astype(F32)
        new_weight, new_first, new_second = updated(
            summed,
            tokens * n_dp,
            current,
            anchor.astype(F32),
            first_moment,
            second_moment,
            lambda value: 1.0 / value,
        )
        new_weight = new_weight.astype(BF16)
    input_grad = sum(
        lax.slice_in_dim(gparts, k * share, (k + 1) * share).astype(F32) for k in range(n_col)
    ).astype(BF16)
    return (outputs, input_grad, new_weight, new_first, new_second)


def solution(mesh):
    in_specs = (
        P("dp", "row"),
        P("row", "col"),
        P(("dp", "row"), "col"),
        P(("row", "dp"), "col"),
        P(("row", "dp"), "col"),
        P(("row", "dp"), "col"),
    )
    out_specs = (
        P(("dp", "row"), "col"),
        P(("dp", "col"), "row"),
        P(("row", "dp"), "col"),
        P(("row", "dp"), "col"),
        P(("row", "dp"), "col"),
    )
    return jax.shard_map(
        per_device, mesh=mesh, in_specs=in_specs, out_specs=out_specs, check_vma=False
    )
```

```python
import functools
import math

import jax
import jax.numpy as jnp
from jax import lax
from jax.experimental import pallas as pl
from jax.experimental.pallas import tpu as pltpu
from jax.sharding import PartitionSpec as P

beta_one = 0.9
beta_two = 0.999
learn_rate = 0.002
anchor_pull = 0.5
epsilon = 1e-08
step_count = 100.0

BF16, F32 = jnp.bfloat16, jnp.float32
MIB = 1 << 20


def block_of(size, most):
    return max(b for b in range(128, most + 1, 128) if size % b == 0)


def struct(shape, dtype):
    return jax.ShapeDtypeStruct(shape, dtype)


def run(kernel, name, grid, in_specs, out_specs, out_shape, scratch, limit, args, bytes_moved=1):
    return pl.pallas_call(
        kernel,
        name=name,
        grid_spec=pltpu.PrefetchScalarGridSpec(
            num_scalar_prefetch=1,
            grid=grid,
            in_specs=in_specs,
            out_specs=out_specs,
            scratch_shapes=scratch,
        ),
        out_shape=out_shape,
        compiler_params=pltpu.CompilerParams(vmem_limit_bytes=limit * MIB),
        cost_estimate=pl.CostEstimate(
            flops=1, bytes_accessed=bytes_moved, transcendentals=0
        ),
    )(*args)


def in_hbm(array):
    return pltpu.with_memory_space_constraint(array, pltpu.HBM)


def load_parts(source, target, sems, axis, part):
    loads = []
    for k in range(source.shape[axis] // part):
        at = (slice(None),) * axis + (pl.ds(k * part, part),)
        loads.append((at, pltpu.make_async_copy(source.at[at], target.at[at], sems.at[k])))
    for _, load in loads:
        load.start()
    return loads


def fixed(shape):
    return pl.BlockSpec(shape, lambda j, place: (0,) * len(shape))


def columns(rows, width):
    return pl.BlockSpec((rows, width), lambda j, place: (0, j))


def forward_kernel(n_row, own, slice_rows, targets, part, place, x_ref, w_hbm, *rest):
    outs, sent, (xs, ws, sems) = rest[:n_row], rest[n_row:-3], rest[-3:]
    dp, row = place[0], place[1]
    tokens = x_ref.shape[0]
    loads = load_parts(w_hbm, ws, sems, 1, part)
    for s in range(n_row):
        start = pl.multiple_of(lax.rem(row + s, n_row) * own, own)
        xs[s * own : (s + 1) * own, :] = x_ref[pl.ds(start, own), :]
    for out, owners in zip(sent, targets):
        for k, owner in enumerate(owners):
            start = pl.multiple_of(owner(dp) * slice_rows, slice_rows)
            out[k * tokens : (k + 1) * tokens, :] = x_ref[:, pl.ds(start, slice_rows)]
    for at, load in loads:
        load.wait()
        acc = jnp.dot(xs[...], ws[at], preferred_element_type=F32)
        for s in range(n_row):
            outs[s][at] = acc[s * own : (s + 1) * own].astype(outs[s].dtype)


def forward_call(place, inputs, weight, own, n_row, slice_rows, targets):
    tokens, depth = inputs.shape
    width = weight.shape[1]
    part = block_of(width, 512)
    sent = [(len(owners) * tokens, slice_rows) for owners in targets]
    return run(
        functools.partial(forward_kernel, n_row, own, slice_rows, targets, part),
        "forward",
        (1,),
        [fixed((tokens, depth)), pl.BlockSpec(memory_space=pltpu.HBM)],
        [fixed((own, width))] * n_row + [fixed(shape) for shape in sent],
        [struct((own, width), F32)]
        + [struct((own, width), BF16)] * (n_row - 1)
        + [struct(shape, BF16) for shape in sent],
        [
            pltpu.VMEM((tokens, depth), BF16),
            pltpu.VMEM((depth, width), BF16),
            pltpu.SemaphoreType.DMA((width // part,)),
        ],
        28,
        (place, inputs, in_hbm(weight)),
    )


def input_grad_kernel(n_row, own, part, place, *rest):
    pieces, w_hbm, out, (cs, ws, sems) = rest[:n_row], rest[n_row], rest[n_row + 1], rest[-3:]
    loads = load_parts(w_hbm, ws, sems, 0, part)
    for s in range(n_row):
        start = pl.multiple_of(lax.rem(place[1] - s + n_row, n_row) * own, own)
        cs[pl.ds(start, own), :] = pieces[s][...]
    for k, (at, load) in enumerate(loads):
        load.wait()
        acc = lax.dot_general(
            cs[...], ws[at], (((1,), (1,)), ((), ())), preferred_element_type=F32
        )
        out[:, k * part : (k + 1) * part] = acc.astype(BF16)


def input_grad_call(place, by_row, weight, n_row):
    own, width = by_row[0].shape
    depth = weight.shape[0]
    part = block_of(depth, 256)
    return run(
        functools.partial(input_grad_kernel, n_row, own, part),
        "input_grad",
        (1,),
        [fixed((own, width))] * n_row + [pl.BlockSpec(memory_space=pltpu.HBM)],
        fixed((n_row * own, depth)),
        struct((n_row * own, depth), BF16),
        [
            pltpu.VMEM((n_row * own, width), BF16),
            pltpu.VMEM((depth, width), BF16),
            pltpu.SemaphoreType.DMA((depth // part,)),
        ],
        28,
        (place, *by_row, in_hbm(weight)),
    )


def features_kernel(sources, tokens, place, *rest):
    n = len(sources)
    pieces, out, xs = rest[:n], rest[n], rest[n + 1]
    for piece, (origin, skip) in zip(pieces, sources):
        start = pl.multiple_of(origin(place[0]) * tokens, tokens)
        xs[pl.ds(start, tokens), :] = piece[skip : skip + tokens, :]
    out[...] = xs[...].T


def features_call(place, inputs, held, sources, slice_rows):
    tokens, n_dp = inputs.shape[0], len(sources)
    return run(
        functools.partial(features_kernel, sources, tokens),
        "features",
        (1,),
        [pl.BlockSpec((tokens, slice_rows), lambda j, place: (0, place[0]))]
        + [fixed(piece.shape) for piece in held],
        fixed((slice_rows, n_dp * tokens)),
        struct((slice_rows, n_dp * tokens), BF16),
        [pltpu.VMEM((n_dp * tokens, slice_rows), BF16)],
        16,
        (place, inputs, *held),
    )


def inverse(value):
    guess = pl.reciprocal(value, approx=True)
    return guess * (2.0 - value * guess)


def updated(grad_sum, tokens_all, current, anchor, first, second, invert):
    grad = grad_sum * (1.0 / tokens_all) + anchor_pull * (current - anchor)
    first = beta_one * first + (1.0 - beta_one) * grad
    second = beta_two * second + (1.0 - beta_two) * grad * grad
    root = math.sqrt(1.0 / (1.0 - beta_two**step_count))
    scale = learn_rate / (1.0 - beta_one**step_count) / root
    spread = second * lax.rsqrt(second) + epsilon / root
    return current - (scale * first) * invert(spread), first, second


def update_kernel(origins, tokens_all, chunk, place, x_ref, *rest):
    n = len(origins)
    pieces = rest[:n]
    w_ref, a_ref, m_ref, v_ref = rest[n : n + 4]
    new_w, new_m, new_v, cs, acc = rest[-5:]
    own = pieces[0].shape[0]
    for piece, origin in zip(pieces, origins):
        cs[pl.ds(pl.multiple_of(origin(place[0], place[1]) * own, own), own), :] = piece[...]
    acc[...] = jnp.dot(x_ref[...], cs[...], preferred_element_type=F32)

    @pl.loop(0, acc.shape[0] // chunk, unroll=4)
    def _(i):
        at = pl.ds(pl.multiple_of(i * chunk, chunk), chunk)
        weight, first, second = updated(
            acc[at, :],
            tokens_all,
            w_ref[at, :].astype(F32),
            a_ref[at, :].astype(F32),
            m_ref[at, :],
            v_ref[at, :],
            inverse,
        )
        new_w[at, :] = weight.astype(BF16)
        new_m[at, :] = first
        new_v[at, :] = second


def update_call(place, features, pieces, origins, start, stop, held, made):
    weight, anchor, first, second = held
    rows, width = first.shape
    tokens_all = features.shape[1]
    block = block_of(math.gcd(start, stop), 512)
    own = pieces[0].shape[0]
    base = start // block

    def from_base(rows):
        return pl.BlockSpec((rows, block), lambda j, place: (0, j + base))

    tile = from_base(rows)
    return pl.pallas_call(
        functools.partial(update_kernel, origins, tokens_all, math.gcd(rows, 32)),
        name="update",
        grid_spec=pltpu.PrefetchScalarGridSpec(
            num_scalar_prefetch=1,
            grid=((stop - start) // block,),
            in_specs=[fixed((rows, tokens_all))]
            + [from_base(own) if p.shape[1] == width else columns(own, block) for p in pieces]
            + [pl.BlockSpec((rows, block), lambda j, place: (place[0], j + base))]
            + [tile] * 3
            + [pl.BlockSpec(memory_space=pltpu.HBM)] * len(made),
            out_specs=[tile] * 3,
            scratch_shapes=[pltpu.VMEM((tokens_all, block), BF16), pltpu.VMEM((rows, block), F32)],
        ),
        out_shape=[
            struct((rows, width), BF16),
            struct((rows, width), F32),
            struct((rows, width), F32),
        ],
        input_output_aliases={6 + len(pieces) + k: k for k in range(len(made))},
        compiler_params=pltpu.CompilerParams(vmem_limit_bytes=28 * MIB),
        cost_estimate=pl.CostEstimate(flops=1, bytes_accessed=1, transcendentals=0),
    )(place, features, *pieces, *map(in_hbm, held), *made)


def after(value, *others):
    return lax.optimization_barrier((value, *others))[0]


def per_device(inputs, weight, cotangent, anchor, first_moment, second_moment):
    n_dp, n_row, n_col = (lax.axis_size(a) for a in ("dp", "row", "col"))
    dp, row, col = (lax.axis_index(a) for a in ("dp", "row", "col"))
    place = jnp.stack([dp, row, col]).astype(jnp.int32)
    cores = 2 if n_dp % 2 == 0 else 1
    chips = n_dp // cores
    tokens = inputs.shape[0]
    own = cotangent.shape[0]
    share = tokens // n_col
    slice_rows = weight.shape[0] // n_dp
    tiled = own % 16 == 0 and share % 16 == 0 and slice_rows % 128 == 0

    def along(axis, n, shift):
        return lambda a: lax.ppermute(a, axis, [(i, (i + shift) % n) for i in range(n)])

    def chip_shift(shift):
        return along("dp", n_dp, shift * cores)

    def swap_cores(a):
        return lax.ppermute(a, "dp", [(i, i ^ 1) for i in range(n_dp)])

    def in_order(pieces, places, rows):
        whole = jnp.zeros((len(pieces) * rows, pieces[0].shape[1]), pieces[0].dtype)
        for piece, at in zip(pieces, places):
            whole = lax.dynamic_update_slice_in_dim(whole, piece, at * rows, 0)
        return whole

    def dp_of(dp, c, flip):
        core = lax.rem(dp, cores)
        return lax.rem(dp - core - c * cores + n_dp, n_dp) + (1 - core if flip else core)

    by_row = [cotangent] + [along("row", n_row, s)(cotangent) for s in range(1, n_row)]
    by_chip = {(c, 0): chip_shift(c)(cotangent) for c in range(1, chips)}
    swapped = {(0, 0): swap_cores(cotangent)} if cores == 2 else {}

    flips = range(cores)
    targets = [[functools.partial(dp_of, c=0, flip=1)]] if cores == 2 else []
    targets += [[functools.partial(dp_of, c=chips - c, flip=f) for f in flips] for c in range(1, chips)]
    if tiled:
        made = forward_call(place, inputs, weight, own, n_row, slice_rows, targets)
        parts, to_send = made[:n_row], made[n_row:]
    else:
        part = jnp.dot(inputs, weight, preferred_element_type=F32)
        parts = [
            lax.dynamic_slice_in_dim(part, lax.rem(row + s, n_row) * own, own, 0).astype(
                BF16 if s else F32
            )
            for s in range(n_row)
        ]
        to_send = [
            jnp.concatenate(
                [
                    lax.dynamic_slice_in_dim(inputs, owner(dp) * slice_rows, slice_rows, 1)
                    for owner in owners
                ],
                0,
            )
            for owners in targets
        ]
    to_send = list(to_send)
    sums = [
        along("row", n_row, s)(after(parts[s], *swapped.values())) for s in range(1, n_row)
    ]
    near = [swap_cores(to_send.pop(0))] if cores == 2 else []
    first = [by_chip[c, 0] for c in range(1, chips)]
    far = [chip_shift(c)(after(to_send[c - 1], *first)) for c in range(1, chips)]
    for s in range(1, n_row):
        by_row[s] = after(by_row[s], parts[0], *near, *first, *swapped.values())
        if cores == 2:
            swapped[0, s] = swap_cores(by_row[s])
    if cores == 2:
        for c in range(1, chips):
            swapped[c, 0] = swap_cores(by_chip[c, 0])

    if tiled:
        gpart = input_grad_call(place, by_row, weight, n_row)
    else:
        gathered = in_order(by_row, [lax.rem(row - s + n_row, n_row) for s in range(n_row)], own)
        gpart = lax.dot_general(
            gathered, weight, (((1,), (1,)), ((), ())), preferred_element_type=F32
        ).astype(BF16)
    gparts = lax.all_to_all(gpart, "col", 0, 0, tiled=True)
    width = cotangent.shape[1]
    block = block_of(width, 512)
    middle = (width // block + 1) // 2 * block
    cuts = [(0, middle), (middle, width)] if tiled and middle < width else [(0, width)]
    relayed = [{} for _ in cuts]
    for k, (start, stop) in enumerate(cuts):
        for s in range(1, n_row):
            for c in range(1, chips):
                piece = lax.slice_in_dim(by_row[s], start, stop, axis=1)
                if k:
                    piece = after(piece, *sums)
                relayed[k][c, s] = chip_shift(c)(piece)
    outputs = parts[0]
    for part in sums:
        outputs = outputs + part.astype(F32)
    outputs = outputs.astype(BF16)

    held, sources = list(near), [(functools.partial(dp_of, c=0, flip=0), 0)]
    if cores == 2:
        sources.append((functools.partial(dp_of, c=0, flip=1), 0))
    for c in range(1, chips):
        for f in flips:
            piece = far[c - 1]
            held.append(swap_cores(piece) if f else piece)
            sources.append((functools.partial(dp_of, c=c, flip=f), f * tokens))
    by_chip.update({(0, s): by_row[s] for s in range(n_row)})
    origins = []
    for c in range(chips):
        for s in range(n_row):
            for flip in range(cores):

                def origin(dp, row, c=c, s=s, flip=flip):
                    return dp_of(dp, c, flip) * n_row + lax.rem(row - s + n_row, n_row)

                origins.append(origin)

    def pieces_of(k, *before):
        pieces = []
        for c in range(chips):
            for s in range(n_row):
                piece = by_chip[c, s] if (c, s) in by_chip else relayed[k][c, s]
                pieces.append(piece)
                if cores == 2:
                    if (c, s) in by_chip and (c, s) not in swapped:
                        swapped[c, s] = swap_cores(piece)
                    pieces.append(
                        swapped[c, s] if (c, s) in swapped else swap_cores(after(piece, *before))
                    )
        return pieces

    if tiled:
        features = features_call(place, inputs, held, sources, slice_rows)
        held = (weight, anchor, first_moment, second_moment)
        made = []
        for k, (start, stop) in enumerate(cuts):
            made = update_call(place, features, pieces_of(k, *made[:1]), origins, start, stop, held, made)
        new_weight, new_first, new_second = made
    else:
        mine = lax.dynamic_slice_in_dim(inputs, dp * slice_rows, slice_rows, 1)
        features = in_order(
            [mine] + [h[skip : skip + tokens] for h, (_, skip) in zip(held, sources[1:])],
            [origin(dp) for origin, _ in sources],
            tokens,
        )
        gathered = in_order(pieces_of(0), [origin(dp, row) for origin in origins], own)
        summed = lax.dot_general(
            features, gathered, (((0,), (0,)), ((), ())), preferred_element_type=F32
        )
        current = lax.dynamic_slice_in_dim(weight, dp * slice_rows, slice_rows, 0).astype(F32)
        new_weight, new_first, new_second = updated(
            summed,
            tokens * n_dp,
            current,
            anchor.astype(F32),
            first_moment,
            second_moment,
            lambda value: 1.0 / value,
        )
        new_weight = new_weight.astype(BF16)
    gparts = after(gparts, new_first)
    input_grad = sum(
        lax.slice_in_dim(gparts, k * share, (k + 1) * share).astype(F32) for k in range(n_col)
    ).astype(BF16)
    return (outputs, input_grad, new_weight, new_first, new_second)


def solution(mesh):
    in_specs = (
        P("dp", "row"),
        P("row", "col"),
        P(("dp", "row"), "col"),
        P(("row", "dp"), "col"),
        P(("row", "dp"), "col"),
        P(("row", "dp"), "col"),
    )
    out_specs = (
        P(("dp", "row"), "col"),
        P(("dp", "col"), "row"),
        P(("row", "dp"), "col"),
        P(("row", "dp"), "col"),
        P(("row", "dp"), "col"),
    )
    return jax.shard_map(
        per_device, mesh=mesh, in_specs=in_specs, out_specs=out_specs, check_vma=False
    )
```

```python
import functools
import math

import jax
import jax.numpy as jnp
from jax import lax
from jax.experimental import pallas as pl
from jax.experimental.pallas import tpu as pltpu
from jax.sharding import PartitionSpec as P

beta_one = 0.9
beta_two = 0.999
learn_rate = 0.002
anchor_pull = 0.5
epsilon = 1e-08
step_count = 100.0

BF16, F32 = jnp.bfloat16, jnp.float32
MIB = 1 << 20


def block_of(size, most):
    return max(b for b in range(128, most + 1, 128) if size % b == 0)


def struct(shape, dtype):
    return jax.ShapeDtypeStruct(shape, dtype)


def run(kernel, name, grid, in_specs, out_specs, out_shape, scratch, limit, args, bytes_moved=1):
    return pl.pallas_call(
        kernel,
        name=name,
        grid_spec=pltpu.PrefetchScalarGridSpec(
            num_scalar_prefetch=1,
            grid=grid,
            in_specs=in_specs,
            out_specs=out_specs,
            scratch_shapes=scratch,
        ),
        out_shape=out_shape,
        compiler_params=pltpu.CompilerParams(vmem_limit_bytes=limit * MIB),
        cost_estimate=pl.CostEstimate(
            flops=1, bytes_accessed=bytes_moved, transcendentals=0
        ),
    )(*args)


def in_hbm(array):
    return pltpu.with_memory_space_constraint(array, pltpu.HBM)


def load_parts(source, target, sems, axis, part):
    loads = []
    for k in range(source.shape[axis] // part):
        at = (slice(None),) * axis + (pl.ds(k * part, part),)
        loads.append((at, pltpu.make_async_copy(source.at[at], target.at[at], sems.at[k])))
    for _, load in loads:
        load.start()
    return loads


def fixed(shape):
    return pl.BlockSpec(shape, lambda j, place: (0,) * len(shape))


def columns(rows, width):
    return pl.BlockSpec((rows, width), lambda j, place: (0, j))


def forward_kernel(n_row, own, slice_rows, targets, part, place, x_ref, w_hbm, *rest):
    outs, sent, (xs, ws, sems) = rest[:n_row], rest[n_row:-3], rest[-3:]
    dp, row = place[0], place[1]
    tokens = x_ref.shape[0]
    loads = load_parts(w_hbm, ws, sems, 1, part)
    for s in range(n_row):
        start = pl.multiple_of(lax.rem(row + s, n_row) * own, own)
        xs[s * own : (s + 1) * own, :] = x_ref[pl.ds(start, own), :]
    for out, owners in zip(sent, targets):
        for k, owner in enumerate(owners):
            start = pl.multiple_of(owner(dp) * slice_rows, slice_rows)
            out[k * tokens : (k + 1) * tokens, :] = x_ref[:, pl.ds(start, slice_rows)]
    for at, load in loads:
        load.wait()
        acc = jnp.dot(xs[...], ws[at], preferred_element_type=F32)
        for s in range(n_row):
            outs[s][at] = acc[s * own : (s + 1) * own].astype(outs[s].dtype)


def forward_call(place, inputs, weight, own, n_row, slice_rows, targets):
    tokens, depth = inputs.shape
    width = weight.shape[1]
    part = block_of(width, 512)
    sent = [(len(owners) * tokens, slice_rows) for owners in targets]
    return run(
        functools.partial(forward_kernel, n_row, own, slice_rows, targets, part),
        "forward",
        (1,),
        [fixed((tokens, depth)), pl.BlockSpec(memory_space=pltpu.HBM)],
        [fixed((own, width))] * n_row + [fixed(shape) for shape in sent],
        [struct((own, width), F32)]
        + [struct((own, width), BF16)] * (n_row - 1)
        + [struct(shape, BF16) for shape in sent],
        [
            pltpu.VMEM((tokens, depth), BF16),
            pltpu.VMEM((depth, width), BF16),
            pltpu.SemaphoreType.DMA((width // part,)),
        ],
        28,
        (place, inputs, in_hbm(weight)),
    )


def input_grad_kernel(n_row, own, part, place, *rest):
    pieces, w_hbm, out = rest[:n_row], rest[n_row], rest[n_row + 1]
    cs, turned, ws, sems = rest[-4:]
    loads = load_parts(w_hbm, ws, sems, 0, part)
    for s in range(n_row):
        start = pl.multiple_of(lax.rem(place[1] - s + n_row, n_row) * own, own)
        cs[pl.ds(start, own), :] = pieces[s][...]
    turned[...] = cs[...].T
    for k, (at, load) in enumerate(loads):
        load.wait()
        acc = jnp.dot(ws[at], turned[...], preferred_element_type=F32)
        out[:, k * part : (k + 1) * part] = acc.T.astype(BF16)


def input_grad_call(place, by_row, weight, n_row):
    own, width = by_row[0].shape
    depth = weight.shape[0]
    part = block_of(depth, 256)
    return run(
        functools.partial(input_grad_kernel, n_row, own, part),
        "input_grad",
        (1,),
        [fixed((own, width))] * n_row + [pl.BlockSpec(memory_space=pltpu.HBM)],
        fixed((n_row * own, depth)),
        struct((n_row * own, depth), BF16),
        [
            pltpu.VMEM((n_row * own, width), BF16),
            pltpu.VMEM((width, n_row * own), BF16),
            pltpu.VMEM((depth, width), BF16),
            pltpu.SemaphoreType.DMA((depth // part,)),
        ],
        28,
        (place, *by_row, in_hbm(weight)),
    )


def features_kernel(sources, tokens, place, *rest):
    n = len(sources)
    pieces, out, xs = rest[:n], rest[n], rest[n + 1]
    for piece, (origin, skip) in zip(pieces, sources):
        start = pl.multiple_of(origin(place[0]) * tokens, tokens)
        xs[pl.ds(start, tokens), :] = piece[skip : skip + tokens, :]
    out[...] = xs[...].T


def features_call(place, inputs, held, sources, slice_rows):
    tokens, n_dp = inputs.shape[0], len(sources)
    return run(
        functools.partial(features_kernel, sources, tokens),
        "features",
        (1,),
        [pl.BlockSpec((tokens, slice_rows), lambda j, place: (0, place[0]))]
        + [fixed(piece.shape) for piece in held],
        fixed((slice_rows, n_dp * tokens)),
        struct((slice_rows, n_dp * tokens), BF16),
        [pltpu.VMEM((n_dp * tokens, slice_rows), BF16)],
        16,
        (place, inputs, *held),
    )


def inverse(value):
    guess = pl.reciprocal(value, approx=True)
    return guess * (2.0 - value * guess)


def updated(grad_sum, tokens_all, current, anchor, first, second, invert):
    grad = grad_sum * (1.0 / tokens_all) + anchor_pull * (current - anchor)
    first = beta_one * first + (1.0 - beta_one) * grad
    second = beta_two * second + (1.0 - beta_two) * grad * grad
    root = math.sqrt(1.0 / (1.0 - beta_two**step_count))
    scale = learn_rate / (1.0 - beta_one**step_count) / root
    spread = second * lax.rsqrt(second) + epsilon / root
    return current - (scale * first) * invert(spread), first, second


def update_kernel(origins, tokens_all, chunk, place, x_ref, *rest):
    n = len(origins)
    pieces = rest[:n]
    w_ref, a_ref, m_ref, v_ref = rest[n : n + 4]
    new_w, new_m, new_v, cs, acc = rest[-5:]
    own = pieces[0].shape[0]
    for piece, origin in zip(pieces, origins):
        cs[pl.ds(pl.multiple_of(origin(place[0], place[1]) * own, own), own), :] = piece[...]
    acc[...] = jnp.dot(x_ref[...], cs[...], preferred_element_type=F32)

    @pl.loop(0, acc.shape[0] // chunk, unroll=4)
    def _(i):
        at = pl.ds(pl.multiple_of(i * chunk, chunk), chunk)
        weight, first, second = updated(
            acc[at, :],
            tokens_all,
            w_ref[at, :].astype(F32),
            a_ref[at, :].astype(F32),
            m_ref[at, :],
            v_ref[at, :],
            inverse,
        )
        new_w[at, :] = weight.astype(BF16)
        new_m[at, :] = first
        new_v[at, :] = second


def update_call(place, features, pieces, origins, start, stop, held, made):
    weight, anchor, first, second = held
    rows, width = first.shape
    tokens_all = features.shape[1]
    block = block_of(math.gcd(start, stop), 256)
    own = pieces[0].shape[0]
    base = start // block

    def from_base(rows):
        return pl.BlockSpec((rows, block), lambda j, place: (0, j + base))

    tile = from_base(rows)
    return pl.pallas_call(
        functools.partial(update_kernel, origins, tokens_all, math.gcd(rows, 32)),
        name="update",
        grid_spec=pltpu.PrefetchScalarGridSpec(
            num_scalar_prefetch=1,
            grid=((stop - start) // block,),
            in_specs=[fixed((rows, tokens_all))]
            + [from_base(own) if p.shape[1] == width else columns(own, block) for p in pieces]
            + [pl.BlockSpec((rows, block), lambda j, place: (place[0], j + base))]
            + [tile] * 3
            + [pl.BlockSpec(memory_space=pltpu.HBM)] * len(made),
            out_specs=[tile] * 3,
            scratch_shapes=[pltpu.VMEM((tokens_all, block), BF16), pltpu.VMEM((rows, block), F32)],
        ),
        out_shape=[
            struct((rows, width), BF16),
            struct((rows, width), F32),
            struct((rows, width), F32),
        ],
        input_output_aliases={6 + len(pieces) + k: k for k in range(len(made))},
        compiler_params=pltpu.CompilerParams(vmem_limit_bytes=28 * MIB),
        cost_estimate=pl.CostEstimate(flops=1, bytes_accessed=1, transcendentals=0),
    )(place, features, *pieces, *map(in_hbm, held), *made)


def after(value, *others):
    return lax.optimization_barrier((value, *others))[0]


def per_device(inputs, weight, cotangent, anchor, first_moment, second_moment):
    n_dp, n_row, n_col = (lax.axis_size(a) for a in ("dp", "row", "col"))
    dp, row, col = (lax.axis_index(a) for a in ("dp", "row", "col"))
    place = jnp.stack([dp, row, col]).astype(jnp.int32)
    cores = 2 if n_dp % 2 == 0 else 1
    chips = n_dp // cores
    tokens = inputs.shape[0]
    own = cotangent.shape[0]
    share = tokens // n_col
    slice_rows = weight.shape[0] // n_dp
    tiled = own % 16 == 0 and share % 16 == 0 and slice_rows % 128 == 0

    def along(axis, n, shift):
        return lambda a: lax.ppermute(a, axis, [(i, (i + shift) % n) for i in range(n)])

    def chip_shift(shift):
        return along("dp", n_dp, shift * cores)

    def swap_cores(a):
        return lax.ppermute(a, "dp", [(i, i ^ 1) for i in range(n_dp)])

    def in_order(pieces, places, rows):
        whole = jnp.zeros((len(pieces) * rows, pieces[0].shape[1]), pieces[0].dtype)
        for piece, at in zip(pieces, places):
            whole = lax.dynamic_update_slice_in_dim(whole, piece, at * rows, 0)
        return whole

    def dp_of(dp, c, flip):
        core = lax.rem(dp, cores)
        return lax.rem(dp - core - c * cores + n_dp, n_dp) + (1 - core if flip else core)

    by_row = [cotangent] + [along("row", n_row, s)(cotangent) for s in range(1, n_row)]
    by_chip = {(c, 0): chip_shift(c)(cotangent) for c in range(1, chips)}
    swapped = {(0, 0): swap_cores(cotangent)} if cores == 2 else {}

    flips = range(cores)
    targets = [[functools.partial(dp_of, c=0, flip=1)]] if cores == 2 else []
    targets += [[functools.partial(dp_of, c=chips - c, flip=f) for f in flips] for c in range(1, chips)]
    if tiled:
        made = forward_call(place, inputs, weight, own, n_row, slice_rows, targets)
        parts, to_send = made[:n_row], made[n_row:]
    else:
        part = jnp.dot(inputs, weight, preferred_element_type=F32)
        parts = [
            lax.dynamic_slice_in_dim(part, lax.rem(row + s, n_row) * own, own, 0).astype(
                BF16 if s else F32
            )
            for s in range(n_row)
        ]
        to_send = [
            jnp.concatenate(
                [
                    lax.dynamic_slice_in_dim(inputs, owner(dp) * slice_rows, slice_rows, 1)
                    for owner in owners
                ],
                0,
            )
            for owners in targets
        ]
    to_send = list(to_send)
    sums = [
        along("row", n_row, s)(after(parts[s], *swapped.values())) for s in range(1, n_row)
    ]
    near = [swap_cores(to_send.pop(0))] if cores == 2 else []
    first = [by_chip[c, 0] for c in range(1, chips)]
    far = [chip_shift(c)(after(to_send[c - 1], *first)) for c in range(1, chips)]
    for s in range(1, n_row):
        by_row[s] = after(by_row[s], parts[0], *near, *first, *swapped.values())
        if cores == 2:
            swapped[0, s] = swap_cores(by_row[s])
    if cores == 2:
        for c in range(1, chips):
            swapped[c, 0] = swap_cores(by_chip[c, 0])

    if tiled:
        gpart = input_grad_call(place, by_row, weight, n_row)
    else:
        gathered = in_order(by_row, [lax.rem(row - s + n_row, n_row) for s in range(n_row)], own)
        gpart = lax.dot_general(
            gathered, weight, (((1,), (1,)), ((), ())), preferred_element_type=F32
        ).astype(BF16)
    gparts = lax.all_to_all(gpart, "col", 0, 0, tiled=True)
    width = cotangent.shape[1]
    block = block_of(width, 512)
    middle = (width // block + 1) // 2 * block
    cuts = [(0, middle), (middle, width)] if tiled and middle < width else [(0, width)]
    relayed = [{} for _ in cuts]
    for k, (start, stop) in enumerate(cuts):
        for s in range(1, n_row):
            for c in range(1, chips):
                piece = lax.slice_in_dim(by_row[s], start, stop, axis=1)
                if k:
                    piece = after(piece, gpart)
                relayed[k][c, s] = chip_shift(c)(piece)
    outputs = parts[0]
    for part in sums:
        outputs = outputs + part.astype(F32)
    outputs = outputs.astype(BF16)

    held, sources = list(near), [(functools.partial(dp_of, c=0, flip=0), 0)]
    if cores == 2:
        sources.append((functools.partial(dp_of, c=0, flip=1), 0))
    for c in range(1, chips):
        for f in flips:
            piece = far[c - 1]
            held.append(swap_cores(piece) if f else piece)
            sources.append((functools.partial(dp_of, c=c, flip=f), f * tokens))
    by_chip.update({(0, s): by_row[s] for s in range(n_row)})
    origins = []
    for c in range(chips):
        for s in range(n_row):
            for flip in range(cores):

                def origin(dp, row, c=c, s=s, flip=flip):
                    return dp_of(dp, c, flip) * n_row + lax.rem(row - s + n_row, n_row)

                origins.append(origin)

    def pieces_of(k, *before):
        pieces = []
        for c in range(chips):
            for s in range(n_row):
                piece = by_chip[c, s] if (c, s) in by_chip else relayed[k][c, s]
                pieces.append(piece)
                if cores == 2:
                    if (c, s) in by_chip and (c, s) not in swapped:
                        swapped[c, s] = swap_cores(piece)
                    pieces.append(
                        swapped[c, s] if (c, s) in swapped else swap_cores(after(piece, *before))
                    )
        return pieces

    if tiled:
        features = features_call(place, inputs, held, sources, slice_rows)
        held = (weight, anchor, first_moment, second_moment)
        made = []
        for k, (start, stop) in enumerate(cuts):
            made = update_call(place, features, pieces_of(k, *made[:1]), origins, start, stop, held, made)
        new_weight, new_first, new_second = made
    else:
        mine = lax.dynamic_slice_in_dim(inputs, dp * slice_rows, slice_rows, 1)
        features = in_order(
            [mine] + [h[skip : skip + tokens] for h, (_, skip) in zip(held, sources[1:])],
            [origin(dp) for origin, _ in sources],
            tokens,
        )
        gathered = in_order(pieces_of(0), [origin(dp, row) for origin in origins], own)
        summed = lax.dot_general(
            features, gathered, (((0,), (0,)), ((), ())), preferred_element_type=F32
        )
        current = lax.dynamic_slice_in_dim(weight, dp * slice_rows, slice_rows, 0).astype(F32)
        new_weight, new_first, new_second = updated(
            summed,
            tokens * n_dp,
            current,
            anchor.astype(F32),
            first_moment,
            second_moment,
            lambda value: 1.0 / value,
        )
        new_weight = new_weight.astype(BF16)
    gparts = after(gparts, new_first)
    input_grad = sum(
        lax.slice_in_dim(gparts, k * share, (k + 1) * share).astype(F32) for k in range(n_col)
    ).astype(BF16)
    return (outputs, input_grad, new_weight, new_first, new_second)


def solution(mesh):
    in_specs = (
        P("dp", "row"),
        P("row", "col"),
        P(("dp", "row"), "col"),
        P(("row", "dp"), "col"),
        P(("row", "dp"), "col"),
        P(("row", "dp"), "col"),
    )
    out_specs = (
        P(("dp", "row"), "col"),
        P(("dp", "col"), "row"),
        P(("row", "dp"), "col"),
        P(("row", "dp"), "col"),
        P(("row", "dp"), "col"),
    )
    return jax.shard_map(
        per_device, mesh=mesh, in_specs=in_specs, out_specs=out_specs, check_vma=False
    )
```

```python
import functools
import math

import jax
import jax.numpy as jnp
from jax import lax
from jax.experimental import pallas as pl
from jax.experimental.pallas import tpu as pltpu
from jax.sharding import PartitionSpec as P

beta_one = 0.9
beta_two = 0.999
learn_rate = 0.002
anchor_pull = 0.5
epsilon = 1e-08
step_count = 100.0

BF16, F32 = jnp.bfloat16, jnp.float32
MIB = 1 << 20


def block_of(size, most):
    return max(b for b in range(128, most + 1, 128) if size % b == 0)


def struct(shape, dtype):
    return jax.ShapeDtypeStruct(shape, dtype)


def run(kernel, name, grid, in_specs, out_specs, out_shape, scratch, limit, args, bytes_moved=1):
    return pl.pallas_call(
        kernel,
        name=name,
        grid_spec=pltpu.PrefetchScalarGridSpec(
            num_scalar_prefetch=1,
            grid=grid,
            in_specs=in_specs,
            out_specs=out_specs,
            scratch_shapes=scratch,
        ),
        out_shape=out_shape,
        compiler_params=pltpu.CompilerParams(vmem_limit_bytes=limit * MIB),
        cost_estimate=pl.CostEstimate(
            flops=1, bytes_accessed=bytes_moved, transcendentals=0
        ),
    )(*args)


def in_hbm(array):
    return pltpu.with_memory_space_constraint(array, pltpu.HBM)


def load_parts(source, target, sems, axis, part):
    loads = []
    for k in range(source.shape[axis] // part):
        at = (slice(None),) * axis + (pl.ds(k * part, part),)
        loads.append((at, pltpu.make_async_copy(source.at[at], target.at[at], sems.at[k])))
    for _, load in loads:
        load.start()
    return loads


def fixed(shape):
    return pl.BlockSpec(shape, lambda j, place: (0,) * len(shape))


def columns(rows, width):
    return pl.BlockSpec((rows, width), lambda j, place: (0, j))


def forward_kernel(n_row, own, slice_rows, targets, part, place, x_hbm, w_hbm, *rest):
    outs, sent = rest[:n_row], rest[n_row:-4]
    xs, ws, x_sems, w_sems = rest[-4:]
    dp, row = place[0], place[1]
    tokens = xs.shape[0]
    x_loads = []
    for s in range(n_row):
        start = pl.multiple_of(lax.rem(row + s, n_row) * own, own)
        at = pl.ds(s * own, own)
        x_loads.append(
            pltpu.make_async_copy(x_hbm.at[pl.ds(start, own), :], xs.at[at, :], x_sems.at[s])
        )
        x_loads[-1].start()
    loads = load_parts(w_hbm, ws, w_sems, 1, part)
    for load in x_loads:
        load.wait()
    for out, owners in zip(sent, targets):
        for k, owner in enumerate(owners):
            columns = pl.ds(pl.multiple_of(owner(dp) * slice_rows, slice_rows), slice_rows)
            for s in range(n_row):
                start = pl.multiple_of(k * tokens + lax.rem(row + s, n_row) * own, own)
                out[pl.ds(start, own), :] = xs[s * own : (s + 1) * own, columns]
    for at, load in loads:
        load.wait()
        acc = jnp.dot(xs[...], ws[at], preferred_element_type=F32).astype(BF16)
        for s in range(n_row):
            outs[s][at] = acc[s * own : (s + 1) * own]


def forward_call(place, inputs, weight, own, n_row, slice_rows, targets):
    tokens, depth = inputs.shape
    width = weight.shape[1]
    part = block_of(width, 512)
    sent = [(len(owners) * tokens, slice_rows) for owners in targets]
    return run(
        functools.partial(forward_kernel, n_row, own, slice_rows, targets, part),
        "forward",
        (1,),
        [pl.BlockSpec(memory_space=pltpu.HBM)] * 2,
        [fixed((own, width))] * n_row + [fixed(shape) for shape in sent],
        [struct((own, width), BF16)] * n_row + [struct(shape, BF16) for shape in sent],
        [
            pltpu.VMEM((tokens, depth), BF16),
            pltpu.VMEM((depth, width), BF16),
            pltpu.SemaphoreType.DMA((n_row,)),
            pltpu.SemaphoreType.DMA((width // part,)),
        ],
        28,
        (place, in_hbm(inputs), in_hbm(weight)),
    )


def input_grad_kernel(n_row, own, part, place, *rest):
    pieces, w_hbm, out = rest[:n_row], rest[n_row], rest[n_row + 1]
    cs, turned, ws, acc, c_sems, w_sems = rest[-6:]
    c_loads = []
    for s in range(n_row):
        start = pl.multiple_of(lax.rem(place[1] - s + n_row, n_row) * own, own)
        c_loads.append(pltpu.make_async_copy(pieces[s], cs.at[pl.ds(start, own), :], c_sems.at[s]))
        c_loads[-1].start()
    loads = load_parts(w_hbm, ws, w_sems, 1, part)
    for load in c_loads:
        load.wait()
    turned[...] = cs[...].T
    for k, (at, load) in enumerate(loads):
        load.wait()
        product = jnp.dot(
            ws[at], turned[k * part : (k + 1) * part, :], preferred_element_type=F32
        )
        acc[...] = acc[...] + product if k else product
    out[...] = acc[...].T.astype(BF16)


def input_grad_call(place, by_row, weight, n_row):
    own, width = by_row[0].shape
    depth = weight.shape[0]
    part = block_of(width, 512)
    return run(
        functools.partial(input_grad_kernel, n_row, own, part),
        "input_grad",
        (1,),
        [pl.BlockSpec(memory_space=pl.ANY)] * n_row + [pl.BlockSpec(memory_space=pltpu.HBM)],
        fixed((n_row * own, depth)),
        struct((n_row * own, depth), BF16),
        [
            pltpu.VMEM((n_row * own, width), BF16),
            pltpu.VMEM((width, n_row * own), BF16),
            pltpu.VMEM((depth, width), BF16),
            pltpu.VMEM((depth, n_row * own), F32),
            pltpu.SemaphoreType.DMA((n_row,)),
            pltpu.SemaphoreType.DMA((width // part,)),
        ],
        32,
        (place, *by_row, in_hbm(weight)),
    )


def features_kernel(sources, tokens, place, *rest):
    n = len(sources)
    pieces, out, xs = rest[:n], rest[n], rest[n + 1]
    for piece, (origin, skip) in zip(pieces, sources):
        start = pl.multiple_of(origin(place[0]) * tokens, tokens)
        xs[pl.ds(start, tokens), :] = piece[skip : skip + tokens, :]
    out[...] = xs[...].T


def features_call(place, inputs, held, sources, slice_rows):
    tokens, n_dp = inputs.shape[0], len(sources)
    return run(
        functools.partial(features_kernel, sources, tokens),
        "features",
        (1,),
        [pl.BlockSpec((tokens, slice_rows), lambda j, place: (0, place[0]))]
        + [fixed(piece.shape) for piece in held],
        fixed((slice_rows, n_dp * tokens)),
        struct((slice_rows, n_dp * tokens), BF16),
        [pltpu.VMEM((n_dp * tokens, slice_rows), BF16)],
        16,
        (place, in_hbm(inputs), *held),
    )


def inverse(value):
    guess = pl.reciprocal(value, approx=True)
    return guess * (2.0 - value * guess)


def updated(grad_sum, tokens_all, current, anchor, first, second, invert):
    grad = grad_sum * (1.0 / tokens_all) + anchor_pull * (current - anchor)
    first = beta_one * first + (1.0 - beta_one) * grad
    second = beta_two * second + (1.0 - beta_two) * grad * grad
    root = math.sqrt(1.0 / (1.0 - beta_two**step_count))
    scale = learn_rate / (1.0 - beta_one**step_count) / root
    spread = second * lax.rsqrt(second) + epsilon / root
    return current - (scale * first) * invert(spread), first, second


def update_kernel(origins, tokens_all, chunk, place, x_ref, *rest):
    n = len(origins)
    pieces = rest[:n]
    w_ref, a_ref, m_ref, v_ref = rest[n : n + 4]
    new_w, new_m, new_v, cs, acc = rest[-5:]
    own = pieces[0].shape[0]
    for piece, origin in zip(pieces, origins):
        cs[pl.ds(pl.multiple_of(origin(place[0], place[1]) * own, own), own), :] = piece[...]
    acc[...] = jnp.dot(x_ref[...], cs[...], preferred_element_type=F32)

    @pl.loop(0, acc.shape[0] // chunk, unroll=4)
    def _(i):
        at = pl.ds(pl.multiple_of(i * chunk, chunk), chunk)
        weight, first, second = updated(
            acc[at, :],
            tokens_all,
            w_ref[at, :].astype(F32),
            a_ref[at, :].astype(F32),
            m_ref[at, :],
            v_ref[at, :],
            inverse,
        )
        new_w[at, :] = weight.astype(BF16)
        new_m[at, :] = first
        new_v[at, :] = second


def update_call(place, features, pieces, origins, start, stop, held, made):
    weight, anchor, first, second = held
    rows, width = first.shape
    tokens_all = features.shape[1]
    block = block_of(math.gcd(start, stop), 256)
    own = pieces[0].shape[0]
    base = start // block

    def from_base(rows):
        return pl.BlockSpec((rows, block), lambda j, place: (0, j + base))

    tile = from_base(rows)
    return pl.pallas_call(
        functools.partial(update_kernel, origins, tokens_all, math.gcd(rows, 32)),
        name="update",
        grid_spec=pltpu.PrefetchScalarGridSpec(
            num_scalar_prefetch=1,
            grid=((stop - start) // block,),
            in_specs=[fixed((rows, tokens_all))]
            + [from_base(own) if p.shape[1] == width else columns(own, block) for p in pieces]
            + [pl.BlockSpec((rows, block), lambda j, place: (place[0], j + base))]
            + [tile] * 3
            + [pl.BlockSpec(memory_space=pltpu.HBM)] * len(made),
            out_specs=[tile] * 3,
            scratch_shapes=[pltpu.VMEM((tokens_all, block), BF16), pltpu.VMEM((rows, block), F32)],
        ),
        out_shape=[
            struct((rows, width), BF16),
            struct((rows, width), F32),
            struct((rows, width), F32),
        ],
        input_output_aliases={6 + len(pieces) + k: k for k in range(len(made))},
        compiler_params=pltpu.CompilerParams(vmem_limit_bytes=28 * MIB),
        cost_estimate=pl.CostEstimate(flops=1, bytes_accessed=1, transcendentals=0),
    )(place, features, *pieces, *map(in_hbm, [*held, *made]))


def after(value, *others):
    return lax.optimization_barrier((value, *others))[0]


def per_device(inputs, weight, cotangent, anchor, first_moment, second_moment):
    n_dp, n_row, n_col = (lax.axis_size(a) for a in ("dp", "row", "col"))
    dp, row, col = (lax.axis_index(a) for a in ("dp", "row", "col"))
    place = jnp.stack([dp, row, col]).astype(jnp.int32)
    cores = 2 if n_dp % 2 == 0 else 1
    chips = n_dp // cores
    tokens = inputs.shape[0]
    own = cotangent.shape[0]
    share = tokens // n_col
    slice_rows = weight.shape[0] // n_dp
    tiled = own % 16 == 0 and share % 16 == 0 and slice_rows % 128 == 0

    def along(axis, n, shift):
        return lambda a: lax.ppermute(a, axis, [(i, (i + shift) % n) for i in range(n)])

    def chip_shift(shift):
        return along("dp", n_dp, shift * cores)

    def swap_cores(a):
        return lax.ppermute(a, "dp", [(i, i ^ 1) for i in range(n_dp)])

    def in_order(pieces, places, rows):
        whole = jnp.zeros((len(pieces) * rows, pieces[0].shape[1]), pieces[0].dtype)
        for piece, at in zip(pieces, places):
            whole = lax.dynamic_update_slice_in_dim(whole, piece, at * rows, 0)
        return whole

    def dp_of(dp, c, flip):
        core = lax.rem(dp, cores)
        return lax.rem(dp - core - c * cores + n_dp, n_dp) + (1 - core if flip else core)

    by_row = [cotangent] + [along("row", n_row, s)(cotangent) for s in range(1, n_row)]
    by_chip = {(c, 0): chip_shift(c)(cotangent) for c in range(1, chips)}
    swapped = {(0, 0): swap_cores(cotangent)} if cores == 2 else {}

    flips = range(cores)
    targets = [[functools.partial(dp_of, c=0, flip=1)]] if cores == 2 else []
    targets += [[functools.partial(dp_of, c=chips - c, flip=f) for f in flips] for c in range(1, chips)]
    if tiled:
        made = forward_call(place, inputs, weight, own, n_row, slice_rows, targets)
        parts, to_send = made[:n_row], made[n_row:]
    else:
        part = jnp.dot(inputs, weight, preferred_element_type=F32)
        parts = [
            lax.dynamic_slice_in_dim(part, lax.rem(row + s, n_row) * own, own, 0).astype(
                BF16
            )
            for s in range(n_row)
        ]
        to_send = [
            jnp.concatenate(
                [
                    lax.dynamic_slice_in_dim(inputs, owner(dp) * slice_rows, slice_rows, 1)
                    for owner in owners
                ],
                0,
            )
            for owners in targets
        ]
    to_send = list(to_send)
    sums = [
        along("row", n_row, s)(after(parts[s], *swapped.values())) for s in range(1, n_row)
    ]
    near = [swap_cores(to_send.pop(0))] if cores == 2 else []
    first = [by_chip[c, 0] for c in range(1, chips)]
    far = [chip_shift(c)(after(to_send[c - 1], *first)) for c in range(1, chips)]
    for s in range(1, n_row):
        by_row[s] = after(by_row[s], parts[0], *near, *first, *swapped.values())

    if tiled:
        gpart = input_grad_call(place, by_row, weight, n_row)
    else:
        gathered = in_order(by_row, [lax.rem(row - s + n_row, n_row) for s in range(n_row)], own)
        gpart = lax.dot_general(
            gathered, weight, (((1,), (1,)), ((), ())), preferred_element_type=F32
        ).astype(BF16)
    gparts = lax.all_to_all(gpart, "col", 0, 0, tiled=True)
    width = cotangent.shape[1]
    block = block_of(width, 512)
    middle = (width // block + 1) // 2 * block
    cuts = [(0, middle), (middle, width)] if tiled and middle < width else [(0, width)]
    relayed = [{} for _ in cuts]
    for k, (start, stop) in enumerate(cuts):
        for s in range(1, n_row):
            for c in range(1, chips):
                piece = lax.slice_in_dim(by_row[s], start, stop, axis=1)
                if k:
                    piece = after(piece, gpart)
                relayed[k][c, s] = chip_shift(c)(piece)
    outputs = parts[0].astype(F32)
    for part in sums:
        outputs = outputs + part.astype(F32)
    outputs = outputs.astype(BF16)

    held, sources = list(near), [(functools.partial(dp_of, c=0, flip=0), 0)]
    if cores == 2:
        sources.append((functools.partial(dp_of, c=0, flip=1), 0))
    for c in range(1, chips):
        for f in flips:
            piece = far[c - 1]
            held.append(swap_cores(after(piece, gpart)) if f else piece)
            sources.append((functools.partial(dp_of, c=c, flip=f), f * tokens))
    by_chip.update({(0, s): by_row[s] for s in range(n_row)})
    origins = []
    for c in range(chips):
        for s in range(n_row):
            for flip in range(cores):

                def origin(dp, row, c=c, s=s, flip=flip):
                    return dp_of(dp, c, flip) * n_row + lax.rem(row - s + n_row, n_row)

                origins.append(origin)

    def pieces_of(k, *before):
        pieces = []
        for c in range(chips):
            for s in range(n_row):
                piece = by_chip[c, s] if (c, s) in by_chip else relayed[k][c, s]
                pieces.append(piece)
                if cores == 2:
                    if (c, s) in by_chip and (c, s) not in swapped:
                        swapped[c, s] = swap_cores(after(piece, gpart))
                    pieces.append(
                        swapped[c, s] if (c, s) in swapped else swap_cores(after(piece, *before))
                    )
        return pieces

    if tiled:
        features = features_call(place, inputs, held, sources, slice_rows)
        held = (weight, anchor, first_moment, second_moment)
        made, before = [], [gpart]
        for k, (start, stop) in enumerate(cuts):
            pieces = pieces_of(k, *before)
            made = update_call(place, features, pieces, origins, start, stop, held, made)
            before = [made[0], gparts]
        new_weight, new_first, new_second = made
    else:
        mine = lax.dynamic_slice_in_dim(inputs, dp * slice_rows, slice_rows, 1)
        features = in_order(
            [mine] + [h[skip : skip + tokens] for h, (_, skip) in zip(held, sources[1:])],
            [origin(dp) for origin, _ in sources],
            tokens,
        )
        gathered = in_order(pieces_of(0, gpart), [origin(dp, row) for origin in origins], own)
        summed = lax.dot_general(
            features, gathered, (((0,), (0,)), ((), ())), preferred_element_type=F32
        )
        current = lax.dynamic_slice_in_dim(weight, dp * slice_rows, slice_rows, 0).astype(F32)
        new_weight, new_first, new_second = updated(
            summed,
            tokens * n_dp,
            current,
            anchor.astype(F32),
            first_moment,
            second_moment,
            lambda value: 1.0 / value,
        )
        new_weight = new_weight.astype(BF16)
    gparts = after(gparts, new_first)
    input_grad = sum(
        lax.slice_in_dim(gparts, k * share, (k + 1) * share).astype(F32) for k in range(n_col)
    ).astype(BF16)
    return (outputs, input_grad, new_weight, new_first, new_second)


def solution(mesh):
    in_specs = (
        P("dp", "row"),
        P("row", "col"),
        P(("dp", "row"), "col"),
        P(("row", "dp"), "col"),
        P(("row", "dp"), "col"),
        P(("row", "dp"), "col"),
    )
    out_specs = (
        P(("dp", "row"), "col"),
        P(("dp", "col"), "row"),
        P(("row", "dp"), "col"),
        P(("row", "dp"), "col"),
        P(("row", "dp"), "col"),
    )
    return jax.shard_map(
        per_device, mesh=mesh, in_specs=in_specs, out_specs=out_specs, check_vma=False
    )
```

```python
import functools
import math

import jax
import jax.numpy as jnp
from jax import lax
from jax.experimental import pallas as pl
from jax.experimental.pallas import tpu as pltpu
from jax.sharding import PartitionSpec as P

beta_one = 0.9
beta_two = 0.999
learn_rate = 0.002
anchor_pull = 0.5
epsilon = 1e-08
step_count = 100.0

BF16, F32 = jnp.bfloat16, jnp.float32
MIB = 1 << 20


def block_of(size, most):
    return max(b for b in range(128, most + 1, 128) if size % b == 0)


def struct(shape, dtype):
    return jax.ShapeDtypeStruct(shape, dtype)


def run(kernel, name, grid, in_specs, out_specs, out_shape, scratch, limit, args, bytes_moved=1):
    return pl.pallas_call(
        kernel,
        name=name,
        grid_spec=pltpu.PrefetchScalarGridSpec(
            num_scalar_prefetch=1,
            grid=grid,
            in_specs=in_specs,
            out_specs=out_specs,
            scratch_shapes=scratch,
        ),
        out_shape=out_shape,
        compiler_params=pltpu.CompilerParams(vmem_limit_bytes=limit * MIB),
        cost_estimate=pl.CostEstimate(
            flops=1, bytes_accessed=bytes_moved, transcendentals=0
        ),
    )(*args)


def in_hbm(array):
    return pltpu.with_memory_space_constraint(array, pltpu.HBM)


def in_vmem(array):
    return pltpu.with_memory_space_constraint(array, pltpu.VMEM)


def load_parts(source, target, sems, axis, part):
    loads = []
    for k in range(source.shape[axis] // part):
        at = (slice(None),) * axis + (pl.ds(k * part, part),)
        loads.append((at, pltpu.make_async_copy(source.at[at], target.at[at], sems.at[k])))
    for _, load in loads:
        load.start()
    return loads


def fixed(shape):
    return pl.BlockSpec(shape, lambda j, place: (0,) * len(shape))


def columns(rows, width):
    return pl.BlockSpec((rows, width), lambda j, place: (0, j))


def forward_kernel(n_row, own, slice_rows, targets, part, place, x_ref, w_hbm, *rest):
    outs, sent, (xs, ws, sems) = rest[:n_row], rest[n_row:-3], rest[-3:]
    dp, row = place[0], place[1]
    tokens = x_ref.shape[0]
    loads = load_parts(w_hbm, ws, sems, 1, part)
    for s in range(n_row):
        start = pl.multiple_of(lax.rem(row + s, n_row) * own, own)
        xs[s * own : (s + 1) * own, :] = x_ref[pl.ds(start, own), :]
    for out, owners in zip(sent, targets):
        for k, owner in enumerate(owners):
            start = pl.multiple_of(owner(dp) * slice_rows, slice_rows)
            out[k * tokens : (k + 1) * tokens, :] = x_ref[:, pl.ds(start, slice_rows)]
    for at, load in loads:
        load.wait()
        acc = jnp.dot(xs[...], ws[at], preferred_element_type=F32)
        for s in range(n_row):
            outs[s][at] = acc[s * own : (s + 1) * own].astype(outs[s].dtype)


def forward_call(place, inputs, weight, own, n_row, slice_rows, targets):
    tokens, depth = inputs.shape
    width = weight.shape[1]
    part = block_of(width, 512)
    sent = [(len(owners) * tokens, slice_rows) for owners in targets]
    return run(
        functools.partial(forward_kernel, n_row, own, slice_rows, targets, part),
        "forward",
        (1,),
        [fixed((tokens, depth)), pl.BlockSpec(memory_space=pltpu.HBM)],
        [fixed((own, width))] * n_row + [fixed(shape) for shape in sent],
        [struct((own, width), BF16)] * n_row + [struct(shape, BF16) for shape in sent],
        [
            pltpu.VMEM((tokens, depth), BF16),
            pltpu.VMEM((depth, width), BF16),
            pltpu.SemaphoreType.DMA((width // part,)),
        ],
        28,
        (place, inputs, in_hbm(weight)),
    )


def input_grad_kernel(n_row, own, place, *rest):
    pieces, w_ref, out, cs = rest[:n_row], rest[n_row], rest[n_row + 1], rest[n_row + 2]

    @pl.when(pl.program_id(0) == 0)
    def _():
        for s in range(n_row):
            start = pl.multiple_of(lax.rem(place[1] - s + n_row, n_row) * own, own)
            cs[pl.ds(start, own), :] = pieces[s][...]

    out[...] = lax.dot_general(
        cs[...], w_ref[...], (((1,), (1,)), ((), ())), preferred_element_type=F32
    ).astype(BF16)


def input_grad_call(place, by_row, weight, n_row):
    own, width = by_row[0].shape
    depth = weight.shape[0]
    block = block_of(depth, 256)
    return run(
        functools.partial(input_grad_kernel, n_row, own),
        "input_grad",
        (depth // block,),
        [fixed((own, width))] * n_row + [pl.BlockSpec((block, width), lambda j, place: (j, 0))],
        columns(n_row * own, block),
        struct((n_row * own, depth), BF16),
        [pltpu.VMEM((n_row * own, width), BF16)],
        14,
        (place, *by_row, in_vmem(weight)),
    )


def features_kernel(sources, tokens, place, *rest):
    n = len(sources)
    pieces, out, xs = rest[:n], rest[n], rest[n + 1]
    for piece, (origin, skip) in zip(pieces, sources):
        start = pl.multiple_of(origin(place[0]) * tokens, tokens)
        xs[pl.ds(start, tokens), :] = piece[skip : skip + tokens, :]
    out[...] = xs[...].T


def features_call(place, inputs, held, sources, slice_rows):
    tokens, n_dp = inputs.shape[0], len(sources)
    return run(
        functools.partial(features_kernel, sources, tokens),
        "features",
        (1,),
        [pl.BlockSpec((tokens, slice_rows), lambda j, place: (0, place[0]))]
        + [fixed(piece.shape) for piece in held],
        fixed((slice_rows, n_dp * tokens)),
        struct((slice_rows, n_dp * tokens), BF16),
        [pltpu.VMEM((n_dp * tokens, slice_rows), BF16)],
        16,
        (place, inputs, *held),
    )


def inverse(value):
    guess = pl.reciprocal(value, approx=True)
    return guess * (2.0 - value * guess)


def updated(grad_sum, tokens_all, current, anchor, first, second, invert):
    grad = grad_sum * (1.0 / tokens_all) + anchor_pull * (current - anchor)
    first = beta_one * first + (1.0 - beta_one) * grad
    second = beta_two * second + (1.0 - beta_two) * grad * grad
    root = math.sqrt(1.0 / (1.0 - beta_two**step_count))
    scale = learn_rate / (1.0 - beta_one**step_count) / root
    spread = second * lax.rsqrt(second) + epsilon / root
    return current - (scale * first) * invert(spread), first, second


def update_kernel(origins, tokens_all, chunk, place, x_ref, *rest):
    n = len(origins)
    pieces = rest[:n]
    w_ref, a_ref, m_ref, v_ref = rest[n : n + 4]
    new_w, new_m, new_v, cs, acc = rest[-5:]
    own = pieces[0].shape[0]
    for piece, origin in zip(pieces, origins):
        cs[pl.ds(pl.multiple_of(origin(place[0], place[1]) * own, own), own), :] = piece[...]
    acc[...] = jnp.dot(x_ref[...], cs[...], preferred_element_type=F32)

    @pl.loop(0, acc.shape[0] // chunk, unroll=4)
    def _(i):
        at = pl.ds(pl.multiple_of(i * chunk, chunk), chunk)
        weight, first, second = updated(
            acc[at, :],
            tokens_all,
            w_ref[at, :].astype(F32),
            a_ref[at, :].astype(F32),
            m_ref[at, :],
            v_ref[at, :],
            inverse,
        )
        new_w[at, :] = weight.astype(BF16)
        new_m[at, :] = first
        new_v[at, :] = second


def update_call(place, features, pieces, origins, start, stop, held, made):
    weight, anchor, first, second = held
    rows, width = first.shape
    tokens_all = features.shape[1]
    block = block_of(math.gcd(start, stop), 512)
    own = pieces[0].shape[0]
    base = start // block

    def from_base(rows):
        return pl.BlockSpec((rows, block), lambda j, place: (0, j + base))

    tile = from_base(rows)
    return pl.pallas_call(
        functools.partial(update_kernel, origins, tokens_all, math.gcd(rows, 32)),
        name="update",
        grid_spec=pltpu.PrefetchScalarGridSpec(
            num_scalar_prefetch=1,
            grid=((stop - start) // block,),
            in_specs=[fixed((rows, tokens_all))]
            + [from_base(own) if p.shape[1] == width else columns(own, block) for p in pieces]
            + [pl.BlockSpec((rows, block), lambda j, place: (place[0], j + base))]
            + [tile] * 3
            + [pl.BlockSpec(memory_space=pltpu.HBM)] * len(made),
            out_specs=[tile] * 3,
            scratch_shapes=[pltpu.VMEM((tokens_all, block), BF16), pltpu.VMEM((rows, block), F32)],
        ),
        out_shape=[
            struct((rows, width), BF16),
            struct((rows, width), F32),
            struct((rows, width), F32),
        ],
        input_output_aliases={6 + len(pieces) + k: k for k in range(len(made))},
        compiler_params=pltpu.CompilerParams(vmem_limit_bytes=22 * MIB),
        cost_estimate=pl.CostEstimate(flops=1, bytes_accessed=1, transcendentals=0),
    )(place, features, *pieces, *map(in_hbm, held), *made)


def after(value, *others):
    return lax.optimization_barrier((value, *others))[0]


def per_device(inputs, weight, cotangent, anchor, first_moment, second_moment):
    n_dp, n_row, n_col = (lax.axis_size(a) for a in ("dp", "row", "col"))
    dp, row, col = (lax.axis_index(a) for a in ("dp", "row", "col"))
    place = jnp.stack([dp, row, col]).astype(jnp.int32)
    cores = 2 if n_dp % 2 == 0 else 1
    chips = n_dp // cores
    tokens = inputs.shape[0]
    own = cotangent.shape[0]
    share = tokens // n_col
    slice_rows = weight.shape[0] // n_dp
    tiled = own % 16 == 0 and share % 16 == 0 and slice_rows % 128 == 0

    def along(axis, n, shift):
        return lambda a: lax.ppermute(a, axis, [(i, (i + shift) % n) for i in range(n)])

    def chip_shift(shift):
        return along("dp", n_dp, shift * cores)

    def swap_cores(a):
        return lax.ppermute(a, "dp", [(i, i ^ 1) for i in range(n_dp)])

    def in_order(pieces, places, rows):
        whole = jnp.zeros((len(pieces) * rows, pieces[0].shape[1]), pieces[0].dtype)
        for piece, at in zip(pieces, places):
            whole = lax.dynamic_update_slice_in_dim(whole, piece, at * rows, 0)
        return whole

    def dp_of(dp, c, flip):
        core = lax.rem(dp, cores)
        return lax.rem(dp - core - c * cores + n_dp, n_dp) + (1 - core if flip else core)

    by_row = [cotangent] + [along("row", n_row, s)(cotangent) for s in range(1, n_row)]
    by_chip = {(c, 0): chip_shift(c)(cotangent) for c in range(1, chips)}
    swapped = {(0, 0): swap_cores(cotangent)} if cores == 2 else {}

    flips = range(cores)
    targets = [[functools.partial(dp_of, c=0, flip=1)]] if cores == 2 else []
    targets += [[functools.partial(dp_of, c=chips - c, flip=f) for f in flips] for c in range(1, chips)]
    if tiled:
        made = forward_call(place, inputs, weight, own, n_row, slice_rows, targets)
        parts, to_send = made[:n_row], made[n_row:]
    else:
        part = jnp.dot(inputs, weight, preferred_element_type=F32)
        parts = [
            lax.dynamic_slice_in_dim(part, lax.rem(row + s, n_row) * own, own, 0).astype(
                BF16
            )
            for s in range(n_row)
        ]
        to_send = [
            jnp.concatenate(
                [
                    lax.dynamic_slice_in_dim(inputs, owner(dp) * slice_rows, slice_rows, 1)
                    for owner in owners
                ],
                0,
            )
            for owners in targets
        ]
    to_send = list(to_send)
    sums = [
        along("row", n_row, s)(after(parts[s], *swapped.values())) for s in range(1, n_row)
    ]
    near = [swap_cores(to_send.pop(0))] if cores == 2 else []
    first = [by_chip[c, 0] for c in range(1, chips)]
    far = [chip_shift(c)(after(to_send[c - 1], *first)) for c in range(1, chips)]
    for s in range(1, n_row):
        by_row[s] = after(by_row[s], parts[0], *near, *first, *swapped.values())
        if cores == 2:
            swapped[0, s] = swap_cores(by_row[s])
    if cores == 2:
        for c in range(1, chips):
            swapped[c, 0] = swap_cores(by_chip[c, 0])

    if tiled:
        gpart = input_grad_call(place, by_row, weight, n_row)
    else:
        gathered = in_order(by_row, [lax.rem(row - s + n_row, n_row) for s in range(n_row)], own)
        gpart = lax.dot_general(
            gathered, weight, (((1,), (1,)), ((), ())), preferred_element_type=F32
        ).astype(BF16)
    gparts = lax.all_to_all(gpart, "col", 0, 0, tiled=True)
    width = cotangent.shape[1]
    cuts = [(0, width)]
    relayed = [{} for _ in cuts]
    for k, (start, stop) in enumerate(cuts):
        for s in range(1, n_row):
            for c in range(1, chips):
                piece = lax.slice_in_dim(by_row[s], start, stop, axis=1)
                if k:
                    piece = after(piece, *sums)
                relayed[k][c, s] = chip_shift(c)(piece)
    outputs = parts[0].astype(F32)
    for part in sums:
        outputs = outputs + part.astype(F32)
    outputs = outputs.astype(BF16)

    held, sources = list(near), [(functools.partial(dp_of, c=0, flip=0), 0)]
    if cores == 2:
        sources.append((functools.partial(dp_of, c=0, flip=1), 0))
    for c in range(1, chips):
        for f in flips:
            piece = far[c - 1]
            held.append(swap_cores(piece) if f else piece)
            sources.append((functools.partial(dp_of, c=c, flip=f), f * tokens))
    by_chip.update({(0, s): by_row[s] for s in range(n_row)})
    origins = []
    for c in range(chips):
        for s in range(n_row):
            for flip in range(cores):

                def origin(dp, row, c=c, s=s, flip=flip):
                    return dp_of(dp, c, flip) * n_row + lax.rem(row - s + n_row, n_row)

                origins.append(origin)

    def pieces_of(k, *before):
        pieces = []
        for c in range(chips):
            for s in range(n_row):
                piece = by_chip[c, s] if (c, s) in by_chip else relayed[k][c, s]
                pieces.append(piece)
                if cores == 2:
                    if (c, s) in by_chip and (c, s) not in swapped:
                        swapped[c, s] = swap_cores(piece)
                    pieces.append(
                        swapped[c, s] if (c, s) in swapped else swap_cores(after(piece, *before))
                    )
        return pieces

    if tiled:
        features = features_call(place, inputs, held, sources, slice_rows)
        held = (weight, anchor, first_moment, second_moment)
        made = []
        for k, (start, stop) in enumerate(cuts):
            made = update_call(place, features, pieces_of(k, *made[:1]), origins, start, stop, held, made)
        new_weight, new_first, new_second = made
    else:
        mine = lax.dynamic_slice_in_dim(inputs, dp * slice_rows, slice_rows, 1)
        features = in_order(
            [mine] + [h[skip : skip + tokens] for h, (_, skip) in zip(held, sources[1:])],
            [origin(dp) for origin, _ in sources],
            tokens,
        )
        gathered = in_order(pieces_of(0), [origin(dp, row) for origin in origins], own)
        summed = lax.dot_general(
            features, gathered, (((0,), (0,)), ((), ())), preferred_element_type=F32
        )
        current = lax.dynamic_slice_in_dim(weight, dp * slice_rows, slice_rows, 0).astype(F32)
        new_weight, new_first, new_second = updated(
            summed,
            tokens * n_dp,
            current,
            anchor.astype(F32),
            first_moment,
            second_moment,
            lambda value: 1.0 / value,
        )
        new_weight = new_weight.astype(BF16)
    gparts = after(gparts, new_first)
    input_grad = sum(
        lax.slice_in_dim(gparts, k * share, (k + 1) * share).astype(F32) for k in range(n_col)
    ).astype(BF16)
    return (outputs, input_grad, new_weight, new_first, new_second)


def solution(mesh):
    in_specs = (
        P("dp", "row"),
        P("row", "col"),
        P(("dp", "row"), "col"),
        P(("row", "dp"), "col"),
        P(("row", "dp"), "col"),
        P(("row", "dp"), "col"),
    )
    out_specs = (
        P(("dp", "row"), "col"),
        P(("dp", "col"), "row"),
        P(("row", "dp"), "col"),
        P(("row", "dp"), "col"),
        P(("row", "dp"), "col"),
    )
    return jax.shard_map(
        per_device, mesh=mesh, in_specs=in_specs, out_specs=out_specs, check_vma=False
    )
```

```python
import functools
import math

import jax
import jax.numpy as jnp
from jax import lax
from jax.experimental import pallas as pl
from jax.experimental.pallas import tpu as pltpu
from jax.sharding import PartitionSpec as P

beta_one = 0.9
beta_two = 0.999
learn_rate = 0.002
anchor_pull = 0.5
epsilon = 1e-08
step_count = 100.0

BF16, F32 = jnp.bfloat16, jnp.float32
MIB = 1 << 20


def block_of(size, most):
    return max(b for b in range(128, most + 1, 128) if size % b == 0)


def struct(shape, dtype):
    return jax.ShapeDtypeStruct(shape, dtype)


def run(kernel, name, grid, in_specs, out_specs, out_shape, scratch, limit, args, bytes_moved=1):
    return pl.pallas_call(
        kernel,
        name=name,
        grid_spec=pltpu.PrefetchScalarGridSpec(
            num_scalar_prefetch=1,
            grid=grid,
            in_specs=in_specs,
            out_specs=out_specs,
            scratch_shapes=scratch,
        ),
        out_shape=out_shape,
        compiler_params=pltpu.CompilerParams(vmem_limit_bytes=limit * MIB),
        cost_estimate=pl.CostEstimate(
            flops=1, bytes_accessed=bytes_moved, transcendentals=0
        ),
    )(*args)


def in_hbm(array):
    return pltpu.with_memory_space_constraint(array, pltpu.HBM)


def in_vmem(array):
    return pltpu.with_memory_space_constraint(array, pltpu.VMEM)


def load_parts(source, target, sems, axis, part):
    loads = []
    for k in range(source.shape[axis] // part):
        at = (slice(None),) * axis + (pl.ds(k * part, part),)
        loads.append((at, pltpu.make_async_copy(source.at[at], target.at[at], sems.at[k])))
    for _, load in loads:
        load.start()
    return loads


def fixed(shape):
    return pl.BlockSpec(shape, lambda j, place: (0,) * len(shape))


def columns(rows, width):
    return pl.BlockSpec((rows, width), lambda j, place: (0, j))


def forward_kernel(n_row, own, slice_rows, targets, part, place, x_ref, w_hbm, *rest):
    outs, sent, (xs, ws, sems) = rest[:n_row], rest[n_row:-3], rest[-3:]
    dp, row = place[0], place[1]
    tokens = x_ref.shape[0]
    loads = load_parts(w_hbm, ws, sems, 1, part)
    for s in range(n_row):
        start = pl.multiple_of(lax.rem(row + s, n_row) * own, own)
        xs[s * own : (s + 1) * own, :] = x_ref[pl.ds(start, own), :]
    for out, owners in zip(sent, targets):
        for k, owner in enumerate(owners):
            start = pl.multiple_of(owner(dp) * slice_rows, slice_rows)
            out[k * tokens : (k + 1) * tokens, :] = x_ref[:, pl.ds(start, slice_rows)]
    for at, load in loads:
        load.wait()
        acc = jnp.dot(xs[...], ws[at], preferred_element_type=F32)
        for s in range(n_row):
            outs[s][at] = acc[s * own : (s + 1) * own].astype(outs[s].dtype)


def forward_call(place, inputs, weight, own, n_row, slice_rows, targets):
    tokens, depth = inputs.shape
    width = weight.shape[1]
    part = block_of(width, 512)
    sent = [(len(owners) * tokens, slice_rows) for owners in targets]
    return run(
        functools.partial(forward_kernel, n_row, own, slice_rows, targets, part),
        "forward",
        (1,),
        [fixed((tokens, depth)), pl.BlockSpec(memory_space=pltpu.HBM)],
        [fixed((own, width))] * n_row + [fixed(shape) for shape in sent],
        [struct((own, width), BF16)] * n_row + [struct(shape, BF16) for shape in sent],
        [
            pltpu.VMEM((tokens, depth), BF16),
            pltpu.VMEM((depth, width), BF16),
            pltpu.SemaphoreType.DMA((width // part,)),
        ],
        24,
        (place, inputs, in_hbm(weight)),
    )


def input_grad_kernel(n_row, own, place, *rest):
    pieces, w_ref, out, cs = rest[:n_row], rest[n_row], rest[n_row + 1], rest[n_row + 2]

    @pl.when(pl.program_id(0) == 0)
    def _():
        for s in range(n_row):
            start = pl.multiple_of(lax.rem(place[1] - s + n_row, n_row) * own, own)
            cs[pl.ds(start, own), :] = pieces[s][...]

    out[...] = lax.dot_general(
        cs[...], w_ref[...], (((1,), (1,)), ((), ())), preferred_element_type=F32
    ).astype(BF16)


def input_grad_call(place, by_row, weight, n_row):
    own, width = by_row[0].shape
    depth = weight.shape[0]
    block = block_of(depth, 256)
    return run(
        functools.partial(input_grad_kernel, n_row, own),
        "input_grad",
        (depth // block,),
        [fixed((own, width))] * n_row + [pl.BlockSpec((block, width), lambda j, place: (j, 0))],
        columns(n_row * own, block),
        struct((n_row * own, depth), BF16),
        [pltpu.VMEM((n_row * own, width), BF16)],
        6,
        (place, *by_row, in_vmem(weight)),
    )


def features_kernel(sources, tokens, place, *rest):
    n = len(sources)
    pieces, out, xs = rest[:n], rest[n], rest[n + 1]
    for piece, (origin, skip) in zip(pieces, sources):
        start = pl.multiple_of(origin(place[0]) * tokens, tokens)
        xs[pl.ds(start, tokens), :] = piece[skip : skip + tokens, :]
    out[...] = xs[...].T


def features_call(place, inputs, held, sources, slice_rows):
    tokens, n_dp = inputs.shape[0], len(sources)
    return run(
        functools.partial(features_kernel, sources, tokens),
        "features",
        (1,),
        [pl.BlockSpec((tokens, slice_rows), lambda j, place: (0, place[0]))]
        + [fixed(piece.shape) for piece in held],
        fixed((slice_rows, n_dp * tokens)),
        struct((slice_rows, n_dp * tokens), BF16),
        [pltpu.VMEM((n_dp * tokens, slice_rows), BF16)],
        6,
        (place, inputs, *held),
    )


def total_kernel(place, parts, out):
    share = out.shape[0]
    whole = parts[:share, :].astype(F32)
    for k in range(1, parts.shape[0] // share):
        whole = whole + parts[k * share : (k + 1) * share, :].astype(F32)
    out[...] = whole.astype(BF16)


def total_call(place, parts, n):
    rows, width = parts.shape
    return run(
        total_kernel,
        "total",
        (1,),
        [fixed((rows, width))],
        fixed((rows // n, width)),
        struct((rows // n, width), BF16),
        [],
        8,
        (place, parts),
    )


def inverse(value):
    guess = pl.reciprocal(value, approx=True)
    return guess * (2.0 - value * guess)


def updated(grad_sum, tokens_all, current, anchor, first, second, invert):
    grad = grad_sum * (1.0 / tokens_all) + anchor_pull * (current - anchor)
    first = beta_one * first + (1.0 - beta_one) * grad
    second = beta_two * second + (1.0 - beta_two) * grad * grad
    root = math.sqrt(1.0 / (1.0 - beta_two**step_count))
    scale = learn_rate / (1.0 - beta_one**step_count) / root
    spread = second * lax.rsqrt(second) + epsilon / root
    return current - (scale * first) * invert(spread), first, second


def update_kernel(origins, tokens_all, chunk, place, x_ref, *rest):
    n = len(origins)
    pieces = rest[:n]
    w_ref, a_ref, m_ref, v_ref = rest[n : n + 4]
    new_w, new_m, new_v, cs, acc = rest[-5:]
    own = pieces[0].shape[0]
    for piece, origin in zip(pieces, origins):
        cs[pl.ds(pl.multiple_of(origin(place[0], place[1]) * own, own), own), :] = piece[...]
    acc[...] = jnp.dot(x_ref[...], cs[...], preferred_element_type=F32)

    @pl.loop(0, acc.shape[0] // chunk, unroll=4)
    def _(i):
        at = pl.ds(pl.multiple_of(i * chunk, chunk), chunk)
        weight, first, second = updated(
            acc[at, :],
            tokens_all,
            w_ref[at, :].astype(F32),
            a_ref[at, :].astype(F32),
            m_ref[at, :],
            v_ref[at, :],
            inverse,
        )
        new_w[at, :] = weight.astype(BF16)
        new_m[at, :] = first
        new_v[at, :] = second


def update_call(place, features, pieces, origins, start, stop, held, made):
    weight, anchor, first, second = held
    rows, width = first.shape
    tokens_all = features.shape[1]
    block = block_of(math.gcd(start, stop), 512)
    own = pieces[0].shape[0]
    base = start // block

    def from_base(rows):
        return pl.BlockSpec((rows, block), lambda j, place: (0, j + base))

    tile = from_base(rows)
    return pl.pallas_call(
        functools.partial(update_kernel, origins, tokens_all, math.gcd(rows, 32)),
        name="update",
        grid_spec=pltpu.PrefetchScalarGridSpec(
            num_scalar_prefetch=1,
            grid=((stop - start) // block,),
            in_specs=[fixed((rows, tokens_all))]
            + [from_base(own) if p.shape[1] == width else columns(own, block) for p in pieces]
            + [pl.BlockSpec((rows, block), lambda j, place: (place[0], j + base))]
            + [tile] * 3
            + [pl.BlockSpec(memory_space=pltpu.HBM)] * len(made),
            out_specs=[tile] * 3,
            scratch_shapes=[pltpu.VMEM((tokens_all, block), BF16), pltpu.VMEM((rows, block), F32)],
        ),
        out_shape=[
            struct((rows, width), BF16),
            struct((rows, width), F32),
            struct((rows, width), F32),
        ],
        input_output_aliases={6 + len(pieces) + k: k for k in range(len(made))},
        compiler_params=pltpu.CompilerParams(vmem_limit_bytes=18 * MIB),
        cost_estimate=pl.CostEstimate(flops=1, bytes_accessed=1, transcendentals=0),
    )(place, features, *pieces, in_hbm(held[0]), *map(in_vmem, held[1:]), *made)


def after(value, *others):
    return lax.optimization_barrier((value, *others))[0]


def per_device(inputs, weight, cotangent, anchor, first_moment, second_moment):
    n_dp, n_row, n_col = (lax.axis_size(a) for a in ("dp", "row", "col"))
    dp, row, col = (lax.axis_index(a) for a in ("dp", "row", "col"))
    place = jnp.stack([dp, row, col]).astype(jnp.int32)
    cores = 2 if n_dp % 2 == 0 else 1
    chips = n_dp // cores
    tokens = inputs.shape[0]
    own = cotangent.shape[0]
    share = tokens // n_col
    slice_rows = weight.shape[0] // n_dp
    tiled = own % 16 == 0 and share % 16 == 0 and slice_rows % 128 == 0

    def along(axis, n, shift):
        return lambda a: lax.ppermute(a, axis, [(i, (i + shift) % n) for i in range(n)])

    def chip_shift(shift):
        return along("dp", n_dp, shift * cores)

    def swap_cores(a):
        return lax.ppermute(a, "dp", [(i, i ^ 1) for i in range(n_dp)])

    def in_order(pieces, places, rows):
        whole = jnp.zeros((len(pieces) * rows, pieces[0].shape[1]), pieces[0].dtype)
        for piece, at in zip(pieces, places):
            whole = lax.dynamic_update_slice_in_dim(whole, piece, at * rows, 0)
        return whole

    def dp_of(dp, c, flip):
        core = lax.rem(dp, cores)
        return lax.rem(dp - core - c * cores + n_dp, n_dp) + (1 - core if flip else core)

    by_row = [cotangent] + [along("row", n_row, s)(cotangent) for s in range(1, n_row)]
    by_chip = {(c, 0): chip_shift(c)(cotangent) for c in range(1, chips)}
    swapped = {(0, 0): swap_cores(cotangent)} if cores == 2 else {}

    flips = range(cores)
    targets = [[functools.partial(dp_of, c=0, flip=1)]] if cores == 2 else []
    targets += [[functools.partial(dp_of, c=chips - c, flip=f) for f in flips] for c in range(1, chips)]
    if tiled:
        made = forward_call(place, inputs, weight, own, n_row, slice_rows, targets)
        parts, to_send = made[:n_row], made[n_row:]
    else:
        part = jnp.dot(inputs, weight, preferred_element_type=F32)
        parts = [
            lax.dynamic_slice_in_dim(part, lax.rem(row + s, n_row) * own, own, 0).astype(
                BF16
            )
            for s in range(n_row)
        ]
        to_send = [
            jnp.concatenate(
                [
                    lax.dynamic_slice_in_dim(inputs, owner(dp) * slice_rows, slice_rows, 1)
                    for owner in owners
                ],
                0,
            )
            for owners in targets
        ]
    to_send = list(to_send)
    sums = [
        along("row", n_row, s)(after(parts[s], *swapped.values())) for s in range(1, n_row)
    ]
    near = [swap_cores(to_send.pop(0))] if cores == 2 else []
    first = [by_chip[c, 0] for c in range(1, chips)]
    far = [chip_shift(c)(to_send[c - 1]) for c in range(1, chips)]
    for s in range(1, n_row):
        by_row[s] = after(by_row[s], parts[0], *near, *first, *swapped.values())
        if cores == 2:
            swapped[0, s] = swap_cores(by_row[s])
    if cores == 2:
        for c in range(1, chips):
            swapped[c, 0] = swap_cores(by_chip[c, 0])

    held, sources = list(near), [(functools.partial(dp_of, c=0, flip=0), 0)]
    if cores == 2:
        sources.append((functools.partial(dp_of, c=0, flip=1), 0))
    for c in range(1, chips):
        for f in flips:
            piece = far[c - 1]
            held.append(swap_cores(after(piece, *first, *by_row[1:])) if f else piece)
            sources.append((functools.partial(dp_of, c=c, flip=f), f * tokens))
    if tiled:
        features = features_call(place, inputs, held, sources, slice_rows)
    else:
        mine = lax.dynamic_slice_in_dim(inputs, dp * slice_rows, slice_rows, 1)
        features = in_order(
            [mine] + [h[skip : skip + tokens] for h, (_, skip) in zip(held, sources[1:])],
            [origin(dp) for origin, _ in sources],
            tokens,
        )
    if tiled:
        ready = [by_row[0]] + [after(piece, features) for piece in by_row[1:]]
        gpart = input_grad_call(place, ready, weight, n_row)
    else:
        gathered = in_order(by_row, [lax.rem(row - s + n_row, n_row) for s in range(n_row)], own)
        gpart = lax.dot_general(
            gathered, weight, (((1,), (1,)), ((), ())), preferred_element_type=F32
        ).astype(BF16)
    gparts = lax.all_to_all(gpart, "col", 0, 0, tiled=True)
    width = cotangent.shape[1]
    cuts = [(0, width)]
    relayed = [{} for _ in cuts]
    for k, (start, stop) in enumerate(cuts):
        for s in range(1, n_row):
            for c in range(1, chips):
                piece = lax.slice_in_dim(by_row[s], start, stop, axis=1)
                if k:
                    piece = after(piece, *sums)
                relayed[k][c, s] = chip_shift(c)(piece)
    outputs = parts[0].astype(F32)
    for part in sums:
        outputs = outputs + part.astype(F32)
    outputs = outputs.astype(BF16)

    by_chip.update({(0, s): by_row[s] for s in range(n_row)})
    origins = []
    for c in range(chips):
        for s in range(n_row):
            for flip in range(cores):

                def origin(dp, row, c=c, s=s, flip=flip):
                    return dp_of(dp, c, flip) * n_row + lax.rem(row - s + n_row, n_row)

                origins.append(origin)

    def pieces_of(k, *before):
        pieces = []
        for c in range(chips):
            for s in range(n_row):
                piece = by_chip[c, s] if (c, s) in by_chip else relayed[k][c, s]
                pieces.append(piece)
                if cores == 2:
                    if (c, s) in by_chip and (c, s) not in swapped:
                        swapped[c, s] = swap_cores(piece)
                    pieces.append(
                        swapped[c, s] if (c, s) in swapped else swap_cores(after(piece, *before))
                    )
        return pieces

    if tiled:
        held = (weight, anchor, first_moment, second_moment)
        made = []
        for k, (start, stop) in enumerate(cuts):
            made = update_call(place, features, pieces_of(k, *made[:1]), origins, start, stop, held, made)
        new_weight, new_first, new_second = made
    else:
        gathered = in_order(pieces_of(0), [origin(dp, row) for origin in origins], own)
        summed = lax.dot_general(
            features, gathered, (((0,), (0,)), ((), ())), preferred_element_type=F32
        )
        current = lax.dynamic_slice_in_dim(weight, dp * slice_rows, slice_rows, 0).astype(F32)
        new_weight, new_first, new_second = updated(
            summed,
            tokens * n_dp,
            current,
            anchor.astype(F32),
            first_moment,
            second_moment,
            lambda value: 1.0 / value,
        )
        new_weight = new_weight.astype(BF16)
    gparts = after(gparts, new_first)
    if tiled:
        input_grad = total_call(place, gparts, n_col)
    else:
        input_grad = sum(
            lax.slice_in_dim(gparts, k * share, (k + 1) * share).astype(F32) for k in range(n_col)
        ).astype(BF16)
    return (outputs, input_grad, new_weight, new_first, new_second)


def solution(mesh):
    in_specs = (
        P("dp", "row"),
        P("row", "col"),
        P(("dp", "row"), "col"),
        P(("row", "dp"), "col"),
        P(("row", "dp"), "col"),
        P(("row", "dp"), "col"),
    )
    out_specs = (
        P(("dp", "row"), "col"),
        P(("dp", "col"), "row"),
        P(("row", "dp"), "col"),
        P(("row", "dp"), "col"),
        P(("row", "dp"), "col"),
    )
    return jax.shard_map(
        per_device, mesh=mesh, in_specs=in_specs, out_specs=out_specs, check_vma=False
    )
```

```python
import functools
import math

import jax
import jax.numpy as jnp
from jax import lax
from jax.experimental import pallas as pl
from jax.experimental.pallas import tpu as pltpu
from jax.sharding import PartitionSpec as P

beta_one = 0.9
beta_two = 0.999
learn_rate = 0.002
anchor_pull = 0.5
epsilon = 1e-08
step_count = 100.0

BF16, F32 = jnp.bfloat16, jnp.float32
MIB = 1 << 20


def block_of(size, most):
    return max(b for b in range(128, most + 1, 128) if size % b == 0)


def struct(shape, dtype):
    return jax.ShapeDtypeStruct(shape, dtype)


def run(kernel, name, grid, in_specs, out_specs, out_shape, scratch, limit, args, bytes_moved=1):
    return pl.pallas_call(
        kernel,
        name=name,
        grid_spec=pltpu.PrefetchScalarGridSpec(
            num_scalar_prefetch=1,
            grid=grid,
            in_specs=in_specs,
            out_specs=out_specs,
            scratch_shapes=scratch,
        ),
        out_shape=out_shape,
        compiler_params=pltpu.CompilerParams(vmem_limit_bytes=limit * MIB),
        cost_estimate=pl.CostEstimate(
            flops=1, bytes_accessed=bytes_moved, transcendentals=0
        ),
    )(*args)


def in_hbm(array):
    return pltpu.with_memory_space_constraint(array, pltpu.HBM)


def in_vmem(array):
    return pltpu.with_memory_space_constraint(array, pltpu.VMEM)


def load_parts(source, target, sems, axis, part):
    loads = []
    for k in range(source.shape[axis] // part):
        at = (slice(None),) * axis + (pl.ds(k * part, part),)
        loads.append((at, pltpu.make_async_copy(source.at[at], target.at[at], sems.at[k])))
    for _, load in loads:
        load.start()
    return loads


def fixed(shape):
    return pl.BlockSpec(shape, lambda j, place: (0,) * len(shape))


def columns(rows, width):
    return pl.BlockSpec((rows, width), lambda j, place: (0, j))


def forward_kernel(n_row, own, slice_rows, targets, part, place, x_ref, w_hbm, *rest):
    outs, sent, (xs, ws, sems) = rest[:n_row], rest[n_row:-3], rest[-3:]
    dp, row = place[0], place[1]
    tokens = x_ref.shape[0]
    loads = load_parts(w_hbm, ws, sems, 1, part)
    for s in range(n_row):
        start = pl.multiple_of(lax.rem(row + s, n_row) * own, own)
        xs[s * own : (s + 1) * own, :] = x_ref[pl.ds(start, own), :]
    for out, owners in zip(sent, targets):
        for k, owner in enumerate(owners):
            start = pl.multiple_of(owner(dp) * slice_rows, slice_rows)
            out[k * tokens : (k + 1) * tokens, :] = x_ref[:, pl.ds(start, slice_rows)]
    for at, load in loads:
        load.wait()
        acc = jnp.dot(xs[...], ws[at], preferred_element_type=F32)
        for s in range(n_row):
            outs[s][at] = acc[s * own : (s + 1) * own].astype(outs[s].dtype)


def forward_call(place, inputs, weight, own, n_row, slice_rows, targets):
    tokens, depth = inputs.shape
    width = weight.shape[1]
    part = block_of(width, 512)
    sent = [(len(owners) * tokens, slice_rows) for owners in targets]
    return run(
        functools.partial(forward_kernel, n_row, own, slice_rows, targets, part),
        "forward",
        (1,),
        [fixed((tokens, depth)), pl.BlockSpec(memory_space=pltpu.HBM)],
        [fixed((own, width))] * n_row + [fixed(shape) for shape in sent],
        [struct((own, width), BF16)] * n_row + [struct(shape, BF16) for shape in sent],
        [
            pltpu.VMEM((tokens, depth), BF16),
            pltpu.VMEM((depth, width), BF16),
            pltpu.SemaphoreType.DMA((width // part,)),
        ],
        24,
        (place, inputs, in_hbm(weight)),
    )


def input_grad_kernel(n_row, own, place, *rest):
    pieces, w_ref, out, cs = rest[:n_row], rest[n_row], rest[n_row + 1], rest[n_row + 2]

    @pl.when(pl.program_id(0) == 0)
    def _():
        for s in range(n_row):
            start = pl.multiple_of(lax.rem(place[1] - s + n_row, n_row) * own, own)
            cs[pl.ds(start, own), :] = pieces[s][...]

    out[...] = lax.dot_general(
        cs[...], w_ref[...], (((1,), (1,)), ((), ())), preferred_element_type=F32
    ).astype(BF16)


def input_grad_call(place, by_row, weight, n_row):
    own, width = by_row[0].shape
    depth = weight.shape[0]
    block = block_of(depth, 256)
    return run(
        functools.partial(input_grad_kernel, n_row, own),
        "input_grad",
        (depth // block,),
        [fixed((own, width))] * n_row + [pl.BlockSpec((block, width), lambda j, place: (j, 0))],
        columns(n_row * own, block),
        struct((n_row * own, depth), BF16),
        [pltpu.VMEM((n_row * own, width), BF16)],
        6,
        (place, *by_row, in_vmem(weight)),
    )


def features_kernel(sources, tokens, place, *rest):
    n = len(sources)
    pieces, out, xs = rest[:n], rest[n], rest[n + 1]
    for piece, (origin, skip) in zip(pieces, sources):
        start = pl.multiple_of(origin(place[0]) * tokens, tokens)
        xs[pl.ds(start, tokens), :] = piece[skip : skip + tokens, :]
    out[...] = xs[...].T


def features_call(place, inputs, held, sources, slice_rows):
    tokens, n_dp = inputs.shape[0], len(sources)
    return run(
        functools.partial(features_kernel, sources, tokens),
        "features",
        (1,),
        [pl.BlockSpec((tokens, slice_rows), lambda j, place: (0, place[0]))]
        + [fixed(piece.shape) for piece in held],
        fixed((slice_rows, n_dp * tokens)),
        struct((slice_rows, n_dp * tokens), BF16),
        [pltpu.VMEM((n_dp * tokens, slice_rows), BF16)],
        6,
        (place, inputs, *held),
    )


def total_kernel(place, parts, out):
    share = out.shape[0]
    whole = parts[:share, :].astype(F32)
    for k in range(1, parts.shape[0] // share):
        whole = whole + parts[k * share : (k + 1) * share, :].astype(F32)
    out[...] = whole.astype(BF16)


def total_call(place, parts, n):
    rows, width = parts.shape
    return run(
        total_kernel,
        "total",
        (1,),
        [fixed((rows, width))],
        fixed((rows // n, width)),
        struct((rows // n, width), BF16),
        [],
        8,
        (place, parts),
    )


def inverse(value):
    guess = pl.reciprocal(value, approx=True)
    return guess * (2.0 - value * guess)


def updated(grad_sum, tokens_all, current, anchor, first, second, invert):
    grad = grad_sum * (1.0 / tokens_all) + anchor_pull * (current - anchor)
    first = beta_one * first + (1.0 - beta_one) * grad
    second = beta_two * second + (1.0 - beta_two) * grad * grad
    root = math.sqrt(1.0 / (1.0 - beta_two**step_count))
    scale = learn_rate / (1.0 - beta_one**step_count) / root
    spread = second * lax.rsqrt(second) + epsilon / root
    return current - (scale * first) * invert(spread), first, second


def hold_kernel(place, *refs):
    n = (len(refs) - 1) // 2
    sems = refs[-1]
    copies = []
    for k, (source, target) in enumerate(zip(refs[:n], refs[n:-1])):
        rows = target.shape[0]
        start = pl.multiple_of(place[0] * rows, rows) if source.shape[0] > rows else 0
        copies.append(
            pltpu.make_async_copy(source.at[pl.ds(start, rows), :], target, sems.at[k])
        )
    for copy in copies:
        copy.start()
    for copy in copies:
        copy.wait()


def hold_call(place, arrays, rows):
    n = len(arrays)
    return run(
        hold_kernel,
        "hold",
        (1,),
        [pl.BlockSpec(memory_space=pltpu.HBM)] * n,
        [pl.BlockSpec(memory_space=pl.ANY)] * n,
        [pltpu.VMEM((rows, a.shape[1]), a.dtype) for a in arrays],
        [pltpu.SemaphoreType.DMA((n,))],
        4,
        (place, *map(in_hbm, arrays)),
    )


def update_kernel(origins, tokens_all, chunk, part, place, x_ref, *rest):
    n = len(origins)
    pieces = rest[:n]
    w_ref, a_ref, m_ref, v_ref, new_w, new_m, new_v, cs = rest[n:]
    own, width = pieces[0].shape

    @pl.when(pl.program_id(0) == 0)
    def _():
        for piece, origin in zip(pieces, origins):
            start = pl.multiple_of(origin(place[0], place[1]) * own, own)
            cs[pl.ds(start, own), :] = piece[...]

    for c in range(0, width, part):
        across = slice(c, c + part)
        summed = jnp.dot(x_ref[...], cs[:, across], preferred_element_type=F32)
        for r in range(0, x_ref.shape[0], chunk):
            at = (slice(r, r + chunk), across)
            weight, first, second = updated(
                summed[r : r + chunk],
                tokens_all,
                w_ref[at].astype(F32),
                a_ref[at].astype(F32),
                m_ref[at],
                v_ref[at],
                inverse,
            )
            new_w[at] = weight.astype(BF16)
            new_m[at] = first
            new_v[at] = second


def update_call(place, features, pieces, origins, held):
    rows, width = held[1].shape
    tokens_all = features.shape[1]
    block = math.gcd(rows, 128)
    tile = pl.BlockSpec((block, width), lambda j, place: (j, 0))
    return run(
        functools.partial(
            update_kernel, origins, tokens_all, math.gcd(block, 32), block_of(width, 512)
        ),
        "update",
        (rows // block,),
        [pl.BlockSpec((block, tokens_all), lambda j, place: (j, 0))]
        + [fixed(piece.shape) for piece in pieces]
        + [pl.BlockSpec((block, width), lambda j, place: (place[0] * (rows // block) + j, 0))]
        + [tile] * 3,
        [tile] * 3,
        [struct((rows, width), BF16), struct((rows, width), F32), struct((rows, width), F32)],
        [pltpu.VMEM((tokens_all, width), BF16)],
        22,
        (place, features, *pieces, *held),
    )


def after(value, *others):
    return lax.optimization_barrier((value, *others))[0]


def per_device(inputs, weight, cotangent, anchor, first_moment, second_moment):
    n_dp, n_row, n_col = (lax.axis_size(a) for a in ("dp", "row", "col"))
    dp, row, col = (lax.axis_index(a) for a in ("dp", "row", "col"))
    place = jnp.stack([dp, row, col]).astype(jnp.int32)
    cores = 2 if n_dp % 2 == 0 else 1
    chips = n_dp // cores
    tokens = inputs.shape[0]
    own = cotangent.shape[0]
    share = tokens // n_col
    slice_rows = weight.shape[0] // n_dp
    tiled = own % 16 == 0 and share % 16 == 0 and slice_rows % 128 == 0

    def along(axis, n, shift):
        return lambda a: lax.ppermute(a, axis, [(i, (i + shift) % n) for i in range(n)])

    def chip_shift(shift):
        return along("dp", n_dp, shift * cores)

    def swap_cores(a):
        return lax.ppermute(a, "dp", [(i, i ^ 1) for i in range(n_dp)])

    def in_order(pieces, places, rows):
        whole = jnp.zeros((len(pieces) * rows, pieces[0].shape[1]), pieces[0].dtype)
        for piece, at in zip(pieces, places):
            whole = lax.dynamic_update_slice_in_dim(whole, piece, at * rows, 0)
        return whole

    def dp_of(dp, c, flip):
        core = lax.rem(dp, cores)
        return lax.rem(dp - core - c * cores + n_dp, n_dp) + (1 - core if flip else core)

    by_row = [cotangent] + [along("row", n_row, s)(cotangent) for s in range(1, n_row)]
    by_chip = {(c, 0): chip_shift(c)(cotangent) for c in range(1, chips)}
    swapped = {(0, 0): swap_cores(cotangent)} if cores == 2 else {}

    flips = range(cores)
    targets = [[functools.partial(dp_of, c=0, flip=1)]] if cores == 2 else []
    targets += [[functools.partial(dp_of, c=chips - c, flip=f) for f in flips] for c in range(1, chips)]
    if tiled:
        made = forward_call(place, inputs, weight, own, n_row, slice_rows, targets)
        parts, to_send = made[:n_row], made[n_row:]
    else:
        part = jnp.dot(inputs, weight, preferred_element_type=F32)
        parts = [
            lax.dynamic_slice_in_dim(part, lax.rem(row + s, n_row) * own, own, 0).astype(
                BF16
            )
            for s in range(n_row)
        ]
        to_send = [
            jnp.concatenate(
                [
                    lax.dynamic_slice_in_dim(inputs, owner(dp) * slice_rows, slice_rows, 1)
                    for owner in owners
                ],
                0,
            )
            for owners in targets
        ]
    to_send = list(to_send)
    sums = [
        along("row", n_row, s)(after(parts[s], *swapped.values())) for s in range(1, n_row)
    ]
    near = [swap_cores(to_send.pop(0))] if cores == 2 else []
    first = [by_chip[c, 0] for c in range(1, chips)]
    kept = []
    if tiled:
        arrays = (after(first_moment, parts[0]), second_moment)
        kept = hold_call(place, arrays, slice_rows)
    far = [chip_shift(c)(after(to_send[c - 1], *kept)) for c in range(1, chips)]
    for s in range(1, n_row):
        by_row[s] = after(by_row[s], parts[0], *near, *first, *swapped.values())
        if cores == 2:
            swapped[0, s] = swap_cores(by_row[s])
    if cores == 2:
        for c in range(1, chips):
            swapped[c, 0] = swap_cores(by_chip[c, 0])

    held, sources = list(near), [(functools.partial(dp_of, c=0, flip=0), 0)]
    if cores == 2:
        sources.append((functools.partial(dp_of, c=0, flip=1), 0))
    for c in range(1, chips):
        for f in flips:
            piece = far[c - 1]
            held.append(swap_cores(after(piece, *first, *by_row[1:])) if f else piece)
            sources.append((functools.partial(dp_of, c=c, flip=f), f * tokens))
    if tiled:
        features = features_call(place, inputs, held, sources, slice_rows)
    else:
        mine = lax.dynamic_slice_in_dim(inputs, dp * slice_rows, slice_rows, 1)
        features = in_order(
            [mine] + [h[skip : skip + tokens] for h, (_, skip) in zip(held, sources[1:])],
            [origin(dp) for origin, _ in sources],
            tokens,
        )
    if tiled:
        ready = [by_row[0]] + [after(piece, features) for piece in by_row[1:]]
        gpart = input_grad_call(place, ready, weight, n_row)
    else:
        gathered = in_order(by_row, [lax.rem(row - s + n_row, n_row) for s in range(n_row)], own)
        gpart = lax.dot_general(
            gathered, weight, (((1,), (1,)), ((), ())), preferred_element_type=F32
        ).astype(BF16)
    gparts = lax.all_to_all(gpart, "col", 0, 0, tiled=True)
    for s in range(1, n_row):
        for c in range(1, chips):
            by_chip[c, s] = chip_shift(c)(by_row[s])
    outputs = parts[0].astype(F32)
    for part in sums:
        outputs = outputs + part.astype(F32)
    outputs = outputs.astype(BF16)

    by_chip.update({(0, s): by_row[s] for s in range(n_row)})
    origins = []
    for c in range(chips):
        for s in range(n_row):
            for flip in range(cores):

                def origin(dp, row, c=c, s=s, flip=flip):
                    return dp_of(dp, c, flip) * n_row + lax.rem(row - s + n_row, n_row)

                origins.append(origin)

    pieces = []
    for c in range(chips):
        for s in range(n_row):
            pieces.append(by_chip[c, s])
            if cores == 2:
                if (c, s) not in swapped:
                    swapped[c, s] = swap_cores(by_chip[c, s])
                pieces.append(swapped[c, s])

    if tiled:
        new_weight, new_first, new_second = update_call(
            place, features, pieces, origins, (in_hbm(weight), in_hbm(anchor), *kept)
        )
    else:
        gathered = in_order(pieces, [origin(dp, row) for origin in origins], own)
        summed = lax.dot_general(
            features, gathered, (((0,), (0,)), ((), ())), preferred_element_type=F32
        )
        current = lax.dynamic_slice_in_dim(weight, dp * slice_rows, slice_rows, 0).astype(F32)
        new_weight, new_first, new_second = updated(
            summed,
            tokens * n_dp,
            current,
            anchor.astype(F32),
            first_moment,
            second_moment,
            lambda value: 1.0 / value,
        )
        new_weight = new_weight.astype(BF16)
    gparts = after(gparts, new_first)
    if tiled:
        input_grad = total_call(place, gparts, n_col)
    else:
        input_grad = sum(
            lax.slice_in_dim(gparts, k * share, (k + 1) * share).astype(F32) for k in range(n_col)
        ).astype(BF16)
    return (outputs, input_grad, new_weight, new_first, new_second)


def solution(mesh):
    in_specs = (
        P("dp", "row"),
        P("row", "col"),
        P(("dp", "row"), "col"),
        P(("row", "dp"), "col"),
        P(("row", "dp"), "col"),
        P(("row", "dp"), "col"),
    )
    out_specs = (
        P(("dp", "row"), "col"),
        P(("dp", "col"), "row"),
        P(("row", "dp"), "col"),
        P(("row", "dp"), "col"),
        P(("row", "dp"), "col"),
    )
    return jax.shard_map(
        per_device, mesh=mesh, in_specs=in_specs, out_specs=out_specs, check_vma=False
    )
```

```python
import functools
import math

import jax
import jax.numpy as jnp
from jax import lax
from jax.experimental import pallas as pl
from jax.experimental.pallas import tpu as pltpu
from jax.sharding import PartitionSpec as P

beta_one = 0.9
beta_two = 0.999
learn_rate = 0.002
anchor_pull = 0.5
epsilon = 1e-08
step_count = 100.0

BF16, F32 = jnp.bfloat16, jnp.float32
MIB = 1 << 20


def block_of(size, most):
    return max(b for b in range(128, most + 1, 128) if size % b == 0)


def struct(shape, dtype):
    return jax.ShapeDtypeStruct(shape, dtype)


def run(kernel, name, grid, in_specs, out_specs, out_shape, scratch, limit, args, bytes_moved=1):
    return pl.pallas_call(
        kernel,
        name=name,
        grid_spec=pltpu.PrefetchScalarGridSpec(
            num_scalar_prefetch=1,
            grid=grid,
            in_specs=in_specs,
            out_specs=out_specs,
            scratch_shapes=scratch,
        ),
        out_shape=out_shape,
        compiler_params=pltpu.CompilerParams(vmem_limit_bytes=limit * MIB),
        cost_estimate=pl.CostEstimate(
            flops=1, bytes_accessed=bytes_moved, transcendentals=0
        ),
    )(*args)


def in_hbm(array):
    return pltpu.with_memory_space_constraint(array, pltpu.HBM)


def in_vmem(array):
    return pltpu.with_memory_space_constraint(array, pltpu.VMEM)


def load_parts(source, target, sems, axis, part):
    loads = []
    for k in range(source.shape[axis] // part):
        at = (slice(None),) * axis + (pl.ds(k * part, part),)
        loads.append((at, pltpu.make_async_copy(source.at[at], target.at[at], sems.at[k])))
    for _, load in loads:
        load.start()
    return loads


def fixed(shape):
    return pl.BlockSpec(shape, lambda j, place: (0,) * len(shape))


def columns(rows, width):
    return pl.BlockSpec((rows, width), lambda j, place: (0, j))


def forward_kernel(n_row, own, slice_rows, targets, part, place, x_ref, w_hbm, *rest):
    outs, sent, (xs, ws, sems) = rest[:n_row], rest[n_row:-3], rest[-3:]
    dp, row = place[0], place[1]
    tokens = x_ref.shape[0]
    loads = load_parts(w_hbm, ws, sems, 1, part)
    for s in range(n_row):
        start = pl.multiple_of(lax.rem(row + s, n_row) * own, own)
        xs[s * own : (s + 1) * own, :] = x_ref[pl.ds(start, own), :]
    for out, owners in zip(sent, targets):
        for k, owner in enumerate(owners):
            start = pl.multiple_of(owner(dp) * slice_rows, slice_rows)
            out[k * tokens : (k + 1) * tokens, :] = x_ref[:, pl.ds(start, slice_rows)]
    for at, load in loads:
        load.wait()
        acc = jnp.dot(xs[...], ws[at], preferred_element_type=F32)
        for s in range(n_row):
            outs[s][at] = acc[s * own : (s + 1) * own].astype(outs[s].dtype)


def forward_call(place, inputs, weight, own, n_row, slice_rows, targets):
    tokens, depth = inputs.shape
    width = weight.shape[1]
    part = block_of(width, 512)
    sent = [(len(owners) * tokens, slice_rows) for owners in targets]
    return run(
        functools.partial(forward_kernel, n_row, own, slice_rows, targets, part),
        "forward",
        (1,),
        [fixed((tokens, depth)), pl.BlockSpec(memory_space=pltpu.HBM)],
        [fixed((own, width))] * n_row + [fixed(shape) for shape in sent],
        [struct((own, width), BF16)] * n_row + [struct(shape, BF16) for shape in sent],
        [
            pltpu.VMEM((tokens, depth), BF16),
            pltpu.VMEM((depth, width), BF16),
            pltpu.SemaphoreType.DMA((width // part,)),
        ],
        24,
        (place, inputs, in_hbm(weight)),
    )


def input_grad_kernel(n_row, own, place, *rest):
    pieces, w_ref, out, cs = rest[:n_row], rest[n_row], rest[n_row + 1], rest[n_row + 2]

    @pl.when(pl.program_id(0) == 0)
    def _():
        for s in range(n_row):
            start = pl.multiple_of(lax.rem(place[1] - s + n_row, n_row) * own, own)
            cs[pl.ds(start, own), :] = pieces[s][...]

    out[...] = lax.dot_general(
        cs[...], w_ref[...], (((1,), (1,)), ((), ())), preferred_element_type=F32
    ).astype(BF16)


def input_grad_call(place, by_row, weight, n_row):
    own, width = by_row[0].shape
    depth = weight.shape[0]
    block = block_of(depth, 256)
    return run(
        functools.partial(input_grad_kernel, n_row, own),
        "input_grad",
        (depth // block,),
        [fixed((own, width))] * n_row + [pl.BlockSpec((block, width), lambda j, place: (j, 0))],
        columns(n_row * own, block),
        struct((n_row * own, depth), BF16),
        [pltpu.VMEM((n_row * own, width), BF16)],
        6,
        (place, *by_row, in_vmem(weight)),
    )


def features_kernel(sources, tokens, place, *rest):
    n = len(sources)
    pieces, out, xs = rest[:n], rest[n], rest[n + 1]
    for piece, (origin, skip) in zip(pieces, sources):
        start = pl.multiple_of(origin(place[0]) * tokens, tokens)
        xs[pl.ds(start, tokens), :] = piece[skip : skip + tokens, :]
    out[...] = xs[...].T


def features_call(place, inputs, held, sources, slice_rows):
    tokens, n_dp = inputs.shape[0], len(sources)
    return run(
        functools.partial(features_kernel, sources, tokens),
        "features",
        (1,),
        [pl.BlockSpec((tokens, slice_rows), lambda j, place: (0, place[0]))]
        + [fixed(piece.shape) for piece in held],
        fixed((slice_rows, n_dp * tokens)),
        struct((slice_rows, n_dp * tokens), BF16),
        [pltpu.VMEM((n_dp * tokens, slice_rows), BF16)],
        6,
        (place, inputs, *held),
    )


def total_kernel(place, parts, out):
    share = out.shape[0]
    whole = parts[:share, :].astype(F32)
    for k in range(1, parts.shape[0] // share):
        whole = whole + parts[k * share : (k + 1) * share, :].astype(F32)
    out[...] = whole.astype(BF16)


def total_call(place, parts, n):
    rows, width = parts.shape
    return run(
        total_kernel,
        "total",
        (1,),
        [fixed((rows, width))],
        fixed((rows // n, width)),
        struct((rows // n, width), BF16),
        [],
        8,
        (place, parts),
    )


def sum_kernel(place, *refs):
    whole = refs[0][...].astype(F32)
    for part in refs[1:-1]:
        whole = whole + part[...].astype(F32)
    refs[-1][...] = whole.astype(BF16)


def sum_call(place, parts):
    shape = parts[0].shape
    return run(
        sum_kernel,
        "outputs",
        (1,),
        [fixed(shape)] * len(parts),
        fixed(shape),
        struct(shape, BF16),
        [],
        8,
        (place, *parts),
    )


def inverse(value):
    guess = pl.reciprocal(value, approx=True)
    return guess * (2.0 - value * guess)


def updated(grad_sum, tokens_all, current, anchor, first, second, invert):
    grad = grad_sum * (1.0 / tokens_all) + anchor_pull * (current - anchor)
    first = beta_one * first + (1.0 - beta_one) * grad
    second = beta_two * second + (1.0 - beta_two) * grad * grad
    root = math.sqrt(1.0 / (1.0 - beta_two**step_count))
    scale = learn_rate / (1.0 - beta_one**step_count) / root
    spread = second * lax.rsqrt(second) + epsilon / root
    return current - (scale * first) * invert(spread), first, second


def hold_kernel(place, *refs):
    n = (len(refs) - 1) // 2
    sems = refs[-1]
    copies = []
    for k, (source, target) in enumerate(zip(refs[:n], refs[n:-1])):
        rows = target.shape[0]
        start = pl.multiple_of(place[0] * rows, rows) if source.shape[0] > rows else 0
        copies.append(
            pltpu.make_async_copy(source.at[pl.ds(start, rows), :], target, sems.at[k])
        )
    for copy in copies:
        copy.start()
    for copy in copies:
        copy.wait()


def hold_call(place, arrays, rows):
    n = len(arrays)
    return run(
        hold_kernel,
        "hold",
        (1,),
        [pl.BlockSpec(memory_space=pltpu.HBM)] * n,
        [pl.BlockSpec(memory_space=pl.ANY)] * n,
        [pltpu.VMEM((rows, a.shape[1]), a.dtype) for a in arrays],
        [pltpu.SemaphoreType.DMA((n,))],
        4,
        (place, *map(in_hbm, arrays)),
    )


def update_kernel(origins, tokens_all, chunk, part, place, x_ref, *rest):
    n = len(origins)
    pieces = rest[:n]
    w_ref, a_ref, m_ref, v_ref, new_w, new_m, new_v, cs = rest[n:]
    own, width = pieces[0].shape

    @pl.when(pl.program_id(0) == 0)
    def _():
        for piece, origin in zip(pieces, origins):
            start = pl.multiple_of(origin(place[0], place[1]) * own, own)
            cs[pl.ds(start, own), :] = piece[...]

    for c in range(0, width, part):
        across = slice(c, c + part)
        summed = jnp.dot(x_ref[...], cs[:, across], preferred_element_type=F32)
        for r in range(0, x_ref.shape[0], chunk):
            at = (slice(r, r + chunk), across)
            weight, first, second = updated(
                summed[r : r + chunk],
                tokens_all,
                w_ref[at].astype(F32),
                a_ref[at].astype(F32),
                m_ref[at],
                v_ref[at],
                inverse,
            )
            new_w[at] = weight.astype(BF16)
            new_m[at] = first
            new_v[at] = second


def update_call(place, features, pieces, origins, held):
    rows, width = held[1].shape
    tokens_all = features.shape[1]
    block = math.gcd(rows, 128)
    tile = pl.BlockSpec((block, width), lambda j, place: (j, 0))
    return run(
        functools.partial(
            update_kernel, origins, tokens_all, math.gcd(block, 32), block_of(width, 512)
        ),
        "update",
        (rows // block,),
        [pl.BlockSpec((block, tokens_all), lambda j, place: (j, 0))]
        + [fixed(piece.shape) for piece in pieces]
        + [pl.BlockSpec((block, width), lambda j, place: (place[0] * (rows // block) + j, 0))]
        + [tile] * 3,
        [tile] * 3,
        [struct((rows, width), BF16), struct((rows, width), F32), struct((rows, width), F32)],
        [pltpu.VMEM((tokens_all, width), BF16)],
        22,
        (place, features, *pieces, *held),
    )


def after(value, *others):
    return lax.optimization_barrier((value, *others))[0]


def per_device(inputs, weight, cotangent, anchor, first_moment, second_moment):
    n_dp, n_row, n_col = (lax.axis_size(a) for a in ("dp", "row", "col"))
    dp, row, col = (lax.axis_index(a) for a in ("dp", "row", "col"))
    place = jnp.stack([dp, row, col]).astype(jnp.int32)
    cores = 2 if n_dp % 2 == 0 else 1
    chips = n_dp // cores
    tokens = inputs.shape[0]
    own = cotangent.shape[0]
    share = tokens // n_col
    slice_rows = weight.shape[0] // n_dp
    tiled = own % 16 == 0 and share % 16 == 0 and slice_rows % 128 == 0

    def along(axis, n, shift):
        return lambda a: lax.ppermute(a, axis, [(i, (i + shift) % n) for i in range(n)])

    def chip_shift(shift):
        return along("dp", n_dp, shift * cores)

    def swap_cores(a):
        return lax.ppermute(a, "dp", [(i, i ^ 1) for i in range(n_dp)])

    def in_order(pieces, places, rows):
        whole = jnp.zeros((len(pieces) * rows, pieces[0].shape[1]), pieces[0].dtype)
        for piece, at in zip(pieces, places):
            whole = lax.dynamic_update_slice_in_dim(whole, piece, at * rows, 0)
        return whole

    def dp_of(dp, c, flip):
        core = lax.rem(dp, cores)
        return lax.rem(dp - core - c * cores + n_dp, n_dp) + (1 - core if flip else core)

    by_row = [cotangent] + [along("row", n_row, s)(cotangent) for s in range(1, n_row)]
    by_chip = {(c, 0): chip_shift(c)(cotangent) for c in range(1, chips)}
    swapped = {(0, 0): swap_cores(cotangent)} if cores == 2 else {}

    flips = range(cores)
    targets = [[functools.partial(dp_of, c=0, flip=1)]] if cores == 2 else []
    targets += [[functools.partial(dp_of, c=chips - c, flip=f) for f in flips] for c in range(1, chips)]
    if tiled:
        made = forward_call(place, inputs, weight, own, n_row, slice_rows, targets)
        parts, to_send = made[:n_row], made[n_row:]
    else:
        part = jnp.dot(inputs, weight, preferred_element_type=F32)
        parts = [
            lax.dynamic_slice_in_dim(part, lax.rem(row + s, n_row) * own, own, 0).astype(
                BF16
            )
            for s in range(n_row)
        ]
        to_send = [
            jnp.concatenate(
                [
                    lax.dynamic_slice_in_dim(inputs, owner(dp) * slice_rows, slice_rows, 1)
                    for owner in owners
                ],
                0,
            )
            for owners in targets
        ]
    to_send = list(to_send)
    sums = [
        along("row", n_row, s)(after(parts[s], *swapped.values())) for s in range(1, n_row)
    ]
    near = [swap_cores(to_send.pop(0))] if cores == 2 else []
    first = [by_chip[c, 0] for c in range(1, chips)]
    kept = []
    if tiled:
        arrays = (after(first_moment, parts[0]), second_moment)
        kept = hold_call(place, arrays, slice_rows)
    far = [chip_shift(c)(after(to_send[c - 1], *kept)) for c in range(1, chips)]
    for s in range(1, n_row):
        by_row[s] = after(by_row[s], parts[0], *near, *first, *swapped.values())
        if cores == 2:
            swapped[0, s] = swap_cores(by_row[s])
    if cores == 2:
        for c in range(1, chips):
            swapped[c, 0] = swap_cores(by_chip[c, 0])

    held, sources = list(near), [(functools.partial(dp_of, c=0, flip=0), 0)]
    if cores == 2:
        sources.append((functools.partial(dp_of, c=0, flip=1), 0))
    for c in range(1, chips):
        for f in flips:
            piece = far[c - 1]
            held.append(swap_cores(after(piece, *first, *by_row[1:])) if f else piece)
            sources.append((functools.partial(dp_of, c=c, flip=f), f * tokens))
    if tiled:
        features = features_call(place, inputs, held, sources, slice_rows)
    else:
        mine = lax.dynamic_slice_in_dim(inputs, dp * slice_rows, slice_rows, 1)
        features = in_order(
            [mine] + [h[skip : skip + tokens] for h, (_, skip) in zip(held, sources[1:])],
            [origin(dp) for origin, _ in sources],
            tokens,
        )
    if tiled:
        ready = [by_row[0]] + [after(piece, features) for piece in by_row[1:]]
        gpart = input_grad_call(place, ready, weight, n_row)
    else:
        gathered = in_order(by_row, [lax.rem(row - s + n_row, n_row) for s in range(n_row)], own)
        gpart = lax.dot_general(
            gathered, weight, (((1,), (1,)), ((), ())), preferred_element_type=F32
        ).astype(BF16)
    gparts = lax.all_to_all(gpart, "col", 0, 0, tiled=True)
    for s in range(1, n_row):
        for c in range(1, chips):
            by_chip[c, s] = chip_shift(c)(by_row[s])
    if tiled:
        outputs = sum_call(place, [parts[0], *sums])
    else:
        outputs = sum(part.astype(F32) for part in [parts[0], *sums]).astype(BF16)

    by_chip.update({(0, s): by_row[s] for s in range(n_row)})
    origins = []
    for c in range(chips):
        for s in range(n_row):
            for flip in range(cores):

                def origin(dp, row, c=c, s=s, flip=flip):
                    return dp_of(dp, c, flip) * n_row + lax.rem(row - s + n_row, n_row)

                origins.append(origin)

    pieces = []
    for c in range(chips):
        for s in range(n_row):
            pieces.append(by_chip[c, s])
            if cores == 2:
                if (c, s) not in swapped:
                    swapped[c, s] = swap_cores(by_chip[c, s])
                pieces.append(swapped[c, s])

    if tiled:
        new_weight, new_first, new_second = update_call(
            place, features, pieces, origins, (in_hbm(weight), in_hbm(anchor), *kept)
        )
    else:
        gathered = in_order(pieces, [origin(dp, row) for origin in origins], own)
        summed = lax.dot_general(
            features, gathered, (((0,), (0,)), ((), ())), preferred_element_type=F32
        )
        current = lax.dynamic_slice_in_dim(weight, dp * slice_rows, slice_rows, 0).astype(F32)
        new_weight, new_first, new_second = updated(
            summed,
            tokens * n_dp,
            current,
            anchor.astype(F32),
            first_moment,
            second_moment,
            lambda value: 1.0 / value,
        )
        new_weight = new_weight.astype(BF16)
    gparts = after(gparts, new_first)
    if tiled:
        input_grad = total_call(place, gparts, n_col)
    else:
        input_grad = sum(
            lax.slice_in_dim(gparts, k * share, (k + 1) * share).astype(F32) for k in range(n_col)
        ).astype(BF16)
    return (outputs, input_grad, new_weight, new_first, new_second)


def solution(mesh):
    in_specs = (
        P("dp", "row"),
        P("row", "col"),
        P(("dp", "row"), "col"),
        P(("row", "dp"), "col"),
        P(("row", "dp"), "col"),
        P(("row", "dp"), "col"),
    )
    out_specs = (
        P(("dp", "row"), "col"),
        P(("dp", "col"), "row"),
        P(("row", "dp"), "col"),
        P(("row", "dp"), "col"),
        P(("row", "dp"), "col"),
    )
    return jax.shard_map(
        per_device, mesh=mesh, in_specs=in_specs, out_specs=out_specs, check_vma=False
    )
```

```python
import functools
import math

import jax
import jax.numpy as jnp
from jax import lax
from jax.experimental import pallas as pl
from jax.experimental.pallas import tpu as pltpu
from jax.sharding import PartitionSpec as P

beta_one = 0.9
beta_two = 0.999
learn_rate = 0.002
anchor_pull = 0.5
epsilon = 1e-08
step_count = 100.0

BF16, F32 = jnp.bfloat16, jnp.float32
MIB = 1 << 20


def block_of(size, most):
    return max(b for b in range(128, most + 1, 128) if size % b == 0)


def struct(shape, dtype):
    return jax.ShapeDtypeStruct(shape, dtype)


def run(kernel, name, grid, in_specs, out_specs, out_shape, scratch, limit, args, bytes_moved=1):
    return pl.pallas_call(
        kernel,
        name=name,
        grid_spec=pltpu.PrefetchScalarGridSpec(
            num_scalar_prefetch=1,
            grid=grid,
            in_specs=in_specs,
            out_specs=out_specs,
            scratch_shapes=scratch,
        ),
        out_shape=out_shape,
        compiler_params=pltpu.CompilerParams(vmem_limit_bytes=limit * MIB),
        cost_estimate=pl.CostEstimate(
            flops=1, bytes_accessed=bytes_moved, transcendentals=0
        ),
    )(*args)


def in_hbm(array):
    return pltpu.with_memory_space_constraint(array, pltpu.HBM)


def in_vmem(array):
    return pltpu.with_memory_space_constraint(array, pltpu.VMEM)


def load_parts(source, target, sems, axis, part):
    loads = []
    for k in range(source.shape[axis] // part):
        at = (slice(None),) * axis + (pl.ds(k * part, part),)
        loads.append((at, pltpu.make_async_copy(source.at[at], target.at[at], sems.at[k])))
    for _, load in loads:
        load.start()
    return loads


def fixed(shape):
    return pl.BlockSpec(shape, lambda j, place: (0,) * len(shape))


def columns(rows, width):
    return pl.BlockSpec((rows, width), lambda j, place: (0, j))


def forward_kernel(n_row, own, slice_rows, targets, part, place, x_ref, w_hbm, *rest):
    outs, sent, (xs, ws, sems) = rest[:n_row], rest[n_row:-3], rest[-3:]
    dp, row = place[0], place[1]
    tokens = x_ref.shape[0]
    loads = load_parts(w_hbm, ws, sems, 1, part)
    for s in range(n_row):
        start = pl.multiple_of(lax.rem(row + s, n_row) * own, own)
        xs[s * own : (s + 1) * own, :] = x_ref[pl.ds(start, own), :]
    for out, owners in zip(sent, targets):
        for k, owner in enumerate(owners):
            start = pl.multiple_of(owner(dp) * slice_rows, slice_rows)
            out[k * tokens : (k + 1) * tokens, :] = x_ref[:, pl.ds(start, slice_rows)]
    for at, load in loads:
        load.wait()
        acc = jnp.dot(xs[...], ws[at], preferred_element_type=F32)
        for s in range(n_row):
            outs[s][at] = acc[s * own : (s + 1) * own].astype(outs[s].dtype)


def forward_call(place, inputs, weight, own, n_row, slice_rows, targets):
    tokens, depth = inputs.shape
    width = weight.shape[1]
    part = block_of(width, 512)
    sent = [(len(owners) * tokens, slice_rows) for owners in targets]
    return run(
        functools.partial(forward_kernel, n_row, own, slice_rows, targets, part),
        "forward",
        (1,),
        [fixed((tokens, depth)), pl.BlockSpec(memory_space=pltpu.HBM)],
        [fixed((own, width))] * n_row + [fixed(shape) for shape in sent],
        [struct((own, width), BF16)] * n_row + [struct(shape, BF16) for shape in sent],
        [
            pltpu.VMEM((tokens, depth), BF16),
            pltpu.VMEM((depth, width), BF16),
            pltpu.SemaphoreType.DMA((width // part,)),
        ],
        24,
        (place, inputs, in_hbm(weight)),
    )


def input_grad_kernel(n_row, own, place, *rest):
    pieces, w_ref, out, cs = rest[:n_row], rest[n_row], rest[n_row + 1], rest[n_row + 2]

    @pl.when(pl.program_id(0) == 0)
    def _():
        for s in range(n_row):
            start = pl.multiple_of(lax.rem(place[1] - s + n_row, n_row) * own, own)
            cs[pl.ds(start, own), :] = pieces[s][...]

    out[...] = lax.dot_general(
        cs[...], w_ref[...], (((1,), (1,)), ((), ())), preferred_element_type=F32
    ).astype(BF16)


def input_grad_call(place, by_row, weight, n_row):
    own, width = by_row[0].shape
    depth = weight.shape[0]
    block = block_of(depth, 256)
    return run(
        functools.partial(input_grad_kernel, n_row, own),
        "input_grad",
        (depth // block,),
        [fixed((own, width))] * n_row + [pl.BlockSpec((block, width), lambda j, place: (j, 0))],
        columns(n_row * own, block),
        struct((n_row * own, depth), BF16),
        [pltpu.VMEM((n_row * own, width), BF16)],
        6,
        (place, *by_row, in_vmem(weight)),
    )


def features_kernel(sources, tokens, place, *rest):
    n = len(sources)
    pieces, out, xs = rest[:n], rest[n], rest[n + 1]
    for piece, (origin, skip) in zip(pieces, sources):
        start = pl.multiple_of(origin(place[0]) * tokens, tokens)
        xs[pl.ds(start, tokens), :] = piece[skip : skip + tokens, :]
    out[...] = xs[...].T


def features_call(place, inputs, held, sources, slice_rows):
    tokens, n_dp = inputs.shape[0], len(sources)
    return run(
        functools.partial(features_kernel, sources, tokens),
        "features",
        (1,),
        [pl.BlockSpec((tokens, slice_rows), lambda j, place: (0, place[0]))]
        + [fixed(piece.shape) for piece in held],
        fixed((slice_rows, n_dp * tokens)),
        struct((slice_rows, n_dp * tokens), BF16),
        [pltpu.VMEM((n_dp * tokens, slice_rows), BF16)],
        6,
        (place, inputs, *held),
    )


def total_kernel(place, parts, out):
    share = out.shape[0]
    whole = parts[:share, :].astype(F32)
    for k in range(1, parts.shape[0] // share):
        whole = whole + parts[k * share : (k + 1) * share, :].astype(F32)
    out[...] = whole.astype(BF16)


def total_call(place, parts, n):
    rows, width = parts.shape
    return run(
        total_kernel,
        "total",
        (1,),
        [fixed((rows, width))],
        fixed((rows // n, width)),
        struct((rows // n, width), BF16),
        [],
        8,
        (place, parts),
    )


def inverse(value):
    guess = pl.reciprocal(value, approx=True)
    return guess * (2.0 - value * guess)


def updated(grad_sum, tokens_all, current, anchor, first, second, invert):
    grad = grad_sum * (1.0 / tokens_all) + anchor_pull * (current - anchor)
    first = beta_one * first + (1.0 - beta_one) * grad
    second = beta_two * second + (1.0 - beta_two) * grad * grad
    root = math.sqrt(1.0 / (1.0 - beta_two**step_count))
    scale = learn_rate / (1.0 - beta_one**step_count) / root
    spread = second * lax.rsqrt(second) + epsilon / root
    return current - (scale * first) * invert(spread), first, second


def update_kernel(origins, tokens_all, chunk, part, place, x_ref, *rest):
    n = len(origins)
    pieces = rest[:n]
    w_ref, a_ref, m_ref, v_ref, new_w, new_m, new_v, cs = rest[n:]
    own, width = pieces[0].shape

    @pl.when(pl.program_id(0) == 0)
    def _():
        for piece, origin in zip(pieces, origins):
            start = pl.multiple_of(origin(place[0], place[1]) * own, own)
            cs[pl.ds(start, own), :] = piece[...]

    for c in range(0, width, part):
        across = slice(c, c + part)
        summed = jnp.dot(x_ref[...], cs[:, across], preferred_element_type=F32)
        for r in range(0, x_ref.shape[0], chunk):
            at = (slice(r, r + chunk), across)
            weight, first, second = updated(
                summed[r : r + chunk],
                tokens_all,
                w_ref[at].astype(F32),
                a_ref[at].astype(F32),
                m_ref[at],
                v_ref[at],
                inverse,
            )
            new_w[at] = weight.astype(BF16)
            new_m[at] = first
            new_v[at] = second


def update_call(place, features, pieces, origins, held):
    rows, width = held[1].shape
    tokens_all = features.shape[1]
    block = math.gcd(rows, 128)
    tile = pl.BlockSpec((block, width), lambda j, place: (j, 0))
    return run(
        functools.partial(
            update_kernel, origins, tokens_all, math.gcd(block, 32), block_of(width, 512)
        ),
        "update",
        (rows // block,),
        [pl.BlockSpec((block, tokens_all), lambda j, place: (j, 0))]
        + [fixed(piece.shape) for piece in pieces]
        + [pl.BlockSpec((block, width), lambda j, place: (place[0] * (rows // block) + j, 0))]
        + [tile] * 3,
        [tile] * 3,
        [struct((rows, width), BF16), struct((rows, width), F32), struct((rows, width), F32)],
        [pltpu.VMEM((tokens_all, width), BF16)],
        38,
        (place, features, *pieces, *held),
    )


def after(value, *others):
    return lax.optimization_barrier((value, *others))[0]


def per_device(inputs, weight, cotangent, anchor, first_moment, second_moment):
    n_dp, n_row, n_col = (lax.axis_size(a) for a in ("dp", "row", "col"))
    dp, row, col = (lax.axis_index(a) for a in ("dp", "row", "col"))
    place = jnp.stack([dp, row, col]).astype(jnp.int32)
    cores = 2 if n_dp % 2 == 0 else 1
    chips = n_dp // cores
    tokens = inputs.shape[0]
    own = cotangent.shape[0]
    share = tokens // n_col
    slice_rows = weight.shape[0] // n_dp
    tiled = own % 16 == 0 and share % 16 == 0 and slice_rows % 128 == 0

    def along(axis, n, shift):
        return lambda a: lax.ppermute(a, axis, [(i, (i + shift) % n) for i in range(n)])

    def chip_shift(shift):
        return along("dp", n_dp, shift * cores)

    def swap_cores(a):
        return lax.ppermute(a, "dp", [(i, i ^ 1) for i in range(n_dp)])

    def in_order(pieces, places, rows):
        whole = jnp.zeros((len(pieces) * rows, pieces[0].shape[1]), pieces[0].dtype)
        for piece, at in zip(pieces, places):
            whole = lax.dynamic_update_slice_in_dim(whole, piece, at * rows, 0)
        return whole

    def dp_of(dp, c, flip):
        core = lax.rem(dp, cores)
        return lax.rem(dp - core - c * cores + n_dp, n_dp) + (1 - core if flip else core)

    by_row = [cotangent] + [along("row", n_row, s)(cotangent) for s in range(1, n_row)]
    by_chip = {(c, 0): chip_shift(c)(cotangent) for c in range(1, chips)}
    swapped = {(0, 0): swap_cores(cotangent)} if cores == 2 else {}

    flips = range(cores)
    targets = [[functools.partial(dp_of, c=0, flip=1)]] if cores == 2 else []
    targets += [[functools.partial(dp_of, c=chips - c, flip=f) for f in flips] for c in range(1, chips)]
    if tiled:
        made = forward_call(place, inputs, weight, own, n_row, slice_rows, targets)
        parts, to_send = made[:n_row], made[n_row:]
    else:
        part = jnp.dot(inputs, weight, preferred_element_type=F32)
        parts = [
            lax.dynamic_slice_in_dim(part, lax.rem(row + s, n_row) * own, own, 0).astype(
                BF16
            )
            for s in range(n_row)
        ]
        to_send = [
            jnp.concatenate(
                [
                    lax.dynamic_slice_in_dim(inputs, owner(dp) * slice_rows, slice_rows, 1)
                    for owner in owners
                ],
                0,
            )
            for owners in targets
        ]
    to_send = list(to_send)
    sums = [
        along("row", n_row, s)(after(parts[s], *swapped.values())) for s in range(1, n_row)
    ]
    near = [swap_cores(to_send.pop(0))] if cores == 2 else []
    first = [by_chip[c, 0] for c in range(1, chips)]
    far = [chip_shift(c)(to_send[c - 1]) for c in range(1, chips)]
    for s in range(1, n_row):
        by_row[s] = after(by_row[s], parts[0], *near, *first, *swapped.values())
        if cores == 2:
            swapped[0, s] = swap_cores(by_row[s])
    if cores == 2:
        for c in range(1, chips):
            swapped[c, 0] = swap_cores(by_chip[c, 0])

    held, sources = list(near), [(functools.partial(dp_of, c=0, flip=0), 0)]
    if cores == 2:
        sources.append((functools.partial(dp_of, c=0, flip=1), 0))
    for c in range(1, chips):
        for f in flips:
            piece = far[c - 1]
            held.append(swap_cores(after(piece, *first, *by_row[1:])) if f else piece)
            sources.append((functools.partial(dp_of, c=c, flip=f), f * tokens))
    if tiled:
        features = features_call(place, inputs, held, sources, slice_rows)
    else:
        mine = lax.dynamic_slice_in_dim(inputs, dp * slice_rows, slice_rows, 1)
        features = in_order(
            [mine] + [h[skip : skip + tokens] for h, (_, skip) in zip(held, sources[1:])],
            [origin(dp) for origin, _ in sources],
            tokens,
        )
    if tiled:
        ready = [by_row[0]] + [after(piece, features) for piece in by_row[1:]]
        gpart = input_grad_call(place, ready, weight, n_row)
    else:
        gathered = in_order(by_row, [lax.rem(row - s + n_row, n_row) for s in range(n_row)], own)
        gpart = lax.dot_general(
            gathered, weight, (((1,), (1,)), ((), ())), preferred_element_type=F32
        ).astype(BF16)
    gparts = lax.all_to_all(gpart, "col", 0, 0, tiled=True)
    for s in range(1, n_row):
        for c in range(1, chips):
            by_chip[c, s] = chip_shift(c)(by_row[s])
    outputs = parts[0].astype(F32)
    for part in sums:
        outputs = outputs + part.astype(F32)
    outputs = outputs.astype(BF16)

    by_chip.update({(0, s): by_row[s] for s in range(n_row)})
    origins = []
    for c in range(chips):
        for s in range(n_row):
            for flip in range(cores):

                def origin(dp, row, c=c, s=s, flip=flip):
                    return dp_of(dp, c, flip) * n_row + lax.rem(row - s + n_row, n_row)

                origins.append(origin)

    pieces = []
    for c in range(chips):
        for s in range(n_row):
            pieces.append(by_chip[c, s])
            if cores == 2:
                if (c, s) not in swapped:
                    swapped[c, s] = swap_cores(by_chip[c, s])
                pieces.append(swapped[c, s])

    if tiled:
        streamed = map(in_hbm, (weight, anchor, first_moment, second_moment))
        new_weight, new_first, new_second = update_call(
            place, features, pieces, origins, tuple(streamed)
        )
    else:
        gathered = in_order(pieces, [origin(dp, row) for origin in origins], own)
        summed = lax.dot_general(
            features, gathered, (((0,), (0,)), ((), ())), preferred_element_type=F32
        )
        current = lax.dynamic_slice_in_dim(weight, dp * slice_rows, slice_rows, 0).astype(F32)
        new_weight, new_first, new_second = updated(
            summed,
            tokens * n_dp,
            current,
            anchor.astype(F32),
            first_moment,
            second_moment,
            lambda value: 1.0 / value,
        )
        new_weight = new_weight.astype(BF16)
    gparts = after(gparts, new_first)
    if tiled:
        input_grad = total_call(place, gparts, n_col)
    else:
        input_grad = sum(
            lax.slice_in_dim(gparts, k * share, (k + 1) * share).astype(F32) for k in range(n_col)
        ).astype(BF16)
    return (outputs, input_grad, new_weight, new_first, new_second)


def solution(mesh):
    in_specs = (
        P("dp", "row"),
        P("row", "col"),
        P(("dp", "row"), "col"),
        P(("row", "dp"), "col"),
        P(("row", "dp"), "col"),
        P(("row", "dp"), "col"),
    )
    out_specs = (
        P(("dp", "row"), "col"),
        P(("dp", "col"), "row"),
        P(("row", "dp"), "col"),
        P(("row", "dp"), "col"),
        P(("row", "dp"), "col"),
    )
    return jax.shard_map(
        per_device, mesh=mesh, in_specs=in_specs, out_specs=out_specs, check_vma=False
    )
```

```python
import functools
import math

import jax
import jax.numpy as jnp
from jax import lax
from jax.experimental import pallas as pl
from jax.experimental.pallas import tpu as pltpu
from jax.sharding import PartitionSpec as P

beta_one = 0.9
beta_two = 0.999
learn_rate = 0.002
anchor_pull = 0.5
epsilon = 1e-08
step_count = 100.0

BF16, F32 = jnp.bfloat16, jnp.float32
MIB = 1 << 20


def block_of(size, most):
    return max(b for b in range(128, most + 1, 128) if size % b == 0)


def struct(shape, dtype):
    return jax.ShapeDtypeStruct(shape, dtype)


def run(kernel, name, grid, in_specs, out_specs, out_shape, scratch, limit, args, bytes_moved=1):
    return pl.pallas_call(
        kernel,
        name=name,
        grid_spec=pltpu.PrefetchScalarGridSpec(
            num_scalar_prefetch=1,
            grid=grid,
            in_specs=in_specs,
            out_specs=out_specs,
            scratch_shapes=scratch,
        ),
        out_shape=out_shape,
        compiler_params=pltpu.CompilerParams(vmem_limit_bytes=limit * MIB),
        cost_estimate=pl.CostEstimate(
            flops=1, bytes_accessed=bytes_moved, transcendentals=0
        ),
    )(*args)


def in_hbm(array):
    return pltpu.with_memory_space_constraint(array, pltpu.HBM)


def in_vmem(array):
    return pltpu.with_memory_space_constraint(array, pltpu.VMEM)


def load_parts(source, target, sems, axis, part):
    loads = []
    for k in range(source.shape[axis] // part):
        at = (slice(None),) * axis + (pl.ds(k * part, part),)
        loads.append((at, pltpu.make_async_copy(source.at[at], target.at[at], sems.at[k])))
    for _, load in loads:
        load.start()
    return loads


def fixed(shape):
    return pl.BlockSpec(shape, lambda j, place: (0,) * len(shape))


def columns(rows, width):
    return pl.BlockSpec((rows, width), lambda j, place: (0, j))


def forward_kernel(n_row, own, slice_rows, targets, part, place, x_ref, w_hbm, *rest):
    outs, sent, (xs, ws, sems) = rest[:n_row], rest[n_row:-3], rest[-3:]
    dp, row = place[0], place[1]
    tokens = x_ref.shape[0]
    loads = load_parts(w_hbm, ws, sems, 1, part)
    for s in range(n_row):
        start = pl.multiple_of(lax.rem(row + s, n_row) * own, own)
        xs[s * own : (s + 1) * own, :] = x_ref[pl.ds(start, own), :]
    for out, owners in zip(sent, targets):
        for k, owner in enumerate(owners):
            start = pl.multiple_of(owner(dp) * slice_rows, slice_rows)
            out[k * tokens : (k + 1) * tokens, :] = x_ref[:, pl.ds(start, slice_rows)]
    for at, load in loads:
        load.wait()
        acc = jnp.dot(xs[...], ws[at], preferred_element_type=F32)
        for s in range(n_row):
            outs[s][at] = acc[s * own : (s + 1) * own].astype(outs[s].dtype)


def forward_call(place, inputs, weight, own, n_row, slice_rows, targets):
    tokens, depth = inputs.shape
    width = weight.shape[1]
    part = block_of(width, 512)
    sent = [(len(owners) * tokens, slice_rows) for owners in targets]
    return run(
        functools.partial(forward_kernel, n_row, own, slice_rows, targets, part),
        "forward",
        (1,),
        [fixed((tokens, depth)), pl.BlockSpec(memory_space=pltpu.HBM)],
        [fixed((own, width))] * n_row + [fixed(shape) for shape in sent],
        [struct((own, width), BF16)] * n_row + [struct(shape, BF16) for shape in sent],
        [
            pltpu.VMEM((tokens, depth), BF16),
            pltpu.VMEM((depth, width), BF16),
            pltpu.SemaphoreType.DMA((width // part,)),
        ],
        24,
        (place, inputs, in_hbm(weight)),
    )


def input_grad_kernel(n_row, own, place, *rest):
    pieces, w_ref, out, cs = rest[:n_row], rest[n_row], rest[n_row + 1], rest[n_row + 2]

    @pl.when(pl.program_id(0) == 0)
    def _():
        for s in range(n_row):
            start = pl.multiple_of(lax.rem(place[1] - s + n_row, n_row) * own, own)
            cs[pl.ds(start, own), :] = pieces[s][...]

    out[...] = lax.dot_general(
        cs[...], w_ref[...], (((1,), (1,)), ((), ())), preferred_element_type=F32
    ).astype(BF16)


def input_grad_call(place, by_row, weight, n_row):
    own, width = by_row[0].shape
    depth = weight.shape[0]
    block = block_of(depth, 256)
    return run(
        functools.partial(input_grad_kernel, n_row, own),
        "input_grad",
        (depth // block,),
        [fixed((own, width))] * n_row + [pl.BlockSpec((block, width), lambda j, place: (j, 0))],
        columns(n_row * own, block),
        struct((n_row * own, depth), BF16),
        [pltpu.VMEM((n_row * own, width), BF16)],
        6,
        (place, *by_row, in_vmem(weight)),
    )


def features_kernel(sources, tokens, place, *rest):
    n = len(sources)
    pieces, out, xs = rest[:n], rest[n], rest[n + 1]
    for piece, (origin, skip) in zip(pieces, sources):
        start = pl.multiple_of(origin(place[0]) * tokens, tokens)
        xs[pl.ds(start, tokens), :] = piece[skip : skip + tokens, :]
    out[...] = xs[...].T


def features_call(place, inputs, held, sources, slice_rows):
    tokens, n_dp = inputs.shape[0], len(sources)
    return run(
        functools.partial(features_kernel, sources, tokens),
        "features",
        (1,),
        [pl.BlockSpec((tokens, slice_rows), lambda j, place: (0, place[0]))]
        + [fixed(piece.shape) for piece in held],
        fixed((slice_rows, n_dp * tokens)),
        struct((slice_rows, n_dp * tokens), BF16),
        [pltpu.VMEM((n_dp * tokens, slice_rows), BF16)],
        6,
        (place, inputs, *held),
    )


def total(parts):
    whole = parts[0].astype(F32)
    for part in parts[1:]:
        whole = whole + part.astype(F32)
    return whole.astype(BF16)


def totals_kernel(n, place, parts, *rest):
    sums, (grad, out) = rest[:-2], rest[-2:]
    share = grad.shape[0]
    grad[...] = total([parts[k * share : (k + 1) * share, :] for k in range(n)])
    out[...] = total([part[...] for part in sums])


def totals_call(place, parts, sums, n):
    rows, width = parts.shape
    return run(
        functools.partial(totals_kernel, n),
        "totals",
        (1,),
        [fixed(parts.shape)] + [fixed(part.shape) for part in sums],
        [fixed((rows // n, width)), fixed(sums[0].shape)],
        [struct((rows // n, width), BF16), struct(sums[0].shape, BF16)],
        [],
        10,
        (place, parts, *sums),
    )


def inverse(value):
    guess = pl.reciprocal(value, approx=True)
    return guess * (2.0 - value * guess)


def updated(grad_sum, tokens_all, current, anchor, first, second, invert):
    grad = grad_sum * (1.0 / tokens_all) + anchor_pull * (current - anchor)
    first = beta_one * first + (1.0 - beta_one) * grad
    second = beta_two * second + (1.0 - beta_two) * grad * grad
    root = math.sqrt(1.0 / (1.0 - beta_two**step_count))
    scale = learn_rate / (1.0 - beta_one**step_count) / root
    spread = second * lax.rsqrt(second) + epsilon / root
    return current - (scale * first) * invert(spread), first, second


def update_kernel(origins, tokens_all, chunk, part, place, x_ref, *rest):
    n = len(origins)
    pieces = rest[:n]
    w_ref, a_ref, m_ref, v_ref, new_w, new_m, new_v, cs = rest[n:]
    own, width = pieces[0].shape

    @pl.when(pl.program_id(0) == 0)
    def _():
        for piece, origin in zip(pieces, origins):
            start = pl.multiple_of(origin(place[0], place[1]) * own, own)
            cs[pl.ds(start, own), :] = piece[...]

    for c in range(0, width, part):
        across = slice(c, c + part)
        summed = jnp.dot(x_ref[...], cs[:, across], preferred_element_type=F32)
        for r in range(0, x_ref.shape[0], chunk):
            at = (slice(r, r + chunk), across)
            weight, first, second = updated(
                summed[r : r + chunk],
                tokens_all,
                w_ref[at].astype(F32),
                a_ref[at].astype(F32),
                m_ref[at],
                v_ref[at],
                inverse,
            )
            new_w[at] = weight.astype(BF16)
            new_m[at] = first
            new_v[at] = second


def update_call(place, features, pieces, origins, held):
    rows, width = held[1].shape
    tokens_all = features.shape[1]
    block = math.gcd(rows, 128)
    tile = pl.BlockSpec((block, width), lambda j, place: (j, 0))
    return run(
        functools.partial(
            update_kernel, origins, tokens_all, math.gcd(block, 32), block_of(width, 512)
        ),
        "update",
        (rows // block,),
        [pl.BlockSpec((block, tokens_all), lambda j, place: (j, 0))]
        + [fixed(piece.shape) for piece in pieces]
        + [pl.BlockSpec((block, width), lambda j, place: (place[0] * (rows // block) + j, 0))]
        + [tile] * 3,
        [tile] * 3,
        [struct((rows, width), BF16), struct((rows, width), F32), struct((rows, width), F32)],
        [pltpu.VMEM((tokens_all, width), BF16)],
        38,
        (place, features, *pieces, *held),
    )


def after(value, *others):
    return lax.optimization_barrier((value, *others))[0]


def per_device(inputs, weight, cotangent, anchor, first_moment, second_moment):
    n_dp, n_row, n_col = (lax.axis_size(a) for a in ("dp", "row", "col"))
    dp, row, col = (lax.axis_index(a) for a in ("dp", "row", "col"))
    place = jnp.stack([dp, row, col]).astype(jnp.int32)
    cores = 2 if n_dp % 2 == 0 else 1
    chips = n_dp // cores
    tokens = inputs.shape[0]
    own = cotangent.shape[0]
    share = tokens // n_col
    slice_rows = weight.shape[0] // n_dp
    tiled = own % 16 == 0 and share % 16 == 0 and slice_rows % 128 == 0

    def along(axis, n, shift):
        return lambda a: lax.ppermute(a, axis, [(i, (i + shift) % n) for i in range(n)])

    def chip_shift(shift):
        return along("dp", n_dp, shift * cores)

    def swap_cores(a):
        return lax.ppermute(a, "dp", [(i, i ^ 1) for i in range(n_dp)])

    def in_order(pieces, places, rows):
        whole = jnp.zeros((len(pieces) * rows, pieces[0].shape[1]), pieces[0].dtype)
        for piece, at in zip(pieces, places):
            whole = lax.dynamic_update_slice_in_dim(whole, piece, at * rows, 0)
        return whole

    def dp_of(dp, c, flip):
        core = lax.rem(dp, cores)
        return lax.rem(dp - core - c * cores + n_dp, n_dp) + (1 - core if flip else core)

    by_row = [cotangent] + [along("row", n_row, s)(cotangent) for s in range(1, n_row)]
    by_chip = {(c, 0): chip_shift(c)(cotangent) for c in range(1, chips)}
    swapped = {(0, 0): swap_cores(cotangent)} if cores == 2 else {}

    flips = range(cores)
    targets = [[functools.partial(dp_of, c=0, flip=1)]] if cores == 2 else []
    targets += [[functools.partial(dp_of, c=chips - c, flip=f) for f in flips] for c in range(1, chips)]
    if tiled:
        made = forward_call(place, inputs, weight, own, n_row, slice_rows, targets)
        parts, to_send = made[:n_row], made[n_row:]
    else:
        part = jnp.dot(inputs, weight, preferred_element_type=F32)
        parts = [
            lax.dynamic_slice_in_dim(part, lax.rem(row + s, n_row) * own, own, 0).astype(
                BF16
            )
            for s in range(n_row)
        ]
        to_send = [
            jnp.concatenate(
                [
                    lax.dynamic_slice_in_dim(inputs, owner(dp) * slice_rows, slice_rows, 1)
                    for owner in owners
                ],
                0,
            )
            for owners in targets
        ]
    to_send = list(to_send)
    sums = [
        along("row", n_row, s)(after(parts[s], *swapped.values())) for s in range(1, n_row)
    ]
    near = [swap_cores(to_send.pop(0))] if cores == 2 else []
    first = [by_chip[c, 0] for c in range(1, chips)]
    far = [chip_shift(c)(to_send[c - 1]) for c in range(1, chips)]
    for s in range(1, n_row):
        by_row[s] = after(by_row[s], parts[0], *near, *first, *swapped.values())
        if cores == 2:
            swapped[0, s] = swap_cores(by_row[s])
    if cores == 2:
        for c in range(1, chips):
            swapped[c, 0] = swap_cores(by_chip[c, 0])

    held, sources = list(near), [(functools.partial(dp_of, c=0, flip=0), 0)]
    if cores == 2:
        sources.append((functools.partial(dp_of, c=0, flip=1), 0))
    for c in range(1, chips):
        for f in flips:
            piece = far[c - 1]
            held.append(swap_cores(after(piece, *first, *by_row[1:])) if f else piece)
            sources.append((functools.partial(dp_of, c=c, flip=f), f * tokens))
    if tiled:
        features = features_call(place, inputs, held, sources, slice_rows)
    else:
        mine = lax.dynamic_slice_in_dim(inputs, dp * slice_rows, slice_rows, 1)
        features = in_order(
            [mine] + [h[skip : skip + tokens] for h, (_, skip) in zip(held, sources[1:])],
            [origin(dp) for origin, _ in sources],
            tokens,
        )
    if tiled:
        ready = [by_row[0]] + [after(piece, *held) for piece in by_row[1:]]
        gpart = input_grad_call(place, ready, weight, n_row)
    else:
        gathered = in_order(by_row, [lax.rem(row - s + n_row, n_row) for s in range(n_row)], own)
        gpart = lax.dot_general(
            gathered, weight, (((1,), (1,)), ((), ())), preferred_element_type=F32
        ).astype(BF16)
    gparts = lax.all_to_all(gpart, "col", 0, 0, tiled=True)
    for s in range(1, n_row):
        for c in range(1, chips):
            by_chip[c, s] = chip_shift(c)(by_row[s])
    by_chip.update({(0, s): by_row[s] for s in range(n_row)})
    origins = []
    for c in range(chips):
        for s in range(n_row):
            for flip in range(cores):

                def origin(dp, row, c=c, s=s, flip=flip):
                    return dp_of(dp, c, flip) * n_row + lax.rem(row - s + n_row, n_row)

                origins.append(origin)

    pieces = []
    for c in range(chips):
        for s in range(n_row):
            early = c == 0 or s == 0
            pieces.append(in_hbm(by_chip[c, s]) if tiled and early else by_chip[c, s])
            if cores == 2:
                if (c, s) in swapped:
                    first_swap = tiled and (c, s) == (0, 0)
                    pieces.append(in_hbm(swapped[c, s]) if first_swap else swapped[c, s])
                else:
                    pieces.append(swap_cores(by_chip[c, s]))

    if tiled:
        streamed = map(in_hbm, (weight, anchor, first_moment, second_moment))
        new_weight, new_first, new_second = update_call(
            place, features, pieces, origins, tuple(streamed)
        )
    else:
        gathered = in_order(pieces, [origin(dp, row) for origin in origins], own)
        summed = lax.dot_general(
            features, gathered, (((0,), (0,)), ((), ())), preferred_element_type=F32
        )
        current = lax.dynamic_slice_in_dim(weight, dp * slice_rows, slice_rows, 0).astype(F32)
        new_weight, new_first, new_second = updated(
            summed,
            tokens * n_dp,
            current,
            anchor.astype(F32),
            first_moment,
            second_moment,
            lambda value: 1.0 / value,
        )
        new_weight = new_weight.astype(BF16)
    gparts = after(gparts, new_first)
    if tiled:
        input_grad, outputs = totals_call(place, gparts, [parts[0], *sums], n_col)
    else:
        input_grad = total(
            [lax.slice_in_dim(gparts, k * share, (k + 1) * share) for k in range(n_col)]
        )
        outputs = total([parts[0], *sums])
    return (outputs, input_grad, new_weight, new_first, new_second)


def solution(mesh):
    in_specs = (
        P("dp", "row"),
        P("row", "col"),
        P(("dp", "row"), "col"),
        P(("row", "dp"), "col"),
        P(("row", "dp"), "col"),
        P(("row", "dp"), "col"),
    )
    out_specs = (
        P(("dp", "row"), "col"),
        P(("dp", "col"), "row"),
        P(("row", "dp"), "col"),
        P(("row", "dp"), "col"),
        P(("row", "dp"), "col"),
    )
    return jax.shard_map(
        per_device, mesh=mesh, in_specs=in_specs, out_specs=out_specs, check_vma=False
    )
```

```python
import functools
import math

import jax
import jax.numpy as jnp
from jax import lax
from jax.experimental import pallas as pl
from jax.experimental.pallas import tpu as pltpu
from jax.sharding import PartitionSpec as P

beta_one = 0.9
beta_two = 0.999
learn_rate = 0.002
anchor_pull = 0.5
epsilon = 1e-08
step_count = 100.0

BF16, F32 = jnp.bfloat16, jnp.float32
MIB = 1 << 20


def block_of(size, most):
    return max(b for b in range(128, most + 1, 128) if size % b == 0)


def struct(shape, dtype):
    return jax.ShapeDtypeStruct(shape, dtype)


def run(kernel, name, grid, in_specs, out_specs, out_shape, scratch, limit, args, bytes_moved=1):
    return pl.pallas_call(
        kernel,
        name=name,
        grid_spec=pltpu.PrefetchScalarGridSpec(
            num_scalar_prefetch=1,
            grid=grid,
            in_specs=in_specs,
            out_specs=out_specs,
            scratch_shapes=scratch,
        ),
        out_shape=out_shape,
        compiler_params=pltpu.CompilerParams(vmem_limit_bytes=limit * MIB),
        cost_estimate=pl.CostEstimate(
            flops=1, bytes_accessed=bytes_moved, transcendentals=0
        ),
    )(*args)


def in_hbm(array):
    return pltpu.with_memory_space_constraint(array, pltpu.HBM)


def in_vmem(array):
    return pltpu.with_memory_space_constraint(array, pltpu.VMEM)


def load_parts(source, target, sems, axis, part):
    loads = []
    for k in range(source.shape[axis] // part):
        at = (slice(None),) * axis + (pl.ds(k * part, part),)
        loads.append((at, pltpu.make_async_copy(source.at[at], target.at[at], sems.at[k])))
    for _, load in loads:
        load.start()
    return loads


def fixed(shape):
    return pl.BlockSpec(shape, lambda j, place: (0,) * len(shape))


def columns(rows, width):
    return pl.BlockSpec((rows, width), lambda j, place: (0, j))


def forward_kernel(n_row, own, slice_rows, targets, part, place, x_ref, w_hbm, *rest):
    outs, sent, (xs, ws, sems) = rest[:n_row], rest[n_row:-3], rest[-3:]
    dp, row = place[0], place[1]
    tokens = x_ref.shape[0]
    loads = load_parts(w_hbm, ws, sems, 1, part)
    for s in range(n_row):
        start = pl.multiple_of(lax.rem(row + s, n_row) * own, own)
        xs[s * own : (s + 1) * own, :] = x_ref[pl.ds(start, own), :]
    for out, owners in zip(sent, targets):
        for k, owner in enumerate(owners):
            start = pl.multiple_of(owner(dp) * slice_rows, slice_rows)
            out[k * tokens : (k + 1) * tokens, :] = x_ref[:, pl.ds(start, slice_rows)]
    for at, load in loads:
        load.wait()
        acc = jnp.dot(xs[...], ws[at], preferred_element_type=F32)
        for s in range(n_row):
            outs[s][at] = acc[s * own : (s + 1) * own].astype(outs[s].dtype)


def forward_call(place, inputs, weight, own, n_row, slice_rows, targets):
    tokens, depth = inputs.shape
    width = weight.shape[1]
    part = block_of(width, 512)
    sent = [(len(owners) * tokens, slice_rows) for owners in targets]
    return run(
        functools.partial(forward_kernel, n_row, own, slice_rows, targets, part),
        "forward",
        (1,),
        [fixed((tokens, depth)), pl.BlockSpec(memory_space=pltpu.HBM)],
        [fixed((own, width))] * n_row + [fixed(shape) for shape in sent],
        [struct((own, width), BF16)] * n_row + [struct(shape, BF16) for shape in sent],
        [
            pltpu.VMEM((tokens, depth), BF16),
            pltpu.VMEM((depth, width), BF16),
            pltpu.SemaphoreType.DMA((width // part,)),
        ],
        24,
        (place, inputs, in_hbm(weight)),
    )


def input_grad_kernel(n_row, own, place, *rest):
    pieces, w_ref, out, cs = rest[:n_row], rest[n_row], rest[n_row + 1], rest[n_row + 2]

    @pl.when(pl.program_id(0) == 0)
    def _():
        for s in range(n_row):
            start = pl.multiple_of(lax.rem(place[1] - s + n_row, n_row) * own, own)
            cs[pl.ds(start, own), :] = pieces[s][...]

    out[...] = lax.dot_general(
        cs[...], w_ref[...], (((1,), (1,)), ((), ())), preferred_element_type=F32
    ).astype(BF16)


def input_grad_call(place, by_row, weight, n_row):
    own, width = by_row[0].shape
    depth = weight.shape[0]
    block = block_of(depth, 256)
    return run(
        functools.partial(input_grad_kernel, n_row, own),
        "input_grad",
        (depth // block,),
        [fixed((own, width))] * n_row + [pl.BlockSpec((block, width), lambda j, place: (j, 0))],
        columns(n_row * own, block),
        struct((n_row * own, depth), BF16),
        [pltpu.VMEM((n_row * own, width), BF16)],
        6,
        (place, *by_row, in_vmem(weight)),
    )


def features_kernel(sources, tokens, place, *rest):
    n = len(sources)
    pieces, out, xs = rest[:n], rest[n], rest[n + 1]
    for piece, (origin, skip) in zip(pieces, sources):
        start = pl.multiple_of(origin(place[0]) * tokens, tokens)
        xs[pl.ds(start, tokens), :] = piece[skip : skip + tokens, :]
    out[...] = xs[...].T


def features_call(place, inputs, held, sources, slice_rows):
    tokens, n_dp = inputs.shape[0], len(sources)
    return run(
        functools.partial(features_kernel, sources, tokens),
        "features",
        (1,),
        [pl.BlockSpec((tokens, slice_rows), lambda j, place: (0, place[0]))]
        + [fixed(piece.shape) for piece in held],
        fixed((slice_rows, n_dp * tokens)),
        struct((slice_rows, n_dp * tokens), BF16),
        [pltpu.VMEM((n_dp * tokens, slice_rows), BF16)],
        6,
        (place, inputs, *held),
    )


def total(parts):
    whole = parts[0].astype(F32)
    for part in parts[1:]:
        whole = whole + part.astype(F32)
    return whole.astype(BF16)


def totals_kernel(n, place, parts, *rest):
    sums, (grad, out) = rest[:-2], rest[-2:]
    share = grad.shape[0]
    grad[...] = total([parts[k * share : (k + 1) * share, :] for k in range(n)])
    out[...] = total([part[...] for part in sums])


def totals_call(place, parts, sums, n):
    rows, width = parts.shape
    return run(
        functools.partial(totals_kernel, n),
        "totals",
        (1,),
        [fixed(parts.shape)] + [fixed(part.shape) for part in sums],
        [fixed((rows // n, width)), fixed(sums[0].shape)],
        [struct((rows // n, width), BF16), struct(sums[0].shape, BF16)],
        [],
        10,
        (place, parts, *sums),
    )


def inverse(value):
    guess = pl.reciprocal(value, approx=True)
    return guess * (2.0 - value * guess)


def updated(grad_sum, tokens_all, current, anchor, first, second, invert):
    grad = grad_sum * (1.0 / tokens_all) + anchor_pull * (current - anchor)
    first = beta_one * first + (1.0 - beta_one) * grad
    second = beta_two * second + (1.0 - beta_two) * grad * grad
    root = math.sqrt(1.0 / (1.0 - beta_two**step_count))
    scale = learn_rate / (1.0 - beta_one**step_count) / root
    spread = second * lax.rsqrt(second) + epsilon / root
    return current - (scale * first) * invert(spread), first, second


def update_kernel(origins, tokens_all, chunk, part, place, x_ref, *rest):
    n = len(origins)
    pieces = rest[:n]
    w_ref, a_ref, m_ref, v_ref, new_w, new_m, new_v, cs = rest[n:]
    own, width = pieces[0].shape

    @pl.when(pl.program_id(0) == 0)
    def _():
        for piece, origin in zip(pieces, origins):
            start = pl.multiple_of(origin(place[0], place[1]) * own, own)
            cs[pl.ds(start, own), :] = piece[...]

    for c in range(0, width, part):
        across = slice(c, c + part)
        summed = jnp.dot(x_ref[...], cs[:, across], preferred_element_type=F32)
        for r in range(0, x_ref.shape[0], chunk):
            at = (slice(r, r + chunk), across)
            weight, first, second = updated(
                summed[r : r + chunk],
                tokens_all,
                w_ref[at].astype(F32),
                a_ref[at].astype(F32),
                m_ref[at],
                v_ref[at],
                inverse,
            )
            new_w[at] = weight.astype(BF16)
            new_m[at] = first
            new_v[at] = second


def update_call(place, features, pieces, origins, held):
    rows, width = held[1].shape
    tokens_all = features.shape[1]
    block = math.gcd(rows, 128)
    tile = pl.BlockSpec((block, width), lambda j, place: (j, 0))
    return run(
        functools.partial(
            update_kernel, origins, tokens_all, math.gcd(block, 32), block_of(width, 512)
        ),
        "update",
        (rows // block,),
        [pl.BlockSpec((block, tokens_all), lambda j, place: (j, 0))]
        + [fixed(piece.shape) for piece in pieces]
        + [pl.BlockSpec((block, width), lambda j, place: (place[0] * (rows // block) + j, 0))]
        + [tile] * 3,
        [tile] * 3,
        [struct((rows, width), BF16), struct((rows, width), F32), struct((rows, width), F32)],
        [pltpu.VMEM((tokens_all, width), BF16)],
        38,
        (place, features, *pieces, *held),
    )


def after(value, *others):
    return lax.optimization_barrier((value, *others))[0]


def per_device(inputs, weight, cotangent, anchor, first_moment, second_moment):
    n_dp, n_row, n_col = (lax.axis_size(a) for a in ("dp", "row", "col"))
    dp, row, col = (lax.axis_index(a) for a in ("dp", "row", "col"))
    place = jnp.stack([dp, row, col]).astype(jnp.int32)
    cores = 2 if n_dp % 2 == 0 else 1
    chips = n_dp // cores
    tokens = inputs.shape[0]
    own = cotangent.shape[0]
    share = tokens // n_col
    slice_rows = weight.shape[0] // n_dp
    tiled = own % 16 == 0 and share % 16 == 0 and slice_rows % 128 == 0

    def along(axis, n, shift):
        return lambda a: lax.ppermute(a, axis, [(i, (i + shift) % n) for i in range(n)])

    def chip_shift(shift):
        return along("dp", n_dp, shift * cores)

    def swap_cores(a):
        return lax.ppermute(a, "dp", [(i, i ^ 1) for i in range(n_dp)])

    def in_order(pieces, places, rows):
        whole = jnp.zeros((len(pieces) * rows, pieces[0].shape[1]), pieces[0].dtype)
        for piece, at in zip(pieces, places):
            whole = lax.dynamic_update_slice_in_dim(whole, piece, at * rows, 0)
        return whole

    def dp_of(dp, c, flip):
        core = lax.rem(dp, cores)
        return lax.rem(dp - core - c * cores + n_dp, n_dp) + (1 - core if flip else core)

    by_row = [cotangent] + [along("row", n_row, s)(cotangent) for s in range(1, n_row)]
    by_chip = {(c, 0): chip_shift(c)(cotangent) for c in range(1, chips)}
    swapped = {(0, 0): swap_cores(cotangent)} if cores == 2 else {}

    flips = range(cores)
    targets = [[functools.partial(dp_of, c=0, flip=1)]] if cores == 2 else []
    targets += [[functools.partial(dp_of, c=chips - c, flip=f) for f in flips] for c in range(1, chips)]
    if tiled:
        made = forward_call(place, inputs, weight, own, n_row, slice_rows, targets)
        parts, to_send = made[:n_row], made[n_row:]
    else:
        part = jnp.dot(inputs, weight, preferred_element_type=F32)
        parts = [
            lax.dynamic_slice_in_dim(part, lax.rem(row + s, n_row) * own, own, 0).astype(
                BF16
            )
            for s in range(n_row)
        ]
        to_send = [
            jnp.concatenate(
                [
                    lax.dynamic_slice_in_dim(inputs, owner(dp) * slice_rows, slice_rows, 1)
                    for owner in owners
                ],
                0,
            )
            for owners in targets
        ]
    to_send = list(to_send)
    sums = [
        along("row", n_row, s)(after(parts[s], *swapped.values())) for s in range(1, n_row)
    ]
    near = [swap_cores(to_send.pop(0))] if cores == 2 else []
    first = [by_chip[c, 0] for c in range(1, chips)]
    far = [chip_shift(c)(after(to_send[c - 1], *first)) for c in range(1, chips)]
    for s in range(1, n_row):
        by_row[s] = after(by_row[s], parts[0], *near, *first, *swapped.values())
        if cores == 2:
            swapped[0, s] = swap_cores(by_row[s])
    if cores == 2:
        for c in range(1, chips):
            swapped[c, 0] = swap_cores(by_chip[c, 0])

    held, sources = list(near), [(functools.partial(dp_of, c=0, flip=0), 0)]
    if cores == 2:
        sources.append((functools.partial(dp_of, c=0, flip=1), 0))
    for c in range(1, chips):
        for f in flips:
            piece = far[c - 1]
            held.append(swap_cores(piece) if f else piece)
            sources.append((functools.partial(dp_of, c=c, flip=f), f * tokens))
    if tiled:
        features = features_call(place, inputs, held, sources, slice_rows)
    else:
        mine = lax.dynamic_slice_in_dim(inputs, dp * slice_rows, slice_rows, 1)
        features = in_order(
            [mine] + [h[skip : skip + tokens] for h, (_, skip) in zip(held, sources[1:])],
            [origin(dp) for origin, _ in sources],
            tokens,
        )
    if tiled:
        gpart = input_grad_call(place, by_row, weight, n_row)
    else:
        gathered = in_order(by_row, [lax.rem(row - s + n_row, n_row) for s in range(n_row)], own)
        gpart = lax.dot_general(
            gathered, weight, (((1,), (1,)), ((), ())), preferred_element_type=F32
        ).astype(BF16)
    gparts = lax.all_to_all(gpart, "col", 0, 0, tiled=True)
    for s in range(1, n_row):
        for c in range(1, chips):
            by_chip[c, s] = along("row", n_row, s)(by_chip[c, 0])
    by_chip.update({(0, s): by_row[s] for s in range(n_row)})
    origins = []
    for c in range(chips):
        for s in range(n_row):
            for flip in range(cores):

                def origin(dp, row, c=c, s=s, flip=flip):
                    return dp_of(dp, c, flip) * n_row + lax.rem(row - s + n_row, n_row)

                origins.append(origin)

    pieces = []
    for c in range(chips):
        for s in range(n_row):
            early = c == 0 or s == 0
            pieces.append(in_hbm(by_chip[c, s]) if tiled and early else by_chip[c, s])
            if cores == 2:
                if (c, s) in swapped:
                    first_swap = tiled and (c, s) == (0, 0)
                    pieces.append(in_hbm(swapped[c, s]) if first_swap else swapped[c, s])
                else:
                    pieces.append(swap_cores(by_chip[c, s]))

    if tiled:
        streamed = map(in_hbm, (weight, anchor, first_moment, second_moment))
        new_weight, new_first, new_second = update_call(
            place, features, pieces, origins, tuple(streamed)
        )
    else:
        gathered = in_order(pieces, [origin(dp, row) for origin in origins], own)
        summed = lax.dot_general(
            features, gathered, (((0,), (0,)), ((), ())), preferred_element_type=F32
        )
        current = lax.dynamic_slice_in_dim(weight, dp * slice_rows, slice_rows, 0).astype(F32)
        new_weight, new_first, new_second = updated(
            summed,
            tokens * n_dp,
            current,
            anchor.astype(F32),
            first_moment,
            second_moment,
            lambda value: 1.0 / value,
        )
        new_weight = new_weight.astype(BF16)
    gparts = after(gparts, new_first)
    if tiled:
        input_grad, outputs = totals_call(place, gparts, [parts[0], *sums], n_col)
    else:
        input_grad = total(
            [lax.slice_in_dim(gparts, k * share, (k + 1) * share) for k in range(n_col)]
        )
        outputs = total([parts[0], *sums])
    return (outputs, input_grad, new_weight, new_first, new_second)


def solution(mesh):
    in_specs = (
        P("dp", "row"),
        P("row", "col"),
        P(("dp", "row"), "col"),
        P(("row", "dp"), "col"),
        P(("row", "dp"), "col"),
        P(("row", "dp"), "col"),
    )
    out_specs = (
        P(("dp", "row"), "col"),
        P(("dp", "col"), "row"),
        P(("row", "dp"), "col"),
        P(("row", "dp"), "col"),
        P(("row", "dp"), "col"),
    )
    return jax.shard_map(
        per_device, mesh=mesh, in_specs=in_specs, out_specs=out_specs, check_vma=False
    )
```

```python
import functools
import math

import jax
import jax.numpy as jnp
from jax import lax
from jax.experimental import pallas as pl
from jax.experimental.pallas import tpu as pltpu
from jax.sharding import PartitionSpec as P

beta_one = 0.9
beta_two = 0.999
learn_rate = 0.002
anchor_pull = 0.5
epsilon = 1e-08
step_count = 100.0

BF16, F32 = jnp.bfloat16, jnp.float32
MIB = 1 << 20


def block_of(size, most):
    return max(b for b in range(128, most + 1, 128) if size % b == 0)


def struct(shape, dtype):
    return jax.ShapeDtypeStruct(shape, dtype)


def run(kernel, name, grid, in_specs, out_specs, out_shape, scratch, limit, args, bytes_moved=1):
    return pl.pallas_call(
        kernel,
        name=name,
        grid_spec=pltpu.PrefetchScalarGridSpec(
            num_scalar_prefetch=1,
            grid=grid,
            in_specs=in_specs,
            out_specs=out_specs,
            scratch_shapes=scratch,
        ),
        out_shape=out_shape,
        compiler_params=pltpu.CompilerParams(vmem_limit_bytes=limit * MIB),
        cost_estimate=pl.CostEstimate(
            flops=1, bytes_accessed=bytes_moved, transcendentals=0
        ),
    )(*args)


def in_hbm(array):
    return pltpu.with_memory_space_constraint(array, pltpu.HBM)


def in_vmem(array):
    return pltpu.with_memory_space_constraint(array, pltpu.VMEM)


def load_parts(source, target, sems, axis, part):
    loads = []
    for k in range(source.shape[axis] // part):
        at = (slice(None),) * axis + (pl.ds(k * part, part),)
        loads.append((at, pltpu.make_async_copy(source.at[at], target.at[at], sems.at[k])))
    for _, load in loads:
        load.start()
    return loads


def fixed(shape):
    return pl.BlockSpec(shape, lambda j, place: (0,) * len(shape))


def columns(rows, width):
    return pl.BlockSpec((rows, width), lambda j, place: (0, j))


def forward_kernel(n_row, own, slice_rows, targets, part, place, x_ref, w_hbm, *rest):
    outs, sent, (xs, ws, sems) = rest[:n_row], rest[n_row:-3], rest[-3:]
    dp, row = place[0], place[1]
    tokens = x_ref.shape[0]
    loads = load_parts(w_hbm, ws, sems, 1, part)
    for s in range(n_row):
        start = pl.multiple_of(lax.rem(row + s, n_row) * own, own)
        xs[s * own : (s + 1) * own, :] = x_ref[pl.ds(start, own), :]
    for out, owners in zip(sent, targets):
        for k, owner in enumerate(owners):
            start = pl.multiple_of(owner(dp) * slice_rows, slice_rows)
            out[k * tokens : (k + 1) * tokens, :] = x_ref[:, pl.ds(start, slice_rows)]
    for at, load in loads:
        load.wait()
        acc = jnp.dot(xs[...], ws[at], preferred_element_type=F32)
        for s in range(n_row):
            outs[s][at] = acc[s * own : (s + 1) * own].astype(outs[s].dtype)


def forward_call(place, inputs, weight, own, n_row, slice_rows, targets):
    tokens, depth = inputs.shape
    width = weight.shape[1]
    part = block_of(width, 512)
    sent = [(len(owners) * tokens, slice_rows) for owners in targets]
    return run(
        functools.partial(forward_kernel, n_row, own, slice_rows, targets, part),
        "forward",
        (1,),
        [fixed((tokens, depth)), pl.BlockSpec(memory_space=pltpu.HBM)],
        [fixed((own, width))] * n_row + [fixed(shape) for shape in sent],
        [struct((own, width), BF16)] * n_row + [struct(shape, BF16) for shape in sent],
        [
            pltpu.VMEM((tokens, depth), BF16),
            pltpu.VMEM((depth, width), BF16),
            pltpu.SemaphoreType.DMA((width // part,)),
        ],
        24,
        (place, inputs, in_hbm(weight)),
    )


def input_grad_kernel(n_row, own, place, *rest):
    pieces, w_ref, out, cs = rest[:n_row], rest[n_row], rest[n_row + 1], rest[n_row + 2]

    @pl.when(pl.program_id(0) == 0)
    def _():
        for s in range(n_row):
            start = pl.multiple_of(lax.rem(place[1] - s + n_row, n_row) * own, own)
            cs[pl.ds(start, own), :] = pieces[s][...]

    out[...] = lax.dot_general(
        cs[...], w_ref[...], (((1,), (1,)), ((), ())), preferred_element_type=F32
    ).astype(BF16)


def input_grad_call(place, by_row, weight, n_row):
    own, width = by_row[0].shape
    depth = weight.shape[0]
    block = block_of(depth, 256)
    return run(
        functools.partial(input_grad_kernel, n_row, own),
        "input_grad",
        (depth // block,),
        [fixed((own, width))] * n_row + [pl.BlockSpec((block, width), lambda j, place: (j, 0))],
        columns(n_row * own, block),
        struct((n_row * own, depth), BF16),
        [pltpu.VMEM((n_row * own, width), BF16)],
        6,
        (place, *by_row, in_vmem(weight)),
    )


def features_kernel(sources, tokens, place, *rest):
    n = len(sources)
    pieces, out, xs = rest[:n], rest[n], rest[n + 1]
    for piece, (origin, skip) in zip(pieces, sources):
        start = pl.multiple_of(origin(place[0]) * tokens, tokens)
        xs[pl.ds(start, tokens), :] = piece[skip : skip + tokens, :]
    out[...] = xs[...].T


def features_call(place, inputs, held, sources, slice_rows):
    tokens, n_dp = inputs.shape[0], len(sources)
    return run(
        functools.partial(features_kernel, sources, tokens),
        "features",
        (1,),
        [pl.BlockSpec((tokens, slice_rows), lambda j, place: (0, place[0]))]
        + [fixed(piece.shape) for piece in held],
        fixed((slice_rows, n_dp * tokens)),
        struct((slice_rows, n_dp * tokens), BF16),
        [pltpu.VMEM((n_dp * tokens, slice_rows), BF16)],
        6,
        (place, inputs, *held),
    )


def total(parts):
    whole = parts[0].astype(F32)
    for part in parts[1:]:
        whole = whole + part.astype(F32)
    return whole.astype(BF16)


def totals_kernel(n, place, parts, *rest):
    sums, (grad, out) = rest[:-2], rest[-2:]
    share = grad.shape[0]
    grad[...] = total([parts[k * share : (k + 1) * share, :] for k in range(n)])
    out[...] = total([part[...] for part in sums])


def totals_call(place, parts, sums, n):
    rows, width = parts.shape
    return run(
        functools.partial(totals_kernel, n),
        "totals",
        (1,),
        [fixed(parts.shape)] + [fixed(part.shape) for part in sums],
        [fixed((rows // n, width)), fixed(sums[0].shape)],
        [struct((rows // n, width), BF16), struct(sums[0].shape, BF16)],
        [],
        10,
        (place, parts, *sums),
    )


def inverse(value):
    guess = pl.reciprocal(value, approx=True)
    return guess * (2.0 - value * guess)


def updated(grad_sum, tokens_all, current, anchor, first, second, invert):
    grad = grad_sum * (1.0 / tokens_all) + anchor_pull * (current - anchor)
    first = beta_one * first + (1.0 - beta_one) * grad
    second = beta_two * second + (1.0 - beta_two) * grad * grad
    root = math.sqrt(1.0 / (1.0 - beta_two**step_count))
    scale = learn_rate / (1.0 - beta_one**step_count) / root
    spread = second * lax.rsqrt(second) + epsilon / root
    return current - (scale * first) * invert(spread), first, second


def update_kernel(origins, tokens_all, chunk, part, place, x_ref, *rest):
    n = len(origins)
    pieces = rest[:n]
    w_ref, a_ref, m_ref, v_ref, new_w, new_m, new_v, cs = rest[n:]
    own, width = pieces[0].shape

    @pl.when(pl.program_id(0) == 0)
    def _():
        for piece, origin in zip(pieces, origins):
            start = pl.multiple_of(origin(place[0], place[1]) * own, own)
            cs[pl.ds(start, own), :] = piece[...]

    for c in range(0, width, part):
        across = slice(c, c + part)
        summed = jnp.dot(x_ref[...], cs[:, across], preferred_element_type=F32)
        for r in range(0, x_ref.shape[0], chunk):
            at = (slice(r, r + chunk), across)
            weight, first, second = updated(
                summed[r : r + chunk],
                tokens_all,
                w_ref[at].astype(F32),
                a_ref[at].astype(F32),
                m_ref[at],
                v_ref[at],
                inverse,
            )
            new_w[at] = weight.astype(BF16)
            new_m[at] = first
            new_v[at] = second


def update_call(place, features, pieces, origins, held):
    rows, width = held[1].shape
    tokens_all = features.shape[1]
    block = math.gcd(rows, 128)
    tile = pl.BlockSpec((block, width), lambda j, place: (j, 0))
    return run(
        functools.partial(
            update_kernel, origins, tokens_all, math.gcd(block, 32), block_of(width, 512)
        ),
        "update",
        (rows // block,),
        [pl.BlockSpec((block, tokens_all), lambda j, place: (j, 0))]
        + [fixed(piece.shape) for piece in pieces]
        + [pl.BlockSpec((block, width), lambda j, place: (place[0] * (rows // block) + j, 0))]
        + [tile] * 3,
        [tile] * 3,
        [struct((rows, width), BF16), struct((rows, width), F32), struct((rows, width), F32)],
        [pltpu.VMEM((tokens_all, width), BF16)],
        38,
        (place, features, *pieces, *held),
    )


def after(value, *others):
    return lax.optimization_barrier((value, *others))[0]


def per_device(inputs, weight, cotangent, anchor, first_moment, second_moment):
    n_dp, n_row, n_col = (lax.axis_size(a) for a in ("dp", "row", "col"))
    dp, row, col = (lax.axis_index(a) for a in ("dp", "row", "col"))
    place = jnp.stack([dp, row, col]).astype(jnp.int32)
    cores = 2 if n_dp % 2 == 0 else 1
    chips = n_dp // cores
    tokens = inputs.shape[0]
    own = cotangent.shape[0]
    share = tokens // n_col
    slice_rows = weight.shape[0] // n_dp
    tiled = own % 16 == 0 and share % 16 == 0 and slice_rows % 128 == 0

    def along(axis, n, shift):
        return lambda a: lax.ppermute(a, axis, [(i, (i + shift) % n) for i in range(n)])

    def chip_shift(shift):
        return along("dp", n_dp, shift * cores)

    def swap_cores(a):
        return lax.ppermute(a, "dp", [(i, i ^ 1) for i in range(n_dp)])

    def in_order(pieces, places, rows):
        whole = jnp.zeros((len(pieces) * rows, pieces[0].shape[1]), pieces[0].dtype)
        for piece, at in zip(pieces, places):
            whole = lax.dynamic_update_slice_in_dim(whole, piece, at * rows, 0)
        return whole

    def dp_of(dp, c, flip):
        core = lax.rem(dp, cores)
        return lax.rem(dp - core - c * cores + n_dp, n_dp) + (1 - core if flip else core)

    by_row = [cotangent] + [along("row", n_row, s)(cotangent) for s in range(1, n_row)]
    by_chip = {(c, 0): chip_shift(c)(cotangent) for c in range(1, chips)}
    swapped = {(0, 0): swap_cores(cotangent)} if cores == 2 else {}

    flips = range(cores)
    targets = [[functools.partial(dp_of, c=0, flip=1)]] if cores == 2 else []
    targets += [[functools.partial(dp_of, c=chips - c, flip=f) for f in flips] for c in range(1, chips)]
    if tiled:
        made = forward_call(place, inputs, weight, own, n_row, slice_rows, targets)
        parts, to_send = made[:n_row], made[n_row:]
    else:
        part = jnp.dot(inputs, weight, preferred_element_type=F32)
        parts = [
            lax.dynamic_slice_in_dim(part, lax.rem(row + s, n_row) * own, own, 0).astype(
                BF16
            )
            for s in range(n_row)
        ]
        to_send = [
            jnp.concatenate(
                [
                    lax.dynamic_slice_in_dim(inputs, owner(dp) * slice_rows, slice_rows, 1)
                    for owner in owners
                ],
                0,
            )
            for owners in targets
        ]
    to_send = list(to_send)
    sums = [
        along("row", n_row, s)(after(parts[s], *swapped.values())) for s in range(1, n_row)
    ]
    near = [swap_cores(to_send.pop(0))] if cores == 2 else []
    first = [by_chip[c, 0] for c in range(1, chips)]
    far = [chip_shift(c)(after(to_send[c - 1], *first)) for c in range(1, chips)]
    for s in range(1, n_row):
        by_row[s] = after(by_row[s], parts[0], *near, *first, *swapped.values())
        if cores == 2:
            swapped[0, s] = swap_cores(by_row[s])
    if cores == 2:
        for c in range(1, chips):
            swapped[c, 0] = swap_cores(by_chip[c, 0])

    held, sources = list(near), [(functools.partial(dp_of, c=0, flip=0), 0)]
    if cores == 2:
        sources.append((functools.partial(dp_of, c=0, flip=1), 0))
    for c in range(1, chips):
        for f in flips:
            piece = far[c - 1]
            held.append(swap_cores(piece) if f else piece)
            sources.append((functools.partial(dp_of, c=c, flip=f), f * tokens))
    if tiled:
        features = features_call(place, inputs, held, sources, slice_rows)
    else:
        mine = lax.dynamic_slice_in_dim(inputs, dp * slice_rows, slice_rows, 1)
        features = in_order(
            [mine] + [h[skip : skip + tokens] for h, (_, skip) in zip(held, sources[1:])],
            [origin(dp) for origin, _ in sources],
            tokens,
        )
    if tiled:
        gpart = input_grad_call(place, by_row, weight, n_row)
    else:
        gathered = in_order(by_row, [lax.rem(row - s + n_row, n_row) for s in range(n_row)], own)
        gpart = lax.dot_general(
            gathered, weight, (((1,), (1,)), ((), ())), preferred_element_type=F32
        ).astype(BF16)
    gparts = lax.all_to_all(gpart, "col", 0, 0, tiled=True)
    for s in range(1, n_row):
        for c in range(1, chips):
            by_chip[c, s] = along("row", n_row, s)(by_chip[c, 0])
    by_chip.update({(0, s): by_row[s] for s in range(n_row)})
    origins = []
    for c in range(chips):
        for s in range(n_row):
            for flip in range(cores):

                def origin(dp, row, c=c, s=s, flip=flip):
                    return dp_of(dp, c, flip) * n_row + lax.rem(row - s + n_row, n_row)

                origins.append(origin)

    pieces = []
    for c in range(chips):
        for s in range(n_row):
            early = c == 0 or s == 0
            pieces.append(in_hbm(by_chip[c, s]) if tiled and early else by_chip[c, s])
            if cores == 2:
                if (c, s) in swapped:
                    first_swap = tiled and (c, s) == (0, 0)
                    pieces.append(in_hbm(swapped[c, s]) if first_swap else swapped[c, s])
                else:
                    pieces.append(swap_cores(after(by_chip[c, s], features)))

    if tiled:
        streamed = map(in_hbm, (weight, anchor, first_moment, second_moment))
        new_weight, new_first, new_second = update_call(
            place, features, pieces, origins, tuple(streamed)
        )
    else:
        gathered = in_order(pieces, [origin(dp, row) for origin in origins], own)
        summed = lax.dot_general(
            features, gathered, (((0,), (0,)), ((), ())), preferred_element_type=F32
        )
        current = lax.dynamic_slice_in_dim(weight, dp * slice_rows, slice_rows, 0).astype(F32)
        new_weight, new_first, new_second = updated(
            summed,
            tokens * n_dp,
            current,
            anchor.astype(F32),
            first_moment,
            second_moment,
            lambda value: 1.0 / value,
        )
        new_weight = new_weight.astype(BF16)
    gparts = after(gparts, new_first)
    if tiled:
        input_grad, outputs = totals_call(place, gparts, [parts[0], *sums], n_col)
    else:
        input_grad = total(
            [lax.slice_in_dim(gparts, k * share, (k + 1) * share) for k in range(n_col)]
        )
        outputs = total([parts[0], *sums])
    return (outputs, input_grad, new_weight, new_first, new_second)


def solution(mesh):
    in_specs = (
        P("dp", "row"),
        P("row", "col"),
        P(("dp", "row"), "col"),
        P(("row", "dp"), "col"),
        P(("row", "dp"), "col"),
        P(("row", "dp"), "col"),
    )
    out_specs = (
        P(("dp", "row"), "col"),
        P(("dp", "col"), "row"),
        P(("row", "dp"), "col"),
        P(("row", "dp"), "col"),
        P(("row", "dp"), "col"),
    )
    return jax.shard_map(
        per_device, mesh=mesh, in_specs=in_specs, out_specs=out_specs, check_vma=False
    )
```

```python
import functools
import math

import jax
import jax.numpy as jnp
from jax import lax
from jax.experimental import pallas as pl
from jax.experimental.pallas import tpu as pltpu
from jax.sharding import PartitionSpec as P

beta_one = 0.9
beta_two = 0.999
learn_rate = 0.002
anchor_pull = 0.5
epsilon = 1e-08
step_count = 100.0

BF16, F32 = jnp.bfloat16, jnp.float32
MIB = 1 << 20


def block_of(size, most):
    return max(b for b in range(128, most + 1, 128) if size % b == 0)


def struct(shape, dtype):
    return jax.ShapeDtypeStruct(shape, dtype)


def run(kernel, name, grid, in_specs, out_specs, out_shape, scratch, limit, args, bytes_moved=1):
    return pl.pallas_call(
        kernel,
        name=name,
        grid_spec=pltpu.PrefetchScalarGridSpec(
            num_scalar_prefetch=1,
            grid=grid,
            in_specs=in_specs,
            out_specs=out_specs,
            scratch_shapes=scratch,
        ),
        out_shape=out_shape,
        compiler_params=pltpu.CompilerParams(vmem_limit_bytes=limit * MIB),
        cost_estimate=pl.CostEstimate(
            flops=1, bytes_accessed=bytes_moved, transcendentals=0
        ),
    )(*args)


def in_hbm(array):
    return pltpu.with_memory_space_constraint(array, pltpu.HBM)


def in_vmem(array):
    return pltpu.with_memory_space_constraint(array, pltpu.VMEM)


def load_parts(source, target, sems, axis, part):
    loads = []
    for k in range(source.shape[axis] // part):
        at = (slice(None),) * axis + (pl.ds(k * part, part),)
        loads.append((at, pltpu.make_async_copy(source.at[at], target.at[at], sems.at[k])))
    for _, load in loads:
        load.start()
    return loads


def fixed(shape):
    return pl.BlockSpec(shape, lambda j, place: (0,) * len(shape))


def columns(rows, width):
    return pl.BlockSpec((rows, width), lambda j, place: (0, j))


def forward_kernel(n_row, own, slice_rows, targets, part, place, x_ref, w_hbm, *rest):
    outs, sent, (xs, ws, sems) = rest[:n_row], rest[n_row:-3], rest[-3:]
    dp, row = place[0], place[1]
    tokens = x_ref.shape[0]
    loads = load_parts(w_hbm, ws, sems, 1, part)
    for s in range(n_row):
        start = pl.multiple_of(lax.rem(row + s, n_row) * own, own)
        xs[s * own : (s + 1) * own, :] = x_ref[pl.ds(start, own), :]
    for out, owners in zip(sent, targets):
        for k, owner in enumerate(owners):
            start = pl.multiple_of(owner(dp) * slice_rows, slice_rows)
            out[k * tokens : (k + 1) * tokens, :] = x_ref[:, pl.ds(start, slice_rows)]
    for at, load in loads:
        load.wait()
        acc = jnp.dot(xs[...], ws[at], preferred_element_type=F32)
        for s in range(n_row):
            outs[s][at] = acc[s * own : (s + 1) * own].astype(outs[s].dtype)


def forward_call(place, inputs, weight, own, n_row, slice_rows, targets):
    tokens, depth = inputs.shape
    width = weight.shape[1]
    part = block_of(width, 512)
    sent = [(len(owners) * tokens, slice_rows) for owners in targets]
    return run(
        functools.partial(forward_kernel, n_row, own, slice_rows, targets, part),
        "forward",
        (1,),
        [fixed((tokens, depth)), pl.BlockSpec(memory_space=pltpu.HBM)],
        [fixed((own, width))] * n_row + [fixed(shape) for shape in sent],
        [struct((own, width), BF16)] * n_row + [struct(shape, BF16) for shape in sent],
        [
            pltpu.VMEM((tokens, depth), BF16),
            pltpu.VMEM((depth, width), BF16),
            pltpu.SemaphoreType.DMA((width // part,)),
        ],
        24,
        (place, inputs, in_hbm(weight)),
    )


def input_grad_kernel(n_row, own, place, *rest):
    pieces, w_ref, out, cs = rest[:n_row], rest[n_row], rest[n_row + 1], rest[n_row + 2]

    @pl.when(pl.program_id(0) == 0)
    def _():
        for s in range(n_row):
            start = pl.multiple_of(lax.rem(place[1] - s + n_row, n_row) * own, own)
            cs[pl.ds(start, own), :] = pieces[s][...]

    out[...] = lax.dot_general(
        cs[...], w_ref[...], (((1,), (1,)), ((), ())), preferred_element_type=F32
    ).astype(BF16)


def input_grad_call(place, by_row, weight, n_row):
    own, width = by_row[0].shape
    depth = weight.shape[0]
    block = block_of(depth, 256)
    return run(
        functools.partial(input_grad_kernel, n_row, own),
        "input_grad",
        (depth // block,),
        [fixed((own, width))] * n_row + [pl.BlockSpec((block, width), lambda j, place: (j, 0))],
        columns(n_row * own, block),
        struct((n_row * own, depth), BF16),
        [pltpu.VMEM((n_row * own, width), BF16)],
        6,
        (place, *by_row, in_vmem(weight)),
    )


def features_kernel(sources, tokens, place, *rest):
    n = len(sources)
    pieces, moment, out, held, xs, sem = rest[:n], *rest[n:]
    copy = pltpu.make_async_copy(moment, held, sem)
    copy.start()
    for piece, (origin, skip) in zip(pieces, sources):
        start = pl.multiple_of(origin(place[0]) * tokens, tokens)
        xs[pl.ds(start, tokens), :] = piece[skip : skip + tokens, :]
    out[...] = xs[...].T
    copy.wait()


def features_call(place, inputs, held, sources, slice_rows, moment):
    tokens, n_dp = inputs.shape[0], len(sources)
    return run(
        functools.partial(features_kernel, sources, tokens),
        "features",
        (1,),
        [pl.BlockSpec((tokens, slice_rows), lambda j, place: (0, place[0]))]
        + [fixed(piece.shape) for piece in held]
        + [pl.BlockSpec(memory_space=pltpu.HBM)],
        [fixed((slice_rows, n_dp * tokens)), pl.BlockSpec(memory_space=pl.ANY)],
        [
            struct((slice_rows, n_dp * tokens), BF16),
            pltpu.VMEM(moment.shape, moment.dtype),
        ],
        [pltpu.VMEM((n_dp * tokens, slice_rows), BF16), pltpu.SemaphoreType.DMA],
        6,
        (place, inputs, *held, in_hbm(moment)),
    )


def total(parts):
    whole = parts[0].astype(F32)
    for part in parts[1:]:
        whole = whole + part.astype(F32)
    return whole.astype(BF16)


def totals_kernel(n, place, parts, *rest):
    sums, (grad, out) = rest[:-2], rest[-2:]
    share = grad.shape[0]
    grad[...] = total([parts[k * share : (k + 1) * share, :] for k in range(n)])
    out[...] = total([part[...] for part in sums])


def totals_call(place, parts, sums, n):
    rows, width = parts.shape
    return run(
        functools.partial(totals_kernel, n),
        "totals",
        (1,),
        [fixed(parts.shape)] + [fixed(part.shape) for part in sums],
        [fixed((rows // n, width)), fixed(sums[0].shape)],
        [struct((rows // n, width), BF16), struct(sums[0].shape, BF16)],
        [],
        10,
        (place, parts, *sums),
    )


def inverse(value):
    guess = pl.reciprocal(value, approx=True)
    return guess * (2.0 - value * guess)


def updated(grad_sum, tokens_all, current, anchor, first, second, invert):
    grad = grad_sum * (1.0 / tokens_all) + anchor_pull * (current - anchor)
    first = beta_one * first + (1.0 - beta_one) * grad
    second = beta_two * second + (1.0 - beta_two) * grad * grad
    root = math.sqrt(1.0 / (1.0 - beta_two**step_count))
    scale = learn_rate / (1.0 - beta_one**step_count) / root
    spread = second * lax.rsqrt(second) + epsilon / root
    return current - (scale * first) * invert(spread), first, second


def update_kernel(origins, tokens_all, chunk, part, place, x_ref, *rest):
    n = len(origins)
    pieces = rest[:n]
    w_ref, a_ref, m_ref, v_ref, new_w, new_m, new_v, cs = rest[n:]
    own, width = pieces[0].shape

    @pl.when(pl.program_id(0) == 0)
    def _():
        for piece, origin in zip(pieces, origins):
            start = pl.multiple_of(origin(place[0], place[1]) * own, own)
            cs[pl.ds(start, own), :] = piece[...]

    for c in range(0, width, part):
        across = slice(c, c + part)
        summed = jnp.dot(x_ref[...], cs[:, across], preferred_element_type=F32)
        for r in range(0, x_ref.shape[0], chunk):
            at = (slice(r, r + chunk), across)
            weight, first, second = updated(
                summed[r : r + chunk],
                tokens_all,
                w_ref[at].astype(F32),
                a_ref[at].astype(F32),
                m_ref[at],
                v_ref[at],
                inverse,
            )
            new_w[at] = weight.astype(BF16)
            new_m[at] = first
            new_v[at] = second


def update_call(place, features, pieces, origins, held):
    rows, width = held[1].shape
    tokens_all = features.shape[1]
    block = math.gcd(rows, 128)
    tile = pl.BlockSpec((block, width), lambda j, place: (j, 0))
    return run(
        functools.partial(
            update_kernel, origins, tokens_all, math.gcd(block, 32), block_of(width, 512)
        ),
        "update",
        (rows // block,),
        [pl.BlockSpec((block, tokens_all), lambda j, place: (j, 0))]
        + [fixed(piece.shape) for piece in pieces]
        + [pl.BlockSpec((block, width), lambda j, place: (place[0] * (rows // block) + j, 0))]
        + [tile] * 3,
        [tile] * 3,
        [struct((rows, width), BF16), struct((rows, width), F32), struct((rows, width), F32)],
        [pltpu.VMEM((tokens_all, width), BF16)],
        31,
        (place, features, *pieces, *held),
    )


def after(value, *others):
    return lax.optimization_barrier((value, *others))[0]


def per_device(inputs, weight, cotangent, anchor, first_moment, second_moment):
    n_dp, n_row, n_col = (lax.axis_size(a) for a in ("dp", "row", "col"))
    dp, row, col = (lax.axis_index(a) for a in ("dp", "row", "col"))
    place = jnp.stack([dp, row, col]).astype(jnp.int32)
    cores = 2 if n_dp % 2 == 0 else 1
    chips = n_dp // cores
    tokens = inputs.shape[0]
    own = cotangent.shape[0]
    share = tokens // n_col
    slice_rows = weight.shape[0] // n_dp
    tiled = own % 16 == 0 and share % 16 == 0 and slice_rows % 128 == 0

    def along(axis, n, shift):
        return lambda a: lax.ppermute(a, axis, [(i, (i + shift) % n) for i in range(n)])

    def chip_shift(shift):
        return along("dp", n_dp, shift * cores)

    def swap_cores(a):
        return lax.ppermute(a, "dp", [(i, i ^ 1) for i in range(n_dp)])

    def in_order(pieces, places, rows):
        whole = jnp.zeros((len(pieces) * rows, pieces[0].shape[1]), pieces[0].dtype)
        for piece, at in zip(pieces, places):
            whole = lax.dynamic_update_slice_in_dim(whole, piece, at * rows, 0)
        return whole

    def dp_of(dp, c, flip):
        core = lax.rem(dp, cores)
        return lax.rem(dp - core - c * cores + n_dp, n_dp) + (1 - core if flip else core)

    by_row = [cotangent] + [along("row", n_row, s)(cotangent) for s in range(1, n_row)]
    by_chip = {(c, 0): chip_shift(c)(cotangent) for c in range(1, chips)}
    swapped = {(0, 0): swap_cores(cotangent)} if cores == 2 else {}

    flips = range(cores)
    targets = [[functools.partial(dp_of, c=0, flip=1)]] if cores == 2 else []
    targets += [[functools.partial(dp_of, c=chips - c, flip=f) for f in flips] for c in range(1, chips)]
    if tiled:
        made = forward_call(place, inputs, weight, own, n_row, slice_rows, targets)
        parts, to_send = made[:n_row], made[n_row:]
    else:
        part = jnp.dot(inputs, weight, preferred_element_type=F32)
        parts = [
            lax.dynamic_slice_in_dim(part, lax.rem(row + s, n_row) * own, own, 0).astype(
                BF16
            )
            for s in range(n_row)
        ]
        to_send = [
            jnp.concatenate(
                [
                    lax.dynamic_slice_in_dim(inputs, owner(dp) * slice_rows, slice_rows, 1)
                    for owner in owners
                ],
                0,
            )
            for owners in targets
        ]
    to_send = list(to_send)
    sums = [
        along("row", n_row, s)(after(parts[s], *swapped.values())) for s in range(1, n_row)
    ]
    near = [swap_cores(to_send.pop(0))] if cores == 2 else []
    first = [by_chip[c, 0] for c in range(1, chips)]
    far = [chip_shift(c)(after(to_send[c - 1], *first)) for c in range(1, chips)]
    for s in range(1, n_row):
        by_row[s] = after(by_row[s], parts[0], *near, *first, *swapped.values())
        if cores == 2:
            swapped[0, s] = swap_cores(by_row[s])
    if cores == 2:
        for c in range(1, chips):
            swapped[c, 0] = swap_cores(by_chip[c, 0])

    held, sources = list(near), [(functools.partial(dp_of, c=0, flip=0), 0)]
    if cores == 2:
        sources.append((functools.partial(dp_of, c=0, flip=1), 0))
    for c in range(1, chips):
        for f in flips:
            piece = far[c - 1]
            held.append(swap_cores(piece) if f else piece)
            sources.append((functools.partial(dp_of, c=c, flip=f), f * tokens))
    if tiled:
        features, first_held = features_call(
            place, inputs, held, sources, slice_rows, first_moment
        )
    else:
        mine = lax.dynamic_slice_in_dim(inputs, dp * slice_rows, slice_rows, 1)
        features = in_order(
            [mine] + [h[skip : skip + tokens] for h, (_, skip) in zip(held, sources[1:])],
            [origin(dp) for origin, _ in sources],
            tokens,
        )
    if tiled:
        gpart = input_grad_call(place, by_row, weight, n_row)
    else:
        gathered = in_order(by_row, [lax.rem(row - s + n_row, n_row) for s in range(n_row)], own)
        gpart = lax.dot_general(
            gathered, weight, (((1,), (1,)), ((), ())), preferred_element_type=F32
        ).astype(BF16)
    gparts = lax.all_to_all(gpart, "col", 0, 0, tiled=True)
    for s in range(1, n_row):
        for c in range(1, chips):
            by_chip[c, s] = along("row", n_row, s)(by_chip[c, 0])
    by_chip.update({(0, s): by_row[s] for s in range(n_row)})
    origins = []
    for c in range(chips):
        for s in range(n_row):
            for flip in range(cores):

                def origin(dp, row, c=c, s=s, flip=flip):
                    return dp_of(dp, c, flip) * n_row + lax.rem(row - s + n_row, n_row)

                origins.append(origin)

    pieces = []
    for c in range(chips):
        for s in range(n_row):
            early = c == 0 or s == 0
            pieces.append(in_hbm(by_chip[c, s]) if tiled and early else by_chip[c, s])
            if cores == 2:
                if (c, s) in swapped:
                    first_swap = tiled and (c, s) == (0, 0)
                    pieces.append(in_hbm(swapped[c, s]) if first_swap else swapped[c, s])
                else:
                    pieces.append(swap_cores(after(by_chip[c, s], features)))

    if tiled:
        streamed = (in_hbm(weight), in_hbm(anchor), first_held, in_hbm(second_moment))
        new_weight, new_first, new_second = update_call(
            place, features, pieces, origins, streamed
        )
    else:
        gathered = in_order(pieces, [origin(dp, row) for origin in origins], own)
        summed = lax.dot_general(
            features, gathered, (((0,), (0,)), ((), ())), preferred_element_type=F32
        )
        current = lax.dynamic_slice_in_dim(weight, dp * slice_rows, slice_rows, 0).astype(F32)
        new_weight, new_first, new_second = updated(
            summed,
            tokens * n_dp,
            current,
            anchor.astype(F32),
            first_moment,
            second_moment,
            lambda value: 1.0 / value,
        )
        new_weight = new_weight.astype(BF16)
    gparts = after(gparts, new_first)
    if tiled:
        input_grad, outputs = totals_call(place, gparts, [parts[0], *sums], n_col)
    else:
        input_grad = total(
            [lax.slice_in_dim(gparts, k * share, (k + 1) * share) for k in range(n_col)]
        )
        outputs = total([parts[0], *sums])
    return (outputs, input_grad, new_weight, new_first, new_second)


def solution(mesh):
    in_specs = (
        P("dp", "row"),
        P("row", "col"),
        P(("dp", "row"), "col"),
        P(("row", "dp"), "col"),
        P(("row", "dp"), "col"),
        P(("row", "dp"), "col"),
    )
    out_specs = (
        P(("dp", "row"), "col"),
        P(("dp", "col"), "row"),
        P(("row", "dp"), "col"),
        P(("row", "dp"), "col"),
        P(("row", "dp"), "col"),
    )
    return jax.shard_map(
        per_device, mesh=mesh, in_specs=in_specs, out_specs=out_specs, check_vma=False
    )
```

```python
import functools
import math

import jax
import jax.numpy as jnp
from jax import lax
from jax.experimental import pallas as pl
from jax.experimental.pallas import tpu as pltpu
from jax.sharding import PartitionSpec as P

beta_one = 0.9
beta_two = 0.999
learn_rate = 0.002
anchor_pull = 0.5
epsilon = 1e-08
step_count = 100.0

BF16, F32 = jnp.bfloat16, jnp.float32
MIB = 1 << 20


def block_of(size, most):
    return max(b for b in range(128, most + 1, 128) if size % b == 0)


def struct(shape, dtype):
    return jax.ShapeDtypeStruct(shape, dtype)


def run(kernel, name, grid, in_specs, out_specs, out_shape, scratch, limit, args, bytes_moved=1):
    return pl.pallas_call(
        kernel,
        name=name,
        grid_spec=pltpu.PrefetchScalarGridSpec(
            num_scalar_prefetch=1,
            grid=grid,
            in_specs=in_specs,
            out_specs=out_specs,
            scratch_shapes=scratch,
        ),
        out_shape=out_shape,
        compiler_params=pltpu.CompilerParams(vmem_limit_bytes=limit * MIB),
        cost_estimate=pl.CostEstimate(
            flops=1, bytes_accessed=bytes_moved, transcendentals=0
        ),
    )(*args)


def in_hbm(array):
    return pltpu.with_memory_space_constraint(array, pltpu.HBM)


def in_vmem(array):
    return pltpu.with_memory_space_constraint(array, pltpu.VMEM)


def load_parts(source, target, sems, axis, part):
    loads = []
    for k in range(source.shape[axis] // part):
        at = (slice(None),) * axis + (pl.ds(k * part, part),)
        loads.append((at, pltpu.make_async_copy(source.at[at], target.at[at], sems.at[k])))
    for _, load in loads:
        load.start()
    return loads


def fixed(shape):
    return pl.BlockSpec(shape, lambda j, place: (0,) * len(shape))


def columns(rows, width):
    return pl.BlockSpec((rows, width), lambda j, place: (0, j))


def forward_kernel(n_row, own, slice_rows, targets, part, place, x_ref, w_hbm, *rest):
    outs, sent, (xs, ws, sems) = rest[:n_row], rest[n_row:-3], rest[-3:]
    dp, row = place[0], place[1]
    tokens = x_ref.shape[0]
    loads = load_parts(w_hbm, ws, sems, 1, part)
    for s in range(n_row):
        start = pl.multiple_of(lax.rem(row + s, n_row) * own, own)
        xs[s * own : (s + 1) * own, :] = x_ref[pl.ds(start, own), :]
    for out, owners in zip(sent, targets):
        for k, owner in enumerate(owners):
            start = pl.multiple_of(owner(dp) * slice_rows, slice_rows)
            out[k * tokens : (k + 1) * tokens, :] = x_ref[:, pl.ds(start, slice_rows)]
    for at, load in loads:
        load.wait()
        acc = jnp.dot(xs[...], ws[at], preferred_element_type=F32)
        for s in range(n_row):
            outs[s][at] = acc[s * own : (s + 1) * own].astype(outs[s].dtype)


def forward_call(place, inputs, weight, own, n_row, slice_rows, targets):
    tokens, depth = inputs.shape
    width = weight.shape[1]
    part = block_of(width, 512)
    sent = [(len(owners) * tokens, slice_rows) for owners in targets]
    return run(
        functools.partial(forward_kernel, n_row, own, slice_rows, targets, part),
        "forward",
        (1,),
        [fixed((tokens, depth)), pl.BlockSpec(memory_space=pltpu.HBM)],
        [fixed((own, width))] * n_row + [fixed(shape) for shape in sent],
        [struct((own, width), BF16)] * n_row + [struct(shape, BF16) for shape in sent],
        [
            pltpu.VMEM((tokens, depth), BF16),
            pltpu.VMEM((depth, width), BF16),
            pltpu.SemaphoreType.DMA((width // part,)),
        ],
        24,
        (place, inputs, in_hbm(weight)),
    )


def input_grad_kernel(n_row, own, place, *rest):
    pieces, w_ref, out, cs = rest[:n_row], rest[n_row], rest[n_row + 1], rest[n_row + 2]

    @pl.when(pl.program_id(0) == 0)
    def _():
        for s in range(n_row):
            start = pl.multiple_of(lax.rem(place[1] - s + n_row, n_row) * own, own)
            cs[pl.ds(start, own), :] = pieces[s][...]

    out[...] = lax.dot_general(
        cs[...], w_ref[...], (((1,), (1,)), ((), ())), preferred_element_type=F32
    ).astype(BF16)


def input_grad_call(place, by_row, weight, n_row):
    own, width = by_row[0].shape
    depth = weight.shape[0]
    block = block_of(depth, 256)
    return run(
        functools.partial(input_grad_kernel, n_row, own),
        "input_grad",
        (depth // block,),
        [fixed((own, width))] * n_row + [pl.BlockSpec((block, width), lambda j, place: (j, 0))],
        columns(n_row * own, block),
        struct((n_row * own, depth), BF16),
        [pltpu.VMEM((n_row * own, width), BF16)],
        6,
        (place, *by_row, in_vmem(weight)),
    )


def features_kernel(sources, tokens, place, *rest):
    n = len(sources)
    pieces, out, xs = rest[:n], rest[n], rest[n + 1]
    for piece, (origin, skip) in zip(pieces, sources):
        start = pl.multiple_of(origin(place[0]) * tokens, tokens)
        xs[pl.ds(start, tokens), :] = piece[skip : skip + tokens, :]
    out[...] = xs[...].T


def features_call(place, inputs, held, sources, slice_rows):
    tokens, n_dp = inputs.shape[0], len(sources)
    return run(
        functools.partial(features_kernel, sources, tokens),
        "features",
        (1,),
        [pl.BlockSpec((tokens, slice_rows), lambda j, place: (0, place[0]))]
        + [fixed(piece.shape) for piece in held],
        fixed((slice_rows, n_dp * tokens)),
        struct((slice_rows, n_dp * tokens), BF16),
        [pltpu.VMEM((n_dp * tokens, slice_rows), BF16)],
        6,
        (place, inputs, *held),
    )


def total(parts):
    whole = parts[0].astype(F32)
    for part in parts[1:]:
        whole = whole + part.astype(F32)
    return whole.astype(BF16)


def totals_kernel(n, place, parts, *rest):
    sums, (grad, out) = rest[:-2], rest[-2:]
    share = grad.shape[0]
    grad[...] = total([parts[k * share : (k + 1) * share, :] for k in range(n)])
    out[...] = total([part[...] for part in sums])


def totals_call(place, parts, sums, n):
    rows, width = parts.shape
    return run(
        functools.partial(totals_kernel, n),
        "totals",
        (1,),
        [fixed(parts.shape)] + [fixed(part.shape) for part in sums],
        [fixed((rows // n, width)), fixed(sums[0].shape)],
        [struct((rows // n, width), BF16), struct(sums[0].shape, BF16)],
        [],
        10,
        (place, parts, *sums),
    )


def inverse(value):
    guess = pl.reciprocal(value, approx=True)
    return guess * (2.0 - value * guess)


def updated(grad_sum, tokens_all, current, anchor, first, second, invert):
    grad = grad_sum * (1.0 / tokens_all) + anchor_pull * (current - anchor)
    first = beta_one * first + (1.0 - beta_one) * grad
    second = beta_two * second + (1.0 - beta_two) * grad * grad
    root = math.sqrt(1.0 / (1.0 - beta_two**step_count))
    scale = learn_rate / (1.0 - beta_one**step_count) / root
    spread = second * lax.rsqrt(second) + epsilon / root
    return current - (scale * first) * invert(spread), first, second


def update_kernel(origins, tokens_all, chunk, part, place, x_ref, *rest):
    n = len(origins)
    pieces = rest[:n]
    w_ref, a_ref, m_ref, v_ref, new_w, new_m, new_v, cs = rest[n:]
    own, width = pieces[0].shape

    @pl.when(pl.program_id(0) == 0)
    def _():
        for piece, origin in zip(pieces, origins):
            start = pl.multiple_of(origin(place[0], place[1]) * own, own)
            cs[pl.ds(start, own), :] = piece[...]

    for c in range(0, width, part):
        across = slice(c, c + part)
        summed = jnp.dot(x_ref[...], cs[:, across], preferred_element_type=F32)
        for r in range(0, x_ref.shape[0], chunk):
            at = (slice(r, r + chunk), across)
            weight, first, second = updated(
                summed[r : r + chunk],
                tokens_all,
                w_ref[at].astype(F32),
                a_ref[at].astype(F32),
                m_ref[at],
                v_ref[at],
                inverse,
            )
            new_w[at] = weight.astype(BF16)
            new_m[at] = first
            new_v[at] = second


def update_call(place, features, pieces, origins, held):
    rows, width = held[1].shape
    tokens_all = features.shape[1]
    block = math.gcd(rows, 128)
    tile = pl.BlockSpec((block, width), lambda j, place: (j, 0))
    return run(
        functools.partial(
            update_kernel, origins, tokens_all, math.gcd(block, 32), block_of(width, 512)
        ),
        "update",
        (rows // block,),
        [pl.BlockSpec((block, tokens_all), lambda j, place: (j, 0))]
        + [fixed(piece.shape) for piece in pieces]
        + [pl.BlockSpec((block, width), lambda j, place: (place[0] * (rows // block) + j, 0))]
        + [tile] * 3,
        [tile] * 3,
        [struct((rows, width), BF16), struct((rows, width), F32), struct((rows, width), F32)],
        [pltpu.VMEM((tokens_all, width), BF16)],
        38,
        (place, features, *pieces, *held),
    )


def after(value, *others):
    return lax.optimization_barrier((value, *others))[0]


def per_device(inputs, weight, cotangent, anchor, first_moment, second_moment):
    n_dp, n_row, n_col = (lax.axis_size(a) for a in ("dp", "row", "col"))
    dp, row, col = (lax.axis_index(a) for a in ("dp", "row", "col"))
    place = jnp.stack([dp, row, col]).astype(jnp.int32)
    cores = 2 if n_dp % 2 == 0 else 1
    chips = n_dp // cores
    tokens = inputs.shape[0]
    own = cotangent.shape[0]
    share = tokens // n_col
    slice_rows = weight.shape[0] // n_dp
    tiled = own % 16 == 0 and share % 16 == 0 and slice_rows % 128 == 0

    def along(axis, n, shift):
        return lambda a: lax.ppermute(a, axis, [(i, (i + shift) % n) for i in range(n)])

    def chip_shift(shift):
        return along("dp", n_dp, shift * cores)

    def swap_cores(a):
        return lax.ppermute(a, "dp", [(i, i ^ 1) for i in range(n_dp)])

    def in_order(pieces, places, rows):
        whole = jnp.zeros((len(pieces) * rows, pieces[0].shape[1]), pieces[0].dtype)
        for piece, at in zip(pieces, places):
            whole = lax.dynamic_update_slice_in_dim(whole, piece, at * rows, 0)
        return whole

    def dp_of(dp, c, flip):
        core = lax.rem(dp, cores)
        return lax.rem(dp - core - c * cores + n_dp, n_dp) + (1 - core if flip else core)

    by_row = [cotangent] + [along("row", n_row, s)(cotangent) for s in range(1, n_row)]
    by_chip = {(c, 0): chip_shift(c)(cotangent) for c in range(1, chips)}
    swapped = {(0, 0): swap_cores(cotangent)} if cores == 2 else {}

    flips = range(cores)
    targets = [[functools.partial(dp_of, c=0, flip=1)]] if cores == 2 else []
    targets += [[functools.partial(dp_of, c=chips - c, flip=f) for f in flips] for c in range(1, chips)]
    if tiled:
        made = forward_call(place, inputs, weight, own, n_row, slice_rows, targets)
        parts, to_send = made[:n_row], made[n_row:]
    else:
        part = jnp.dot(inputs, weight, preferred_element_type=F32)
        parts = [
            lax.dynamic_slice_in_dim(part, lax.rem(row + s, n_row) * own, own, 0).astype(
                BF16
            )
            for s in range(n_row)
        ]
        to_send = [
            jnp.concatenate(
                [
                    lax.dynamic_slice_in_dim(inputs, owner(dp) * slice_rows, slice_rows, 1)
                    for owner in owners
                ],
                0,
            )
            for owners in targets
        ]
    to_send = list(to_send)
    sums = [
        along("row", n_row, s)(after(parts[s], *swapped.values())) for s in range(1, n_row)
    ]
    near = [swap_cores(to_send.pop(0))] if cores == 2 else []
    first = [by_chip[c, 0] for c in range(1, chips)]
    far = [chip_shift(c)(to_send[c - 1]) for c in range(1, chips)]
    for s in range(1, n_row):
        by_row[s] = after(by_row[s], parts[0], *near, *first, *swapped.values())
        if cores == 2:
            swapped[0, s] = swap_cores(by_row[s])
    if cores == 2:
        for c in range(1, chips):
            swapped[c, 0] = swap_cores(by_chip[c, 0])

    held, sources = list(near), [(functools.partial(dp_of, c=0, flip=0), 0)]
    if cores == 2:
        sources.append((functools.partial(dp_of, c=0, flip=1), 0))
    for c in range(1, chips):
        for f in flips:
            piece = far[c - 1]
            held.append(swap_cores(piece) if f else piece)
            sources.append((functools.partial(dp_of, c=c, flip=f), f * tokens))
    if tiled:
        features = features_call(place, inputs, held, sources, slice_rows)
    else:
        mine = lax.dynamic_slice_in_dim(inputs, dp * slice_rows, slice_rows, 1)
        features = in_order(
            [mine] + [h[skip : skip + tokens] for h, (_, skip) in zip(held, sources[1:])],
            [origin(dp) for origin, _ in sources],
            tokens,
        )
    if tiled:
        gpart = input_grad_call(place, by_row, weight, n_row)
    else:
        gathered = in_order(by_row, [lax.rem(row - s + n_row, n_row) for s in range(n_row)], own)
        gpart = lax.dot_general(
            gathered, weight, (((1,), (1,)), ((), ())), preferred_element_type=F32
        ).astype(BF16)
    gparts = lax.all_to_all(gpart, "col", 0, 0, tiled=True)
    for s in range(1, n_row):
        for c in range(1, chips):
            by_chip[c, s] = along("row", n_row, s)(by_chip[c, 0])
    by_chip.update({(0, s): by_row[s] for s in range(n_row)})
    origins = []
    for c in range(chips):
        for s in range(n_row):
            for flip in range(cores):

                def origin(dp, row, c=c, s=s, flip=flip):
                    return dp_of(dp, c, flip) * n_row + lax.rem(row - s + n_row, n_row)

                origins.append(origin)

    pieces = []
    for c in range(chips):
        for s in range(n_row):
            early = c == 0 or s == 0
            pieces.append(in_hbm(by_chip[c, s]) if tiled and early else by_chip[c, s])
            if cores == 2:
                if (c, s) in swapped:
                    first_swap = tiled and (c, s) == (0, 0)
                    pieces.append(in_hbm(swapped[c, s]) if first_swap else swapped[c, s])
                else:
                    pieces.append(swap_cores(after(by_chip[c, s], features)))

    if tiled:
        streamed = map(in_hbm, (weight, anchor, first_moment, second_moment))
        new_weight, new_first, new_second = update_call(
            place, features, pieces, origins, tuple(streamed)
        )
    else:
        gathered = in_order(pieces, [origin(dp, row) for origin in origins], own)
        summed = lax.dot_general(
            features, gathered, (((0,), (0,)), ((), ())), preferred_element_type=F32
        )
        current = lax.dynamic_slice_in_dim(weight, dp * slice_rows, slice_rows, 0).astype(F32)
        new_weight, new_first, new_second = updated(
            summed,
            tokens * n_dp,
            current,
            anchor.astype(F32),
            first_moment,
            second_moment,
            lambda value: 1.0 / value,
        )
        new_weight = new_weight.astype(BF16)
    gparts = after(gparts, new_first)
    if tiled:
        input_grad, outputs = totals_call(place, gparts, [parts[0], *sums], n_col)
    else:
        input_grad = total(
            [lax.slice_in_dim(gparts, k * share, (k + 1) * share) for k in range(n_col)]
        )
        outputs = total([parts[0], *sums])
    return (outputs, input_grad, new_weight, new_first, new_second)


def solution(mesh):
    in_specs = (
        P("dp", "row"),
        P("row", "col"),
        P(("dp", "row"), "col"),
        P(("row", "dp"), "col"),
        P(("row", "dp"), "col"),
        P(("row", "dp"), "col"),
    )
    out_specs = (
        P(("dp", "row"), "col"),
        P(("dp", "col"), "row"),
        P(("row", "dp"), "col"),
        P(("row", "dp"), "col"),
        P(("row", "dp"), "col"),
    )
    return jax.shard_map(
        per_device, mesh=mesh, in_specs=in_specs, out_specs=out_specs, check_vma=False
    )
```
